512 devices in a mesh: doc: 32 (over y, z_lo, core), cent: 16 (over z_hi, x).
Axes of the slice: x: 4, y: 8, z: 8 (z_hi: 4, z_lo: 2; z = z_hi * 2 + z_lo), core: 2. Of those that a mesh axis runs over, the one named last changes fastest.
Arguments:
- docs: bfloat16 [32768, 256], P('doc'), may hold values from -24 to 24
- centroids: bfloat16 [32768, 256], P('cent'), may hold values from -7 to 7
- shard_ids: int32 [32768], P('doc'), may hold values from 0 to 63
- shard_mass: int32 [64], replicated, may hold values from 1 to 8
Outputs:
- new_centroids: bfloat16 [32768, 256], P('cent')
- row_potential: float32 [32768], P('doc')
The draws below stay inside these ranges and needn't reach their ends.
All inputs are finite; a program needn't handle non-finite values.
Results may differ from the reference program's by a relative error of at most 0.0033.
Values may be sent and summed in bfloat16 or wider, within the bound.
No kernel may reach another device: no remote copies, remote signals or barrier semaphores. Data moves between devices by JAX's collectives and lax.ppermute only.
A program may use at most 64 MiB of HBM per device.

```python
import jax
import jax.numpy as jnp
from jax import lax

D = 256
K = 32768
SHARDS = 64
PASSES = 3
DOC_DEV = 1024
DOCS = 32768
N_DOC = 32


def base_centroids(key):
    return jax.random.normal(key, (K, D), jnp.float32)


def draw_centroids(key, part):
    shared = base_centroids(key)
    key = jax.random.fold_in(key, 11)
    far_key = jax.random.fold_in(key, 5)
    remote = -6.5 + 0.5 * jax.random.uniform(far_key, (K, D), jnp.float32, -1.0, 1.0)
    distant = jnp.arange(K) % 1024 == 7
    shared = jnp.where(distant[:, None], remote, shared)
    return jnp.clip(shared, -7.0, 7.0).astype(jnp.bfloat16)


def draw_docs(key, part):
    key = jax.random.fold_in(key, 12)
    values = jax.random.normal(key, (DOCS, D), jnp.float32)
    values = values + 1.0
    return jnp.clip(values, -24.0, 24.0).astype(jnp.bfloat16)


def set_ends(array, key, low, largest):
    longest = array.shape.index(max(array.shape))
    spots = []
    for shift in (0, 1):
        where = [jax.random.randint(jax.random.fold_in(key, axis), (), 0, length) for axis, length in enumerate(array.shape)]
        where[longest] = (where[longest] + shift) % array.shape[longest]
        spots.append(tuple(where))
    return array.at[spots[0]].set(low).at[spots[1]].set(largest)


def setup_inputs(seed: int = 0) -> dict:
    splits = jax.random.split(jax.random.key(seed), 5)
    return {
        "docs": draw_docs(jax.random.fold_in(splits[4], 71), 0),
        "centroids": draw_centroids(jax.random.fold_in(splits[4], 71), 0),
        "shard_ids": set_ends(jax.random.randint(splits[2], (DOCS,), 0, SHARDS), jax.random.fold_in(splits[2], 1), 0, SHARDS - 1).astype(jnp.int32),
        "shard_mass": set_ends(jax.random.randint(splits[3], (SHARDS,), 1, 9), jax.random.fold_in(splits[3], 1), 1, 8).astype(jnp.int32),
    }


def block_logits(block, centroids):
    return jnp.dot(block, centroids.T, preferred_element_type=jnp.float32) * (4.0 * D ** -0.5)


def combine(first, second):
    top = jnp.maximum(first[0], second[0])
    return (top, first[1] * jnp.exp(first[0] - top) + second[1] * jnp.exp(second[0] - top))


def reference(docs, centroids, shard_ids, shard_mass):
    blocks = docs.reshape(N_DOC, DOC_DEV, D)
    weights = shard_mass.astype(jnp.float32)[shard_ids] / 8.0
    log_mass = jnp.log(weights).reshape(N_DOC, DOC_DEV)
    log_target = jnp.log(jnp.float32(0.5 * DOCS / K))

    def row_pass(col_pot):
        def one(item):
            block, mass_block = item
            tile = block_logits(block, centroids) + col_pot[None, :]
            return mass_block - jax.scipy.special.logsumexp(tile, axis=1)
        return lax.map(one, (blocks, log_mass))

    def col_pass(row_pot):
        def step(carry, item):
            block, pot_block = item
            tile = block_logits(block, centroids) + pot_block[:, None]
            top = jnp.max(tile, axis=0)
            total = jnp.sum(jnp.exp(tile - top[None, :]), axis=0)
            return combine(carry, (top, total)), None
        start = (jnp.full((K,), -jnp.inf, jnp.float32), jnp.zeros((K,), jnp.float32))
        (top, total), _ = lax.scan(step, start, (blocks, row_pot))
        return log_target - (top + jnp.log(total))

    col_pot = jnp.zeros((K,), jnp.float32)
    row_pot = row_pass(col_pot)
    for turn in range(PASSES):
        col_pot = col_pass(row_pot)
        row_pot = row_pass(col_pot)

    def gather_step(carry, item):
        block, pot_block = item
        plan = jnp.exp(block_logits(block, centroids) + pot_block[:, None] + col_pot[None, :])
        sums = carry[0] + jnp.dot(plan.astype(jnp.bfloat16).T, block, preferred_element_type=jnp.float32)
        return (sums, carry[1] + jnp.sum(plan, axis=0)), None

    start = (jnp.zeros((K, D), jnp.float32), jnp.zeros((K,), jnp.float32))
    (sums, mass), _ = lax.scan(gather_step, start, (blocks, row_pot))
    new_centroids = (sums / mass[:, None]).astype(jnp.bfloat16)
    return new_centroids, row_pot.reshape(DOCS)
```

```python
import functools
import math

import jax
import jax.numpy as jnp
from jax import lax
from jax.experimental import pallas as pl
from jax.experimental.pallas import tpu as pltpu
from jax.sharding import Mesh
from jax.sharding import PartitionSpec as P

LOG2E = 1.4426950408889634
LN2 = 0.6931471805599453
LANES = 128
VMEM_LIMIT = 32 * 1024 * 1024
ROWS = ("zl", "zh", "x")
COLS = ("y", "core")
F32 = jnp.float32
BF16 = jnp.bfloat16


def call(kernel, out_shape, n_in, smem=(), scratch=(), flops=0, out_specs=None, in_specs=None):
    vmem = pl.BlockSpec(memory_space=pltpu.VMEM)
    if in_specs is None:
        in_specs = [pl.BlockSpec(memory_space=pltpu.SMEM) if i in smem else vmem for i in range(n_in)]
    if out_specs is None:
        out_specs = jax.tree.map(lambda _: vmem, out_shape)
    return pl.pallas_call(
        kernel,
        out_shape=out_shape,
        in_specs=in_specs,
        out_specs=out_specs,
        scratch_shapes=list(scratch),
        compiler_params=pltpu.CompilerParams(vmem_limit_bytes=VMEM_LIMIT),
        cost_estimate=pl.CostEstimate(flops=flops, bytes_accessed=1 << 20, transcendentals=0),
    )


def lane_iota():
    return lax.broadcasted_iota(jnp.int32, (LANES, LANES), 1)


def to_columns(dense):
    return jnp.concatenate([dense] * (LANES // dense.shape[0]), axis=0).T


def nt_dot(a, b):
    return lax.dot_general(a, b, (((1,), (1,)), ((), ())), preferred_element_type=F32)


def weights_of(ids, mass_ref):
    def step(s, total):
        return jnp.where(ids == s, mass_ref[s].astype(F32), total)

    return lax.fori_loop(0, mass_ref.shape[0], step, jnp.zeros(ids.shape, F32)) * 0.125


def first_rows(scale, peers, docs_ref, cents_ref, out_ref, s_ref):
    n_cent = cents_ref.shape[0]
    block = 64

    def group(g, _):
        docs = docs_ref[pl.ds(pl.multiple_of(g * 256, 256), 256), :]
        top = jnp.full((8, 256), -jnp.inf, F32)
        for q in range(n_cent // 256):
            s = nt_dot(cents_ref[q * 256 : (q + 1) * 256, :], docs)
            s_ref[q * 256 : (q + 1) * 256, :] = s
            top = jnp.maximum(top, jnp.max(s.reshape(32, 8, 256), axis=0))
        top = jnp.max(top, axis=0, keepdims=True) * scale

        def part(q, total):
            s = s_ref[pl.ds(pl.multiple_of(q * block, block), block), :]
            return total + jnp.sum(jnp.exp2(s * scale - top).reshape(block // 8, 8, 256), axis=0)

        total = lax.fori_loop(0, n_cent // block, part, jnp.zeros((8, 256), F32), unroll=8)
        lse = top + jnp.log2(jnp.sum(total, axis=0, keepdims=True))
        for h in range(2):
            row = lse[:, h * LANES : (h + 1) * LANES]
            out_ref[:, pl.ds(g * 2 + h, 1), :] = jnp.broadcast_to(row[None], (peers, 1, LANES))
        return 0

    lax.fori_loop(0, docs_ref.shape[0] // 256, group, 0)


def first_columns(
    scale, peers, zl_ref, mass_ref, parts_ref, ids_ref, other_ids_ref, docs_ref, other_ref, cents_ref,
    out_ref, tile_ref, top_ref, f_ref, w_ref, docs_all_ref,
):
    zl = zl_ref[0]
    n_doc, n_cent = docs_ref.shape[0], cents_ref.shape[0] // 2
    groups = 2 * n_doc // LANES
    docs_all_ref[pl.ds(pl.multiple_of(zl * n_doc, n_doc), n_doc), :] = docs_ref[...]
    docs_all_ref[pl.ds(pl.multiple_of((1 - zl) * n_doc, n_doc), n_doc), :] = other_ref[...]
    own = weights_of(ids_ref[...], mass_ref)
    other = weights_of(other_ids_ref[...], mass_ref)
    w_ref[0:8, :] = jnp.where(zl == 0, own, other)
    w_ref[8:16, :] = jnp.where(zl == 0, other, own)
    half = parts_ref.shape[0] // 2
    for z in range(2):
        parts = parts_ref[z * half : (z + 1) * half]
        top = jnp.max(parts, axis=0)
        lse = top + jnp.log2(jnp.sum(jnp.exp2(parts - top[None]), axis=0))
        f_ref[z * 8 : (z + 1) * 8, :] = jnp.log2(w_ref[z * 8 : (z + 1) * 8, :]) - lse
    base = pl.multiple_of(zl * n_cent, n_cent)

    for g in range(groups // 2):
        f = jnp.concatenate([f_ref[2 * g : 2 * g + 1, :], f_ref[2 * g + 1 : 2 * g + 2, :]], axis=1)
        docs = docs_all_ref[g * 256 : (g + 1) * 256, :]
        for q in range(n_cent // 256):
            cents = cents_ref[pl.ds(pl.multiple_of(base + q * 256, 256), 256), :]
            tile_ref[q * 256 : (q + 1) * 256, g * 256 : (g + 1) * 256] = nt_dot(cents, docs) * scale + f
    lane = lane_iota()
    tops = jnp.zeros((LANES, LANES), F32)
    lses = jnp.zeros((LANES, LANES), F32)
    for r in range(n_cent // LANES):
        rows = slice(r * LANES, (r + 1) * LANES)
        top = tile_ref[rows, 0:LANES]
        for g in range(1, groups):
            top = jnp.maximum(top, tile_ref[rows, g * LANES : (g + 1) * LANES])
        top = jnp.broadcast_to(jnp.max(top, axis=1, keepdims=True), (LANES, LANES))
        total = jnp.zeros((LANES, LANES), F32)
        for g in range(groups):
            e = jnp.exp2(tile_ref[rows, g * LANES : (g + 1) * LANES] - top)
            tile_ref[rows, g * LANES : (g + 1) * LANES] = e
            total = total + e
        tops = jnp.where(lane == r, top, tops)
        lses = jnp.where(lane == r, top + jnp.log2(jnp.sum(total, axis=1, keepdims=True)), lses)
    top_ref[...] = tops.T[0:8, :]
    out_ref[...] = jnp.broadcast_to(lses.T[0:8, :][None], (peers, 8, LANES))


def weigh_columns(c, tile_ref, out_ref):
    groups = tile_ref.shape[1] // LANES
    cols = to_columns(c)
    totals = [jnp.zeros((8, LANES), F32) for _ in range(groups)]
    for r in range(tile_ref.shape[0] // LANES):
        col = jnp.broadcast_to(cols[:, r : r + 1], (LANES, LANES))
        for g in range(groups):
            p = tile_ref[r * LANES : (r + 1) * LANES, g * LANES : (g + 1) * LANES] * col
            totals[g] = totals[g] + jnp.sum(p.reshape(LANES // 8, 8, LANES), axis=0)
    rows = jnp.concatenate([jnp.sum(t, axis=0, keepdims=True) for t in totals], axis=0)
    out_ref[...] = jnp.broadcast_to(rows[None], out_ref.shape).astype(out_ref.dtype)


def rows_after_first(log_target, parts_ref, top_ref, tile_ref, out_ref, c_ref):
    parts = parts_ref[...]
    top = jnp.max(parts, axis=0)
    lse = top + jnp.log2(jnp.sum(jnp.exp2(parts - top[None]), axis=0))
    c = jnp.exp2(top_ref[...] + (log_target - lse))
    c_ref[...] = c
    weigh_columns(c, tile_ref, out_ref)


def rows_after(target, parts_ref, last_ref, tile_ref, out_ref, c_ref):
    c = last_ref[...] * (target / jnp.sum(parts_ref[...].astype(F32), axis=0))
    c_ref[...] = c
    weigh_columns(c, tile_ref, out_ref)


def columns_after(parts_ref, w_ref, c_ref, tile_ref, out_ref):
    groups = tile_ref.shape[1] // LANES
    u = w_ref[...] / jnp.sum(parts_ref[...].astype(F32), axis=0)
    lane = lane_iota()
    sums = jnp.zeros((LANES, LANES), F32)
    for r in range(tile_ref.shape[0] // LANES):
        total = jnp.zeros((LANES, LANES), F32)
        for g in range(groups):
            total = total + tile_ref[r * LANES : (r + 1) * LANES, g * LANES : (g + 1) * LANES] * u[g : g + 1, :]
        sums = jnp.where(lane == r, jnp.sum(total, axis=1, keepdims=True), sums)
    out = sums.T[0:8, :] * c_ref[...]
    out_ref[...] = jnp.broadcast_to(out[None], out_ref.shape).astype(out_ref.dtype)


def final_sums(n_y, n_core, zl_ref, parts_ref, w_ref, f_ref, c_ref, tile_ref, docs_ref, out_ref, pot_ref, p_ref):
    n_cent, n_doc = tile_ref.shape
    groups = n_doc // LANES
    u = w_ref[...] / jnp.sum(parts_ref[...], axis=0)
    pot = (f_ref[...] + jnp.log2(u)) * LN2
    pot_ref[...] = jnp.where(zl_ref[0] == 0, pot[0:8, :], pot[8:16, :])
    cols = to_columns(c_ref[...])
    lane = lane_iota()
    masses = jnp.zeros((LANES, LANES), F32)
    for r in range(n_cent // LANES):
        rows = slice(r * LANES, (r + 1) * LANES)
        col = jnp.broadcast_to(cols[:, r : r + 1], (LANES, LANES))
        total = jnp.zeros((LANES, LANES), F32)
        for g in range(groups):
            lanes = slice(g * LANES, (g + 1) * LANES)
            p = tile_ref[rows, lanes] * u[g : g + 1, :] * col
            total = total + p
            p_ref[rows, lanes] = p.astype(BF16)
        masses = jnp.where(lane == r, jnp.sum(total, axis=1, keepdims=True), masses)
    mass = masses.T[0:8, :]
    high = mass.astype(BF16)
    low = (mass - high.astype(F32)).astype(BF16)
    chunk = n_cent // (n_y * n_core)
    for b in range(n_cent // 256):
        sums = jnp.dot(p_ref[b * 256 : (b + 1) * 256, :], docs_ref[...], preferred_element_type=F32).astype(BF16)
        for k in range(256 // chunk):
            q = b * (256 // chunk) + k
            peer = (q % n_y) * n_core + q // n_y
            out_ref[peer, 0:chunk, :] = sums[k * chunk : (k + 1) * chunk, :]
            r = q * chunk // LANES
            pair = jnp.concatenate([high[r : r + 1, :], low[r : r + 1, :]], axis=1)
            out_ref[peer, chunk : chunk + 16, :] = jnp.broadcast_to(pair.astype(F32), (16, 256)).astype(BF16)


def divide(half_ref, parts_ref, out_ref, mass_ref):
    chunk = parts_ref.shape[1] - 16
    total = jnp.zeros((chunk, 256), F32)
    mass = jnp.zeros((16, 256), F32)
    for p in range(parts_ref.shape[0]):
        total = total + parts_ref[p, 0:chunk, :].astype(F32)
        mass = mass + parts_ref[p, chunk : chunk + 16, :].astype(F32)
    mass = mass[0:8, 0:LANES] + mass[0:8, LANES:256]
    mass_ref[...] = to_columns(mass)
    col = mass_ref[pl.ds(pl.multiple_of(half_ref[0] * chunk, chunk), chunk), :]
    new = (total / jnp.concatenate([col, col], axis=1)).astype(BF16)
    out_ref[...] = jnp.broadcast_to(new[None], out_ref.shape)


def assemble(at_ref, own_ref, zl_ref, core_ref, both_ref, out_ref, sems):
    rows = own_ref.shape[0]
    zl, core = at_ref[0], at_ref[1]
    places = (zl * 2 + core, (1 - zl) * 2 + core, zl * 2 + 1 - core, (1 - zl) * 2 + 1 - core)
    copies = []
    for k, (place, ref) in enumerate(zip(places, (own_ref, zl_ref, core_ref, both_ref))):
        dst = out_ref.at[pl.ds(pl.multiple_of(place * rows, rows), rows), :]
        copies.append(pltpu.make_async_copy(ref, dst, sems.at[k]))
    for copy in copies:
        copy.start()
    for copy in copies:
        copy.wait()


def exchange(x, axes):
    return lax.all_to_all(x, axes, 0, 0)


def per_device(sizes, docs, cents, shard_ids, shard_mass):
    n_y, n_zl, n_core, n_zh, n_x = sizes
    row_peers, col_peers = n_zl * n_zh * n_x, n_y * n_core
    n_doc, n_cent = docs.shape[0] * 2, cents.shape[0] // 2
    doc_rows, cent_rows = n_doc // LANES, n_cent // LANES
    scale = 4.0 * docs.shape[1] ** -0.5 * LOG2E
    target = 0.5 * (docs.shape[0] * n_y * n_zl * n_core) / (cents.shape[0] * n_zh * n_x)
    zl = lax.axis_index("zl")
    core = lax.axis_index("core")
    at = jnp.stack([zl, core]).astype(jnp.int32)
    half = (lax.axis_index("y") % 2).astype(jnp.int32).reshape(1)
    swap = [(0, 1), (1, 0)]
    shape = jax.ShapeDtypeStruct
    tile_shape = pltpu.VMEM((n_cent, n_doc), F32)
    small = shape((cent_rows, LANES), F32)

    other_docs = lax.ppermute(docs, "zl", swap)
    ids = shard_ids.reshape(-1, LANES)
    other_ids = lax.ppermute(ids, "zl", swap)
    parts = call(
        functools.partial(first_rows, scale, row_peers),
        shape((row_peers, doc_rows // 2, LANES), F32),
        2,
        scratch=[pltpu.VMEM((cents.shape[0], 256), F32)],
        flops=2 * docs.shape[0] * cents.shape[0] * 256,
    )(docs, cents)
    parts = exchange(parts, ROWS)
    parts, tile, top, f, w, docs_all = call(
        functools.partial(first_columns, scale, col_peers),
        (
            shape((col_peers, cent_rows, LANES), F32),
            tile_shape,
            small,
            shape((doc_rows, LANES), F32),
            shape((doc_rows, LANES), F32),
            pltpu.VMEM((n_doc, 256), BF16),
        ),
        8,
        smem=(0, 1),
        flops=2 * n_doc * n_cent * 256,
    )(at, shard_mass, parts, ids, other_ids, docs, other_docs, cents)

    def rows_out(dtype):
        return (shape((row_peers, doc_rows, LANES), dtype), small)

    parts = exchange(parts, COLS)
    log_target = math.log2(target)
    parts, c = call(functools.partial(rows_after_first, log_target), rows_out(BF16), 3, flops=2 * n_doc * n_cent)(parts, top, tile)
    for turn in range(2):
        parts = exchange(parts, ROWS)
        parts = call(columns_after, shape((col_peers, cent_rows, LANES), F32), 4, flops=2 * n_doc * n_cent)(parts, w, c, tile)
        parts = exchange(parts, COLS)
        parts, c = call(functools.partial(rows_after, target), rows_out(F32 if turn else BF16), 3, flops=2 * n_doc * n_cent)(parts, c, tile)
    parts = exchange(parts, ROWS)
    chunk = n_cent // col_peers
    sums, pot = call(
        functools.partial(final_sums, n_y, n_core),
        (shape((col_peers, chunk + 16, 256), BF16), shape((doc_rows // 2, LANES), F32)),
        7,
        smem=(0,),
        scratch=[pltpu.VMEM((n_cent, n_doc), BF16)],
        flops=2 * n_doc * n_cent * 256,
    )(at, parts, w, f, c, tile, docs_all)
    sums = exchange(sums, COLS)
    new = call(divide, shape((n_y, chunk, 256), BF16), 2, smem=(0,), scratch=[pltpu.VMEM((LANES, LANES), F32)])(half, sums)
    own = exchange(new, "y").reshape(n_y * chunk, 256)
    by_zl = lax.ppermute(own, "zl", swap)
    by_core = lax.ppermute(own, "core", swap)
    by_both = lax.ppermute(by_zl, "core", swap)
    anywhere = pl.BlockSpec(memory_space=pl.ANY)
    new = call(
        assemble,
        shape((cents.shape[0], 256), BF16),
        5,
        in_specs=[pl.BlockSpec(memory_space=pltpu.SMEM)] + [anywhere] * 4,
        out_specs=anywhere,
        scratch=[pltpu.SemaphoreType.DMA((4,))],
    )(at, own, by_zl, by_core, by_both)
    return new, pot.reshape(-1)


SIZES = (8, 2, 2, 4, 4)


def solution(mesh, sizes=SIZES):
    fine = Mesh(mesh.devices.reshape(sizes), ("y", "zl", "core", "zh", "x"))
    docs, cents = ("y", "zl", "core"), ("zh", "x")
    return jax.shard_map(
        functools.partial(per_device, sizes),
        mesh=fine,
        in_specs=(P(docs, None), P(cents, None), P(docs), P()),
        out_specs=(P(cents, None), P(docs)),
        check_vma=False,
    )
```

```python
import functools
import math

import jax
import jax.numpy as jnp
from jax import lax
from jax.experimental import pallas as pl
from jax.experimental.pallas import tpu as pltpu
from jax.sharding import Mesh
from jax.sharding import PartitionSpec as P

LOG2E = 1.4426950408889634
LN2 = 0.6931471805599453
LANES = 128
VMEM_LIMIT = 32 * 1024 * 1024
ROWS = ("zl", "zh", "x")
COLS = ("y", "core")
F32 = jnp.float32
BF16 = jnp.bfloat16


def call(kernel, out_shape, n_in, smem=(), scratch=(), flops=0, out_specs=None, in_specs=None, alias=None):
    vmem = pl.BlockSpec(memory_space=pltpu.VMEM)
    if in_specs is None:
        in_specs = [pl.BlockSpec(memory_space=pltpu.SMEM) if i in smem else vmem for i in range(n_in)]
    if out_specs is None:
        out_specs = jax.tree.map(lambda _: vmem, out_shape)
    return pl.pallas_call(
        kernel,
        out_shape=out_shape,
        in_specs=in_specs,
        out_specs=out_specs,
        scratch_shapes=list(scratch),
        input_output_aliases=alias or {},
        compiler_params=pltpu.CompilerParams(vmem_limit_bytes=VMEM_LIMIT),
        cost_estimate=pl.CostEstimate(flops=flops, bytes_accessed=1 << 20, transcendentals=0),
    )


def lane_iota():
    return lax.broadcasted_iota(jnp.int32, (LANES, LANES), 1)


def to_columns(dense):
    return jnp.concatenate([dense] * (LANES // dense.shape[0]), axis=0).T


def nt_dot(a, b):
    return lax.dot_general(a, b, (((1,), (1,)), ((), ())), preferred_element_type=F32)


def weights_of(ids, mass_ref):
    def step(s, total):
        return jnp.where(ids == s, mass_ref[s].astype(F32), total)

    return lax.fori_loop(0, mass_ref.shape[0], step, jnp.zeros(ids.shape, F32)) * 0.125


def first_rows(
    scale, peers, mass_ref, ids_ref, docs_hbm, cents_hbm, out_ref, docs_ref, cents_ref, sems
):
    n_doc, n_cent = docs_hbm.shape[0], cents_hbm.shape[0]
    block = 512
    steps = n_cent // block
    copies = [pltpu.make_async_copy(docs_hbm, docs_ref.at[0:n_doc, :], sems.at[steps])]
    for q in range(steps):
        rows = pl.ds(q * block, block)
        copies.append(pltpu.make_async_copy(cents_hbm.at[rows, :], cents_ref.at[rows, :], sems.at[q]))
    for copy in copies:
        copy.start()
    w = weights_of(ids_ref[...], mass_ref)
    pad = jnp.concatenate([jnp.concatenate([w, w], axis=0)] * 2, axis=1)
    docs_ref[n_doc : n_doc + 16, :] = pad.astype(BF16)
    copies[0].wait()
    groups = n_doc // 256
    tops = [jnp.full((8, 256), -jnp.inf, F32)] * groups
    totals = [jnp.zeros((8, 256), F32)] * groups
    for q in range(steps):
        copies[q + 1].wait()
        cents = cents_ref[q * block : (q + 1) * block, :]
        for g in range(groups):
            s = nt_dot(cents, docs_ref[g * 256 : (g + 1) * 256, :]).reshape(block // 8, 8, 256)
            top = jnp.maximum(tops[g], jnp.max(s, axis=0) * scale)
            totals[g] = totals[g] * jnp.exp2(tops[g] - top) + jnp.sum(jnp.exp2(s * scale - top[None]), axis=0)
            tops[g] = top
    rows = []
    for g in range(groups):
        top = jnp.max(tops[g], axis=0, keepdims=True)
        lse = top + jnp.log2(jnp.sum(totals[g] * jnp.exp2(tops[g] - top), axis=0, keepdims=True))
        rows += [lse[:, 0:LANES], lse[:, LANES:256]]
    out_ref[...] = jnp.broadcast_to(jnp.concatenate(rows, axis=0)[None], out_ref.shape)


def first_columns(
    scale, chunk, zl_ref, parts_ref, docs_ref, other_ref, cents_ref,
    out_ref, tile_ref, top_ref, f_ref, w_ref, docs_all_ref, half_ref,
):
    zl = zl_ref[0]
    n_doc, n_cent = docs_ref.shape[0] - 16, cents_ref.shape[0] // 2
    groups = 2 * n_doc // LANES
    docs_all_ref[pl.ds(pl.multiple_of(zl * n_doc, n_doc), n_doc), :] = docs_ref[0:n_doc, :]
    docs_all_ref[pl.ds(pl.multiple_of((1 - zl) * n_doc, n_doc), n_doc), :] = other_ref[0:n_doc, :]
    for q in range(n_cent // chunk):
        rows = pl.ds(pl.multiple_of(q * 2 * chunk + zl * chunk, chunk), chunk)
        half_ref[q * chunk : (q + 1) * chunk, :] = cents_ref[rows, :]
    own = docs_ref[n_doc : n_doc + 16, 0:LANES].astype(F32)[0:8]
    other = other_ref[n_doc : n_doc + 16, 0:LANES].astype(F32)[0:8]
    w_ref[0:8, :] = jnp.where(zl == 0, own, other)
    w_ref[8:16, :] = jnp.where(zl == 0, other, own)
    half = parts_ref.shape[0] // 2
    for z in range(2):
        parts = parts_ref[z * half : (z + 1) * half]
        top = jnp.max(parts, axis=0)
        lse = top + jnp.log2(jnp.sum(jnp.exp2(parts - top[None]), axis=0))
        f_ref[z * 8 : (z + 1) * 8, :] = jnp.log2(w_ref[z * 8 : (z + 1) * 8, :]) - lse

    for g in range(groups // 2):
        f = jnp.concatenate([f_ref[2 * g : 2 * g + 1, :], f_ref[2 * g + 1 : 2 * g + 2, :]], axis=1)
        docs = docs_all_ref[g * 256 : (g + 1) * 256, :]
        for q in range(n_cent // 256):
            cents = half_ref[q * 256 : (q + 1) * 256, :]
            tile_ref[q * 256 : (q + 1) * 256, g * 256 : (g + 1) * 256] = nt_dot(cents, docs) * scale + f
    lane = lane_iota()
    tops = jnp.zeros((LANES, LANES), F32)
    lses = jnp.zeros((LANES, LANES), F32)
    for r in range(n_cent // LANES):
        rows = slice(r * LANES, (r + 1) * LANES)
        top = tile_ref[rows, 0:LANES]
        for g in range(1, groups):
            top = jnp.maximum(top, tile_ref[rows, g * LANES : (g + 1) * LANES])
        top = jnp.broadcast_to(jnp.max(top, axis=1, keepdims=True), (LANES, LANES))
        total = jnp.zeros((LANES, LANES), F32)
        for g in range(groups):
            e = jnp.exp2(tile_ref[rows, g * LANES : (g + 1) * LANES] - top)
            tile_ref[rows, g * LANES : (g + 1) * LANES] = e
            total = total + e
        tops = jnp.where(lane == r, top, tops)
        lses = jnp.where(lane == r, top + jnp.log2(jnp.sum(total, axis=1, keepdims=True)), lses)
    top_ref[...] = tops.T[0:8, :]
    out_ref[...] = jnp.broadcast_to(lses.T[0:8, :][None], out_ref.shape)


def weigh_columns(c, tile_ref, out_ref):
    groups = tile_ref.shape[1] // LANES
    cols = to_columns(c)
    totals = [jnp.zeros((8, LANES), F32) for _ in range(groups)]
    for r in range(tile_ref.shape[0] // LANES):
        col = jnp.broadcast_to(cols[:, r : r + 1], (LANES, LANES))
        for g in range(groups):
            p = tile_ref[r * LANES : (r + 1) * LANES, g * LANES : (g + 1) * LANES] * col
            totals[g] = totals[g] + jnp.sum(p.reshape(LANES // 8, 8, LANES), axis=0)
    rows = jnp.concatenate([jnp.sum(t, axis=0, keepdims=True) for t in totals], axis=0)
    out_ref[...] = jnp.broadcast_to(rows[None], out_ref.shape).astype(out_ref.dtype)


def rows_after_first(log_target, parts_ref, top_ref, tile_ref, out_ref, c_ref):
    parts = parts_ref[...]
    top = jnp.max(parts, axis=0)
    lse = top + jnp.log2(jnp.sum(jnp.exp2(parts - top[None]), axis=0))
    c = jnp.exp2(top_ref[...] + (log_target - lse))
    c_ref[...] = c
    weigh_columns(c, tile_ref, out_ref)


def rows_after(target, parts_ref, last_ref, tile_ref, out_ref, c_ref):
    c = last_ref[...] * (target / jnp.sum(parts_ref[...].astype(F32), axis=0))
    c_ref[...] = c
    weigh_columns(c, tile_ref, out_ref)


def columns_after(parts_ref, w_ref, c_ref, tile_ref, out_ref):
    groups = tile_ref.shape[1] // LANES
    u = w_ref[...] / jnp.sum(parts_ref[...].astype(F32), axis=0)
    lane = lane_iota()
    sums = jnp.zeros((LANES, LANES), F32)
    for r in range(tile_ref.shape[0] // LANES):
        total = jnp.zeros((LANES, LANES), F32)
        for g in range(groups):
            total = total + tile_ref[r * LANES : (r + 1) * LANES, g * LANES : (g + 1) * LANES] * u[g : g + 1, :]
        sums = jnp.where(lane == r, jnp.sum(total, axis=1, keepdims=True), sums)
    out = sums.T[0:8, :] * c_ref[...]
    out_ref[...] = jnp.broadcast_to(out[None], out_ref.shape).astype(out_ref.dtype)


def final_sums(n_y, n_core, zl_ref, parts_ref, w_ref, f_ref, c_ref, tile_ref, docs_ref, out_ref, pot_ref, p_ref):
    n_cent, n_doc = tile_ref.shape
    groups = n_doc // LANES
    u = w_ref[...] / jnp.sum(parts_ref[...], axis=0)
    pot = (f_ref[...] + jnp.log2(u)) * LN2
    pot_ref[...] = jnp.where(zl_ref[0] == 0, pot[0:8, :], pot[8:16, :])
    cols = to_columns(c_ref[...])
    lane = lane_iota()
    masses = jnp.zeros((LANES, LANES), F32)
    for r in range(n_cent // LANES):
        rows = slice(r * LANES, (r + 1) * LANES)
        col = jnp.broadcast_to(cols[:, r : r + 1], (LANES, LANES))
        total = jnp.zeros((LANES, LANES), F32)
        for g in range(groups):
            lanes = slice(g * LANES, (g + 1) * LANES)
            p = tile_ref[rows, lanes] * u[g : g + 1, :] * col
            total = total + p
            p_ref[rows, lanes] = p.astype(BF16)
        masses = jnp.where(lane == r, jnp.sum(total, axis=1, keepdims=True), masses)
    mass = masses.T[0:8, :]
    high = mass.astype(BF16).astype(F32)
    low = mass - high
    chunk = n_cent // (n_y * n_core)
    for b in range(n_cent // 256):
        sums = jnp.dot(p_ref[b * 256 : (b + 1) * 256, :], docs_ref[...], preferred_element_type=F32).astype(BF16)
        for k in range(256 // chunk):
            q = b * (256 // chunk) + k
            peer = (q % n_y) * n_core + q // n_y
            for i in range(chunk // 16):
                for h in range(2):
                    at = (i * 2 + h) * LANES
                    out_ref[peer, :, at : at + LANES] = sums[k * chunk + i * 16 : k * chunk + (i + 1) * 16, h * LANES : (h + 1) * LANES]
            r = q * chunk // LANES
            pair = [jnp.broadcast_to(x[r : r + 1, :], (8, LANES)) for x in (high, low)]
            out_ref[peer, :, 2 * LANES * (chunk // 16) :] = jnp.concatenate(pair, axis=0).astype(BF16)


def divide(half_ref, parts_ref, out_ref, mass_ref):
    total = parts_ref[0].astype(F32)
    for p in range(1, parts_ref.shape[0]):
        total = total + parts_ref[p].astype(F32)
    tiles = total.shape[1] // LANES - 1
    chunk = tiles * 8
    mass = total[0:8, tiles * LANES :] + total[8:16, tiles * LANES :]
    mass_ref[...] = to_columns(mass)
    col = mass_ref[pl.ds(pl.multiple_of(half_ref[0] * chunk, chunk), chunk), :]
    for i in range(chunk // 16):
        pair = [total[:, (i * 2 + h) * LANES : (i * 2 + h + 1) * LANES] / col[i * 16 : (i + 1) * 16, :] for h in range(2)]
        new = jnp.concatenate(pair, axis=1).astype(BF16)
        out_ref[:, i * 16 : (i + 1) * 16, :] = jnp.broadcast_to(new[None], (out_ref.shape[0], 16, 256))


def place_own(at_ref, x_ref, out_ref, sem):
    rows = x_ref.shape[0]
    copy = pltpu.make_async_copy(x_ref, out_ref.at[pl.ds(pl.multiple_of(at_ref[1] * rows, rows), rows), :], sem)
    copy.start()
    copy.wait()


def place_other(at_ref, x_ref, _, out_ref, sem):
    rows = x_ref.shape[0]
    copy = pltpu.make_async_copy(x_ref, out_ref.at[pl.ds(pl.multiple_of((1 - at_ref[1]) * rows, rows), rows), :], sem)
    copy.start()
    copy.wait()


def exchange(x, axes):
    return lax.all_to_all(x, axes, 0, 0)


def per_device(sizes, docs, cents, shard_ids, shard_mass):
    n_y, n_zl, n_core, n_zh, n_x = sizes
    row_peers, col_peers = n_zl * n_zh * n_x, n_y * n_core
    n_doc, n_cent = docs.shape[0] * 2, cents.shape[0] // 2
    doc_rows, cent_rows = n_doc // LANES, n_cent // LANES
    scale = 4.0 * docs.shape[1] ** -0.5 * LOG2E
    target = 0.5 * (docs.shape[0] * n_y * n_zl * n_core) / (cents.shape[0] * n_zh * n_x)
    zl = lax.axis_index("zl")
    core = lax.axis_index("core")
    at = jnp.stack([zl, core]).astype(jnp.int32)
    half = (lax.axis_index("y") % 2).astype(jnp.int32).reshape(1)
    swap = [(0, 1), (1, 0)]
    shape = jax.ShapeDtypeStruct
    tile_shape = pltpu.VMEM((n_cent, n_doc), F32)
    small = shape((cent_rows, LANES), F32)

    any_space = pl.BlockSpec(memory_space=pl.ANY)
    vmem = pl.BlockSpec(memory_space=pltpu.VMEM)
    smem = pl.BlockSpec(memory_space=pltpu.SMEM)
    parts, docs, cents = call(
        functools.partial(first_rows, scale, row_peers),
        (
            shape((row_peers, doc_rows // 2, LANES), F32),
            pltpu.VMEM((docs.shape[0] + 16, 256), BF16),
            pltpu.VMEM(cents.shape, BF16),
        ),
        4,
        in_specs=[smem, vmem, any_space, any_space],
        scratch=[pltpu.SemaphoreType.DMA((5,))],
        flops=2 * docs.shape[0] * cents.shape[0] * 256,
    )(shard_mass, shard_ids.reshape(-1, LANES), docs, cents)
    other_docs = lax.ppermute(docs, "zl", swap)
    parts = exchange(parts, ROWS)
    chunk = n_cent // col_peers
    parts, tile, top, f, w, docs_all = call(
        functools.partial(first_columns, scale, chunk),
        (
            shape((col_peers, cent_rows, LANES), F32),
            tile_shape,
            small,
            shape((doc_rows, LANES), F32),
            shape((doc_rows, LANES), F32),
            pltpu.VMEM((n_doc, 256), BF16),
        ),
        5,
        smem=(0,),
        scratch=[pltpu.VMEM((n_cent, 256), BF16)],
        flops=2 * n_doc * n_cent * 256,
    )(at, parts, docs, other_docs, cents)

    def rows_out(dtype):
        return (shape((row_peers, doc_rows, LANES), dtype), small)

    parts = exchange(parts, COLS)
    log_target = math.log2(target)
    parts, c = call(functools.partial(rows_after_first, log_target), rows_out(BF16), 3, flops=2 * n_doc * n_cent)(parts, top, tile)
    for turn in range(2):
        parts = exchange(parts, ROWS)
        parts = call(columns_after, shape((col_peers, cent_rows, LANES), F32), 4, flops=2 * n_doc * n_cent)(parts, w, c, tile)
        parts = exchange(parts, COLS)
        parts, c = call(functools.partial(rows_after, target), rows_out(F32 if turn else BF16), 3, flops=2 * n_doc * n_cent)(parts, c, tile)
    parts = exchange(parts, ROWS)
    sums, pot = call(
        functools.partial(final_sums, n_y, n_core),
        (shape((col_peers, 16, 2 * LANES * (chunk // 16) + LANES), BF16), shape((doc_rows // 2, LANES), F32)),
        7,
        smem=(0,),
        scratch=[pltpu.VMEM((n_cent, n_doc), BF16)],
        flops=2 * n_doc * n_cent * 256,
    )(at, parts, w, f, c, tile, docs_all)
    sums = exchange(sums, COLS)
    new = call(divide, shape((n_y * n_zl, chunk, 256), BF16), 2, smem=(0,), scratch=[pltpu.VMEM((LANES, LANES), F32)])(half, sums)
    own = exchange(new, ("y", "zl")).reshape(n_y * n_zl * chunk, 256)
    other = lax.ppermute(own, "core", swap)
    placed = shape((cents.shape[0], 256), BF16)
    new = call(place_own, placed, 2, in_specs=[smem, any_space], out_specs=any_space, scratch=[pltpu.SemaphoreType.DMA])(at, own)
    new = call(
        place_other, placed, 3, in_specs=[smem, any_space, any_space], out_specs=any_space, scratch=[pltpu.SemaphoreType.DMA], alias={2: 0}
    )(at, other, new)
    return new, pot.reshape(-1)


SIZES = (8, 2, 2, 4, 4)


def solution(mesh, sizes=SIZES):
    fine = Mesh(mesh.devices.reshape(sizes), ("y", "zl", "core", "zh", "x"))
    docs, cents = ("y", "zl", "core"), ("zh", "x")
    return jax.shard_map(
        functools.partial(per_device, sizes),
        mesh=fine,
        in_specs=(P(docs, None), P(cents, None), P(docs), P()),
        out_specs=(P(cents, None), P(docs)),
        check_vma=False,
    )
```

```python
import functools
import math

import jax
import jax.numpy as jnp
from jax import lax
from jax.experimental import pallas as pl
from jax.experimental.pallas import tpu as pltpu
from jax.sharding import Mesh
from jax.sharding import PartitionSpec as P

LOG2E = 1.4426950408889634
LN2 = 0.6931471805599453
LANES = 128
VMEM_LIMIT = 32 * 1024 * 1024
ROWS = ("zl", "zh", "x")
COLS = ("y", "core")
F32 = jnp.float32
BF16 = jnp.bfloat16


def call(kernel, out_shape, n_in, smem=(), scratch=(), flops=0, out_specs=None, in_specs=None, alias=None):
    vmem = pl.BlockSpec(memory_space=pltpu.VMEM)
    if in_specs is None:
        in_specs = [pl.BlockSpec(memory_space=pltpu.SMEM) if i in smem else vmem for i in range(n_in)]
    if out_specs is None:
        out_specs = jax.tree.map(lambda _: vmem, out_shape)
    return pl.pallas_call(
        kernel,
        out_shape=out_shape,
        in_specs=in_specs,
        out_specs=out_specs,
        scratch_shapes=list(scratch),
        input_output_aliases=alias or {},
        compiler_params=pltpu.CompilerParams(vmem_limit_bytes=VMEM_LIMIT),
        cost_estimate=pl.CostEstimate(flops=flops, bytes_accessed=1 << 20, transcendentals=0),
    )


def lane_iota():
    return lax.broadcasted_iota(jnp.int32, (LANES, LANES), 1)


def to_columns(dense):
    return jnp.concatenate([dense] * (LANES // dense.shape[0]), axis=0).T


def nt_dot(a, b):
    return lax.dot_general(a, b, (((1,), (1,)), ((), ())), preferred_element_type=F32)


def weights_of(ids, mass_ref):
    def step(s, total):
        return jnp.where(ids == s, mass_ref[s].astype(F32), total)

    return lax.fori_loop(0, mass_ref.shape[0], step, jnp.zeros(ids.shape, F32)) * 0.125


def first_rows(
    scale, mass_hbm, ids_hbm, docs_hbm, cents_hbm, out_ref, docs_ref, cents_ref, mass_ref, ids_ref, sems
):
    n_doc, n_cent = docs_hbm.shape[0], cents_hbm.shape[0]
    block = 512
    steps = n_cent // block
    copies = [pltpu.make_async_copy(docs_hbm, docs_ref.at[0:n_doc, :], sems.at[steps])]
    for q in range(steps):
        rows = pl.ds(q * block, block)
        copies.append(pltpu.make_async_copy(cents_hbm.at[rows, :], cents_ref.at[rows, :], sems.at[q]))
    copies.append(pltpu.make_async_copy(mass_hbm, mass_ref, sems.at[steps + 1]))
    copies.append(pltpu.make_async_copy(ids_hbm, ids_ref, sems.at[steps + 2]))
    for copy in copies:
        copy.start()
    copies[0].wait()
    groups = n_doc // 256
    tops = [jnp.full((8, 256), -jnp.inf, F32)] * groups
    totals = [jnp.zeros((8, 256), F32)] * groups
    for q in range(steps):
        copies[q + 1].wait()
        cents = cents_ref[q * block : (q + 1) * block, :]
        for g in range(groups):
            s = nt_dot(cents, docs_ref[g * 256 : (g + 1) * 256, :]).reshape(block // 8, 8, 256)
            top = jnp.maximum(tops[g], jnp.max(s, axis=0) * scale)
            totals[g] = totals[g] * jnp.exp2(tops[g] - top) + jnp.sum(jnp.exp2(s * scale - top[None]), axis=0)
            tops[g] = top
    rows = []
    for g in range(groups):
        top = jnp.max(tops[g], axis=0, keepdims=True)
        lse = top + jnp.log2(jnp.sum(totals[g] * jnp.exp2(tops[g] - top), axis=0, keepdims=True))
        rows += [lse[:, 0:LANES], lse[:, LANES:256]]
    out_ref[...] = jnp.broadcast_to(jnp.concatenate(rows, axis=0)[None], out_ref.shape)
    copies[steps + 1].wait()
    copies[steps + 2].wait()
    w = weights_of(ids_ref[...], mass_ref)
    pad = jnp.concatenate([jnp.concatenate([w, w], axis=0)] * 2, axis=1)
    docs_ref[n_doc : n_doc + 16, :] = pad.astype(BF16)


def first_columns(
    scale, chunk, zl_ref, parts_ref, docs_ref, other_ref, cents_ref,
    out_ref, tile_ref, top_ref, f_ref, w_ref, docs_all_ref, half_ref,
):
    zl = zl_ref[0]
    n_doc, n_cent = docs_ref.shape[0] - 16, cents_ref.shape[0] // 2
    groups = 2 * n_doc // LANES
    docs_all_ref[pl.ds(pl.multiple_of(zl * n_doc, n_doc), n_doc), :] = docs_ref[0:n_doc, :]
    docs_all_ref[pl.ds(pl.multiple_of((1 - zl) * n_doc, n_doc), n_doc), :] = other_ref[0:n_doc, :]
    for q in range(n_cent // chunk):
        rows = pl.ds(pl.multiple_of(q * 2 * chunk + zl * chunk, chunk), chunk)
        half_ref[q * chunk : (q + 1) * chunk, :] = cents_ref[rows, :]
    own = docs_ref[n_doc : n_doc + 16, 0:LANES].astype(F32)[0:8]
    other = other_ref[n_doc : n_doc + 16, 0:LANES].astype(F32)[0:8]
    w_ref[0:8, :] = jnp.where(zl == 0, own, other)
    w_ref[8:16, :] = jnp.where(zl == 0, other, own)
    half = parts_ref.shape[0] // 2
    for z in range(2):
        parts = parts_ref[z * half : (z + 1) * half]
        top = jnp.max(parts, axis=0)
        lse = top + jnp.log2(jnp.sum(jnp.exp2(parts - top[None]), axis=0))
        f_ref[z * 8 : (z + 1) * 8, :] = jnp.log2(w_ref[z * 8 : (z + 1) * 8, :]) - lse

    for g in range(groups // 2):
        f = jnp.concatenate([f_ref[2 * g : 2 * g + 1, :], f_ref[2 * g + 1 : 2 * g + 2, :]], axis=1)
        docs = docs_all_ref[g * 256 : (g + 1) * 256, :]
        for q in range(n_cent // 256):
            cents = half_ref[q * 256 : (q + 1) * 256, :]
            tile_ref[q * 256 : (q + 1) * 256, g * 256 : (g + 1) * 256] = nt_dot(cents, docs) * scale + f
    lane = lane_iota()
    tops = jnp.zeros((LANES, LANES), F32)
    lses = jnp.zeros((LANES, LANES), F32)
    for r in range(n_cent // LANES):
        rows = slice(r * LANES, (r + 1) * LANES)
        top = tile_ref[rows, 0:LANES]
        for g in range(1, groups):
            top = jnp.maximum(top, tile_ref[rows, g * LANES : (g + 1) * LANES])
        top = jnp.broadcast_to(jnp.max(top, axis=1, keepdims=True), (LANES, LANES))
        total = jnp.zeros((LANES, LANES), F32)
        for g in range(groups):
            e = jnp.exp2(tile_ref[rows, g * LANES : (g + 1) * LANES] - top)
            tile_ref[rows, g * LANES : (g + 1) * LANES] = e
            total = total + e
        tops = jnp.where(lane == r, top, tops)
        lses = jnp.where(lane == r, top + jnp.log2(jnp.sum(total, axis=1, keepdims=True)), lses)
    top_ref[...] = tops.T[0:8, :]
    out_ref[...] = jnp.broadcast_to(lses.T[0:8, :][None], out_ref.shape)


def weigh_columns(c, tile_ref, out_ref):
    groups = tile_ref.shape[1] // LANES
    cols = to_columns(c)
    totals = [jnp.zeros((8, LANES), F32) for _ in range(groups)]
    for r in range(tile_ref.shape[0] // LANES):
        col = jnp.broadcast_to(cols[:, r : r + 1], (LANES, LANES))
        for g in range(groups):
            p = tile_ref[r * LANES : (r + 1) * LANES, g * LANES : (g + 1) * LANES] * col
            totals[g] = totals[g] + jnp.sum(p.reshape(LANES // 8, 8, LANES), axis=0)
    rows = jnp.concatenate([jnp.sum(t, axis=0, keepdims=True) for t in totals], axis=0)
    out_ref[...] = jnp.broadcast_to(rows[None], out_ref.shape).astype(out_ref.dtype)


def rows_after_first(log_target, parts_ref, top_ref, tile_ref, out_ref, c_ref):
    parts = parts_ref[...]
    top = jnp.max(parts, axis=0)
    lse = top + jnp.log2(jnp.sum(jnp.exp2(parts - top[None]), axis=0))
    c = jnp.exp2(top_ref[...] + (log_target - lse))
    c_ref[...] = c
    weigh_columns(c, tile_ref, out_ref)


def rows_after(target, parts_ref, last_ref, tile_ref, out_ref, c_ref):
    c = last_ref[...] * (target / jnp.sum(parts_ref[...].astype(F32), axis=0))
    c_ref[...] = c
    weigh_columns(c, tile_ref, out_ref)


def columns_after(parts_ref, w_ref, c_ref, tile_ref, out_ref):
    groups = tile_ref.shape[1] // LANES
    u = w_ref[...] / jnp.sum(parts_ref[...].astype(F32), axis=0)
    lane = lane_iota()
    sums = jnp.zeros((LANES, LANES), F32)
    for r in range(tile_ref.shape[0] // LANES):
        total = jnp.zeros((LANES, LANES), F32)
        for g in range(groups):
            total = total + tile_ref[r * LANES : (r + 1) * LANES, g * LANES : (g + 1) * LANES] * u[g : g + 1, :]
        sums = jnp.where(lane == r, jnp.sum(total, axis=1, keepdims=True), sums)
    out = sums.T[0:8, :] * c_ref[...]
    out_ref[...] = jnp.broadcast_to(out[None], out_ref.shape).astype(out_ref.dtype)


def half_sums(side, u, c_ref, tile_ref, docs_ref, out_ref, p_ref):
    n_half, n_doc = p_ref.shape
    groups = n_doc // LANES
    blocks = n_half // LANES
    cols = to_columns(c_ref[pl.ds(side * blocks, blocks), :])
    base = pl.multiple_of(side * n_half, n_half)
    lane = lane_iota()
    masses = jnp.zeros((LANES, LANES), F32)
    for r in range(blocks):
        rows = pl.ds(pl.multiple_of(base + r * LANES, LANES), LANES)
        col = jnp.broadcast_to(cols[:, r : r + 1], (LANES, LANES))
        total = jnp.zeros((LANES, LANES), F32)
        for g in range(groups):
            lanes = slice(g * LANES, (g + 1) * LANES)
            p = tile_ref[rows, lanes] * u[g : g + 1, :] * col
            total = total + p
            p_ref[r * LANES : (r + 1) * LANES, lanes] = p.astype(BF16)
        masses = jnp.where(lane == r, jnp.sum(total, axis=1, keepdims=True), masses)
    mass = masses.T[0:8, :]
    out_ref[n_half : n_half + 8, :] = jnp.concatenate([mass, mass], axis=1)
    for b in range(n_half // 256):
        rows = slice(b * 256, (b + 1) * 256)
        out_ref[rows, :] = jnp.dot(p_ref[rows, :], docs_ref[...], preferred_element_type=F32)


def final_other(at_ref, parts_ref, w_ref, f_ref, c_ref, tile_ref, docs_ref, out_ref, pot_ref, u_ref, p_ref):
    u = w_ref[...] / jnp.sum(parts_ref[...].astype(F32), axis=0)
    u_ref[...] = u
    pot = (f_ref[...] + jnp.log2(u)) * LN2
    pot_ref[...] = jnp.where(at_ref[0] == 0, pot[0:8, :], pot[8:16, :])
    half_sums(1 - at_ref[1], u, c_ref, tile_ref, docs_ref, out_ref, p_ref)


def final_own(at_ref, u_ref, c_ref, tile_ref, docs_ref, out_ref, p_ref):
    half_sums(at_ref[1], u_ref[...], c_ref, tile_ref, docs_ref, out_ref, p_ref)


def final_join(own_ref, other_ref, out_ref):
    peers = out_ref.shape[0]
    n_half = own_ref.shape[0] - 8
    chunk = n_half // peers
    mass = own_ref[n_half:, 0:LANES] + other_ref[n_half:, 0:LANES]
    high = mass.astype(BF16).astype(F32)
    low = mass - high
    for q in range(peers):
        for i in range(chunk // 16):
            rows = slice(q * chunk + i * 16, q * chunk + (i + 1) * 16)
            out_ref[q, :, i * 256 : (i + 1) * 256] = (own_ref[rows, :] + other_ref[rows, :]).astype(BF16)
        r = q * chunk // LANES
        pair = [jnp.broadcast_to(x[r : r + 1, :], (8, LANES)) for x in (high, low)]
        out_ref[q, :, 256 * (chunk // 16) :] = jnp.concatenate(pair, axis=0).astype(BF16)


def divide(half_ref, parts_ref, out_ref, mass_ref):
    total = parts_ref[0].astype(F32)
    for p in range(1, parts_ref.shape[0]):
        total = total + parts_ref[p].astype(F32)
    tiles = total.shape[1] // LANES - 1
    chunk = tiles * 8
    mass = total[0:8, tiles * LANES :] + total[8:16, tiles * LANES :]
    mass_ref[...] = to_columns(mass)
    col = mass_ref[pl.ds(pl.multiple_of(half_ref[0] * chunk, chunk), chunk), :]
    for i in range(chunk // 16):
        pair = [total[:, (i * 2 + h) * LANES : (i * 2 + h + 1) * LANES] / col[i * 16 : (i + 1) * 16, :] for h in range(2)]
        new = jnp.concatenate(pair, axis=1).astype(BF16)
        out_ref[:, i * 16 : (i + 1) * 16, :] = jnp.broadcast_to(new[None], (out_ref.shape[0], 16, 256))


def place_own(at_ref, x_ref, out_ref, sem):
    rows = x_ref.shape[0]
    copy = pltpu.make_async_copy(x_ref, out_ref.at[pl.ds(pl.multiple_of(at_ref[1] * rows, rows), rows), :], sem)
    copy.start()
    copy.wait()


def place_other(at_ref, x_ref, _, out_ref, sem):
    rows = x_ref.shape[0]
    copy = pltpu.make_async_copy(x_ref, out_ref.at[pl.ds(pl.multiple_of((1 - at_ref[1]) * rows, rows), rows), :], sem)
    copy.start()
    copy.wait()


def exchange(x, axes):
    return lax.all_to_all(x, axes, 0, 0)


def per_device(sizes, docs, cents, shard_ids, shard_mass):
    n_y, n_zl, n_core, n_zh, n_x = sizes
    row_peers, col_peers = n_zl * n_zh * n_x, n_y * n_core
    n_doc, n_cent = docs.shape[0] * 2, cents.shape[0] // 2
    doc_rows, cent_rows = n_doc // LANES, n_cent // LANES
    scale = 4.0 * docs.shape[1] ** -0.5 * LOG2E
    target = 0.5 * (docs.shape[0] * n_y * n_zl * n_core) / (cents.shape[0] * n_zh * n_x)
    zl = lax.axis_index("zl")
    core = lax.axis_index("core")
    at = jnp.stack([zl, core]).astype(jnp.int32)
    half = (lax.axis_index("y") % 2).astype(jnp.int32).reshape(1)
    swap = [(0, 1), (1, 0)]
    shape = jax.ShapeDtypeStruct
    tile_shape = pltpu.VMEM((n_cent, n_doc), F32)
    small = shape((cent_rows, LANES), F32)

    any_space = pl.BlockSpec(memory_space=pl.ANY)
    hbm = pl.BlockSpec(memory_space=pltpu.HBM)
    smem = pl.BlockSpec(memory_space=pltpu.SMEM)
    parts, docs, cents = call(
        functools.partial(first_rows, scale),
        (
            shape((row_peers, doc_rows // 2, LANES), F32),
            pltpu.VMEM((docs.shape[0] + 16, 256), BF16),
            pltpu.VMEM(cents.shape, BF16),
        ),
        4,
        in_specs=[hbm] * 4,
        scratch=[pltpu.SMEM(shard_mass.shape, jnp.int32), pltpu.VMEM((doc_rows // 2, LANES), jnp.int32), pltpu.SemaphoreType.DMA((7,))],
        flops=2 * docs.shape[0] * cents.shape[0] * 256,
    )(*[pltpu.with_memory_space_constraint(x, pltpu.HBM) for x in (shard_mass, shard_ids.reshape(-1, LANES), docs, cents)])
    other_docs = lax.ppermute(docs, "zl", swap)
    parts = exchange(parts, ROWS)
    chunk = n_cent // col_peers
    parts, tile, top, f, w, docs_all = call(
        functools.partial(first_columns, scale, chunk),
        (
            shape((col_peers, cent_rows, LANES), F32),
            tile_shape,
            small,
            shape((doc_rows, LANES), F32),
            shape((doc_rows, LANES), F32),
            pltpu.VMEM((n_doc, 256), BF16),
        ),
        5,
        smem=(0,),
        scratch=[pltpu.VMEM((n_cent, 256), BF16)],
        flops=2 * n_doc * n_cent * 256,
    )(at, parts, docs, other_docs, cents)

    rows_out = (shape((row_peers, doc_rows, LANES), BF16), small)
    parts = exchange(parts, COLS)
    log_target = math.log2(target)
    parts, c = call(functools.partial(rows_after_first, log_target), rows_out, 3, flops=2 * n_doc * n_cent)(parts, top, tile)
    for turn in range(2):
        parts = exchange(parts, ROWS)
        parts = call(columns_after, shape((col_peers, cent_rows, LANES), F32), 4, flops=2 * n_doc * n_cent)(parts, w, c, tile)
        parts = exchange(parts, COLS)
        parts, c = call(functools.partial(rows_after, target), rows_out, 3, flops=2 * n_doc * n_cent)(parts, c, tile)
    parts = exchange(parts, ROWS)
    n_half = n_cent // n_core
    half_flops = 2 * n_doc * n_half * 256
    part_shape = pltpu.VMEM((n_half + 8, 256), F32)
    p_scratch = [pltpu.VMEM((n_half, n_doc), BF16)]
    for_other, pot, u = call(
        final_other,
        (part_shape, shape((doc_rows // 2, LANES), F32), shape((doc_rows, LANES), F32)),
        7,
        smem=(0,),
        scratch=p_scratch,
        flops=half_flops,
    )(at, parts, w, f, c, tile, docs_all)
    from_other = lax.ppermute(for_other, "core", swap)
    for_own = call(final_own, part_shape, 5, smem=(0,), scratch=p_scratch, flops=half_flops)(at, u, c, tile, docs_all)
    sums = call(final_join, shape((n_y, 16, 2 * LANES * (chunk // 16) + LANES), BF16), 2)(for_own, from_other)
    sums = exchange(sums, "y")
    new = call(divide, shape((n_y * n_zl, chunk, 256), BF16), 2, smem=(0,), scratch=[pltpu.VMEM((LANES, LANES), F32)])(half, sums)
    own = exchange(new, ("y", "zl")).reshape(n_y * n_zl * chunk, 256)
    other = lax.ppermute(own, "core", swap)
    placed = shape((cents.shape[0], 256), BF16)
    new = call(place_own, placed, 2, in_specs=[smem, any_space], out_specs=any_space, scratch=[pltpu.SemaphoreType.DMA])(at, own)
    new = call(
        place_other, placed, 3, in_specs=[smem, any_space, any_space], out_specs=any_space, scratch=[pltpu.SemaphoreType.DMA], alias={2: 0}
    )(at, other, new)
    return new, pot.reshape(-1)


SIZES = (8, 2, 2, 4, 4)


def solution(mesh, sizes=SIZES):
    fine = Mesh(mesh.devices.reshape(sizes), ("y", "zl", "core", "zh", "x"))
    docs, cents = ("y", "zl", "core"), ("zh", "x")
    return jax.shard_map(
        functools.partial(per_device, sizes),
        mesh=fine,
        in_specs=(P(docs, None), P(cents, None), P(docs), P()),
        out_specs=(P(cents, None), P(docs)),
        check_vma=False,
    )
```

```python
import functools
import math

import jax
import jax.numpy as jnp
from jax import lax
from jax.experimental import pallas as pl
from jax.experimental.pallas import tpu as pltpu
from jax.sharding import Mesh
from jax.sharding import PartitionSpec as P

LOG2E = 1.4426950408889634
LN2 = 0.6931471805599453
LANES = 128
VMEM_LIMIT = 32 * 1024 * 1024
ROWS = ("zl", "zh", "x")
COLS = ("y", "core")
F32 = jnp.float32
BF16 = jnp.bfloat16


def call(kernel, out_shape, n_in, smem=(), scratch=(), flops=0, out_specs=None, in_specs=None, alias=None):
    vmem = pl.BlockSpec(memory_space=pltpu.VMEM)
    if in_specs is None:
        in_specs = [pl.BlockSpec(memory_space=pltpu.SMEM) if i in smem else vmem for i in range(n_in)]
    if out_specs is None:
        out_specs = jax.tree.map(lambda _: vmem, out_shape)
    return pl.pallas_call(
        kernel,
        out_shape=out_shape,
        in_specs=in_specs,
        out_specs=out_specs,
        scratch_shapes=list(scratch),
        input_output_aliases=alias or {},
        compiler_params=pltpu.CompilerParams(vmem_limit_bytes=VMEM_LIMIT),
        cost_estimate=pl.CostEstimate(flops=flops, bytes_accessed=1 << 20, transcendentals=0),
    )


def lane_iota():
    return lax.broadcasted_iota(jnp.int32, (LANES, LANES), 1)


def to_columns(dense):
    return jnp.concatenate([dense] * (LANES // dense.shape[0]), axis=0).T


def nt_dot(a, b):
    return lax.dot_general(a, b, (((1,), (1,)), ((), ())), preferred_element_type=F32)


def weights_of(ids, mass_ref):
    def step(s, total):
        return jnp.where(ids == s, mass_ref[s].astype(F32), total)

    return lax.fori_loop(0, mass_ref.shape[0], step, jnp.zeros(ids.shape, F32), unroll=True) * 0.125


def first_rows(
    scale, mass_hbm, ids_hbm, docs_hbm, cents_hbm, out_ref, docs_ref, cents_ref, w_ref, mass_ref, ids_ref, sems
):
    n_doc, n_cent = docs_hbm.shape[0], cents_hbm.shape[0]
    block = 512
    steps = n_cent // block
    copies = [pltpu.make_async_copy(docs_hbm, docs_ref, sems.at[steps])]
    for q in range(steps):
        rows = pl.ds(q * block, block)
        copies.append(pltpu.make_async_copy(cents_hbm.at[rows, :], cents_ref.at[rows, :], sems.at[q]))
    copies.append(pltpu.make_async_copy(mass_hbm, mass_ref, sems.at[steps + 1]))
    copies.append(pltpu.make_async_copy(ids_hbm, ids_ref, sems.at[steps + 2]))
    for copy in copies[-2:] + copies[:-2]:
        copy.start()
    copies[steps + 1].wait()
    copies[steps + 2].wait()
    w_ref[...] = weights_of(ids_ref[...], mass_ref)
    copies[0].wait()
    groups = n_doc // 256
    tops = [jnp.full((8, 256), -jnp.inf, F32)] * groups
    totals = [jnp.zeros((8, 256), F32)] * groups
    for q in range(steps):
        copies[q + 1].wait()
        cents = cents_ref[q * block : (q + 1) * block, :]
        for g in range(groups):
            s = nt_dot(cents, docs_ref[g * 256 : (g + 1) * 256, :]).reshape(block // 8, 8, 256)
            top = jnp.maximum(tops[g], jnp.max(s, axis=0) * scale)
            totals[g] = totals[g] * jnp.exp2(tops[g] - top) + jnp.sum(jnp.exp2(s * scale - top[None]), axis=0)
            tops[g] = top
    rows = []
    for g in range(groups):
        top = jnp.max(tops[g], axis=0, keepdims=True)
        lse = top + jnp.log2(jnp.sum(totals[g] * jnp.exp2(tops[g] - top), axis=0, keepdims=True))
        rows += [lse[:, 0:LANES], lse[:, LANES:256]]
    out_ref[...] = jnp.broadcast_to(jnp.concatenate(rows, axis=0)[None], out_ref.shape)


def first_columns(
    scale, chunk, zl_ref, parts_ref, own_w_ref, other_w_ref, docs_ref, other_ref, cents_ref,
    out_ref, tile_ref, top_ref, f_ref, w_ref, docs_all_ref, half_ref,
):
    zl = zl_ref[0]
    n_doc, n_cent = docs_ref.shape[0], cents_ref.shape[0] // 2
    groups = 2 * n_doc // LANES
    docs_all_ref[pl.ds(pl.multiple_of(zl * n_doc, n_doc), n_doc), :] = docs_ref[...]
    docs_all_ref[pl.ds(pl.multiple_of((1 - zl) * n_doc, n_doc), n_doc), :] = other_ref[...]
    for q in range(n_cent // chunk):
        rows = pl.ds(pl.multiple_of(q * 2 * chunk + zl * chunk, chunk), chunk)
        half_ref[q * chunk : (q + 1) * chunk, :] = cents_ref[rows, :]
    own, other = own_w_ref[...], other_w_ref[...]
    w_ref[0:8, :] = jnp.where(zl == 0, own, other)
    w_ref[8:16, :] = jnp.where(zl == 0, other, own)
    half = parts_ref.shape[0] // 2
    for z in range(2):
        parts = parts_ref[z * half : (z + 1) * half]
        top = jnp.max(parts, axis=0)
        lse = top + jnp.log2(jnp.sum(jnp.exp2(parts - top[None]), axis=0))
        f_ref[z * 8 : (z + 1) * 8, :] = jnp.log2(w_ref[z * 8 : (z + 1) * 8, :]) - lse

    for g in range(groups // 2):
        f = jnp.concatenate([f_ref[2 * g : 2 * g + 1, :], f_ref[2 * g + 1 : 2 * g + 2, :]], axis=1)
        docs = docs_all_ref[g * 256 : (g + 1) * 256, :]
        for q in range(n_cent // 256):
            cents = half_ref[q * 256 : (q + 1) * 256, :]
            tile_ref[q * 256 : (q + 1) * 256, g * 256 : (g + 1) * 256] = nt_dot(cents, docs) * scale + f
    lane = lane_iota()
    tops = jnp.zeros((LANES, LANES), F32)
    lses = jnp.zeros((LANES, LANES), F32)
    for r in range(n_cent // LANES):
        rows = slice(r * LANES, (r + 1) * LANES)
        top = tile_ref[rows, 0:LANES]
        for g in range(1, groups):
            top = jnp.maximum(top, tile_ref[rows, g * LANES : (g + 1) * LANES])
        top = jnp.broadcast_to(jnp.max(top, axis=1, keepdims=True), (LANES, LANES))
        total = jnp.zeros((LANES, LANES), F32)
        for g in range(groups):
            e = jnp.exp2(tile_ref[rows, g * LANES : (g + 1) * LANES] - top)
            tile_ref[rows, g * LANES : (g + 1) * LANES] = e
            total = total + e
        tops = jnp.where(lane == r, top, tops)
        lses = jnp.where(lane == r, top + jnp.log2(jnp.sum(total, axis=1, keepdims=True)), lses)
    top_ref[...] = tops.T[0:8, :]
    out_ref[...] = jnp.broadcast_to(lses.T[0:8, :][None], out_ref.shape)


def weigh_columns(c, tile_ref, out_ref):
    groups = tile_ref.shape[1] // LANES
    cols = to_columns(c)
    totals = [jnp.zeros((8, LANES), F32) for _ in range(groups)]
    for r in range(tile_ref.shape[0] // LANES):
        col = jnp.broadcast_to(cols[:, r : r + 1], (LANES, LANES))
        for g in range(groups):
            p = tile_ref[r * LANES : (r + 1) * LANES, g * LANES : (g + 1) * LANES] * col
            totals[g] = totals[g] + jnp.sum(p.reshape(LANES // 8, 8, LANES), axis=0)
    rows = jnp.concatenate([jnp.sum(t, axis=0, keepdims=True) for t in totals], axis=0)
    out_ref[...] = jnp.broadcast_to(rows[None], out_ref.shape).astype(out_ref.dtype)


def rows_after_first(log_target, parts_ref, top_ref, tile_ref, out_ref, c_ref):
    parts = parts_ref[...]
    top = jnp.max(parts, axis=0)
    lse = top + jnp.log2(jnp.sum(jnp.exp2(parts - top[None]), axis=0))
    c = jnp.exp2(top_ref[...] + (log_target - lse))
    c_ref[...] = c
    weigh_columns(c, tile_ref, out_ref)


def rows_after(target, parts_ref, last_ref, tile_ref, out_ref, c_ref):
    c = last_ref[...] * (target / jnp.sum(parts_ref[...].astype(F32), axis=0))
    c_ref[...] = c
    weigh_columns(c, tile_ref, out_ref)


def columns_after(parts_ref, w_ref, c_ref, tile_ref, out_ref):
    groups = tile_ref.shape[1] // LANES
    u = w_ref[...] / jnp.sum(parts_ref[...].astype(F32), axis=0)
    lane = lane_iota()
    sums = jnp.zeros((LANES, LANES), F32)
    for r in range(tile_ref.shape[0] // LANES):
        total = jnp.zeros((LANES, LANES), F32)
        for g in range(groups):
            total = total + tile_ref[r * LANES : (r + 1) * LANES, g * LANES : (g + 1) * LANES] * u[g : g + 1, :]
        sums = jnp.where(lane == r, jnp.sum(total, axis=1, keepdims=True), sums)
    out = sums.T[0:8, :] * c_ref[...]
    out_ref[...] = jnp.broadcast_to(out[None], out_ref.shape).astype(out_ref.dtype)


def half_sums(side, u, c_ref, tile_ref, docs_ref, out_ref, p_ref):
    n_half, n_doc = p_ref.shape
    groups = n_doc // LANES
    blocks = n_half // LANES
    cols = to_columns(c_ref[pl.ds(side * blocks, blocks), :])
    base = pl.multiple_of(side * n_half, n_half)
    lane = lane_iota()
    masses = jnp.zeros((LANES, LANES), F32)
    for r in range(blocks):
        rows = pl.ds(pl.multiple_of(base + r * LANES, LANES), LANES)
        col = jnp.broadcast_to(cols[:, r : r + 1], (LANES, LANES))
        total = jnp.zeros((LANES, LANES), F32)
        for g in range(groups):
            lanes = slice(g * LANES, (g + 1) * LANES)
            p = tile_ref[rows, lanes] * u[g : g + 1, :] * col
            total = total + p
            p_ref[r * LANES : (r + 1) * LANES, lanes] = p.astype(BF16)
        masses = jnp.where(lane == r, jnp.sum(total, axis=1, keepdims=True), masses)
    mass = masses.T[0:8, :]
    out_ref[n_half : n_half + 8, :] = jnp.concatenate([mass, mass], axis=1)
    for b in range(n_half // 256):
        rows = slice(b * 256, (b + 1) * 256)
        out_ref[rows, :] = jnp.dot(p_ref[rows, :], docs_ref[...], preferred_element_type=F32)


def final_other(at_ref, parts_ref, w_ref, f_ref, c_ref, tile_ref, docs_ref, out_ref, pot_ref, u_ref, p_ref):
    u = w_ref[...] / jnp.sum(parts_ref[...].astype(F32), axis=0)
    u_ref[...] = u
    pot = (f_ref[...] + jnp.log2(u)) * LN2
    pot_ref[...] = jnp.where(at_ref[0] == 0, pot[0:8, :], pot[8:16, :])
    half_sums(1 - at_ref[1], u, c_ref, tile_ref, docs_ref, out_ref, p_ref)


def final_own(at_ref, u_ref, c_ref, tile_ref, docs_ref, out_ref, p_ref):
    half_sums(at_ref[1], u_ref[...], c_ref, tile_ref, docs_ref, out_ref, p_ref)


def final_join(own_ref, other_ref, out_ref):
    peers = out_ref.shape[0]
    n_half = own_ref.shape[0] - 8
    chunk = n_half // peers
    mass = own_ref[n_half:, 0:LANES] + other_ref[n_half:, 0:LANES]
    high = mass.astype(BF16).astype(F32)
    low = mass - high
    for q in range(peers):
        for i in range(chunk // 16):
            rows = slice(q * chunk + i * 16, q * chunk + (i + 1) * 16)
            out_ref[q, :, i * 256 : (i + 1) * 256] = (own_ref[rows, :] + other_ref[rows, :]).astype(BF16)
        r = q * chunk // LANES
        pair = [jnp.broadcast_to(x[r : r + 1, :], (8, LANES)) for x in (high, low)]
        out_ref[q, :, 256 * (chunk // 16) :] = jnp.concatenate(pair, axis=0).astype(BF16)


def divide(at_ref, parts_ref, out_ref, mass_ref):
    total = parts_ref[0].astype(F32)
    for p in range(1, parts_ref.shape[0]):
        total = total + parts_ref[p].astype(F32)
    tiles = total.shape[1] // LANES - 1
    chunk = tiles * 8
    mass = total[0:8, tiles * LANES :] + total[8:16, tiles * LANES :]
    mass_ref[...] = to_columns(mass)
    col = mass_ref[pl.ds(pl.multiple_of(at_ref[2] * chunk, chunk), chunk), :]
    for i in range(chunk // 16):
        pair = [total[:, (i * 2 + h) * LANES : (i * 2 + h + 1) * LANES] / col[i * 16 : (i + 1) * 16, :] for h in range(2)]
        new = jnp.concatenate(pair, axis=1).astype(BF16)
        out_ref[:, i * 16 : (i + 1) * 16, :] = jnp.broadcast_to(new[None], (out_ref.shape[0], 16, 256))


def place_own(at_ref, x_ref, out_ref, sem):
    rows = x_ref.shape[0]
    copy = pltpu.make_async_copy(x_ref, out_ref.at[pl.ds(pl.multiple_of(at_ref[1] * rows, rows), rows), :], sem)
    copy.start()
    copy.wait()


def place_other(at_ref, x_ref, _, out_ref, sem):
    rows = x_ref.shape[0]
    copy = pltpu.make_async_copy(x_ref, out_ref.at[pl.ds(pl.multiple_of((1 - at_ref[1]) * rows, rows), rows), :], sem)
    copy.start()
    copy.wait()


def exchange(x, axes):
    return lax.all_to_all(x, axes, 0, 0)


def per_device(sizes, docs, cents, shard_ids, shard_mass):
    n_y, n_zl, n_core, n_zh, n_x = sizes
    row_peers, col_peers = n_zl * n_zh * n_x, n_y * n_core
    n_doc, n_cent = docs.shape[0] * 2, cents.shape[0] // 2
    doc_rows, cent_rows = n_doc // LANES, n_cent // LANES
    scale = 4.0 * docs.shape[1] ** -0.5 * LOG2E
    target = 0.5 * (docs.shape[0] * n_y * n_zl * n_core) / (cents.shape[0] * n_zh * n_x)
    zl = lax.axis_index("zl")
    core = lax.axis_index("core")
    at = jnp.stack([zl, core, lax.axis_index("y") & 1]).astype(jnp.int32)
    swap = [(0, 1), (1, 0)]
    shape = jax.ShapeDtypeStruct
    tile_shape = pltpu.VMEM((n_cent, n_doc), F32)
    small = shape((cent_rows, LANES), F32)

    any_space = pl.BlockSpec(memory_space=pl.ANY)
    hbm = pl.BlockSpec(memory_space=pltpu.HBM)
    smem = pl.BlockSpec(memory_space=pltpu.SMEM)
    other_docs = lax.ppermute(docs, "zl", swap)
    parts, docs, cents, own_w = call(
        functools.partial(first_rows, scale),
        (
            shape((row_peers, doc_rows // 2, LANES), F32),
            pltpu.VMEM(docs.shape, BF16),
            pltpu.VMEM(cents.shape, BF16),
            shape((doc_rows // 2, LANES), F32),
        ),
        4,
        in_specs=[hbm] * 4,
        scratch=[pltpu.SMEM(shard_mass.shape, jnp.int32), pltpu.VMEM((doc_rows // 2, LANES), jnp.int32), pltpu.SemaphoreType.DMA((7,))],
        flops=2 * docs.shape[0] * cents.shape[0] * 256,
    )(*[pltpu.with_memory_space_constraint(x, pltpu.HBM) for x in (shard_mass, shard_ids.reshape(-1, LANES), docs, cents)])
    other_w = lax.ppermute(own_w, "zl", swap)
    parts = exchange(parts, ROWS)
    chunk = n_cent // col_peers
    parts, tile, top, f, w, docs_all = call(
        functools.partial(first_columns, scale, chunk),
        (
            shape((col_peers, cent_rows, LANES), F32),
            tile_shape,
            small,
            shape((doc_rows, LANES), F32),
            shape((doc_rows, LANES), F32),
            pltpu.VMEM((n_doc, 256), BF16),
        ),
        7,
        smem=(0,),
        scratch=[pltpu.VMEM((n_cent, 256), BF16)],
        flops=2 * n_doc * n_cent * 256,
    )(at, parts, own_w, other_w, docs, other_docs, cents)

    rows_out = (shape((row_peers, doc_rows, LANES), BF16), small)
    parts = exchange(parts, COLS)
    log_target = math.log2(target)
    parts, c = call(functools.partial(rows_after_first, log_target), rows_out, 3, flops=2 * n_doc * n_cent)(parts, top, tile)
    for turn in range(2):
        parts = exchange(parts, ROWS)
        parts = call(columns_after, shape((col_peers, cent_rows, LANES), F32), 4, flops=2 * n_doc * n_cent)(parts, w, c, tile)
        parts = exchange(parts, COLS)
        parts, c = call(functools.partial(rows_after, target), rows_out, 3, flops=2 * n_doc * n_cent)(parts, c, tile)
    parts = exchange(parts, ROWS)
    n_half = n_cent // n_core
    half_flops = 2 * n_doc * n_half * 256
    part_shape = pltpu.VMEM((n_half + 8, 256), F32)
    p_scratch = [pltpu.VMEM((n_half, n_doc), BF16)]
    for_other, pot, u = call(
        final_other,
        (part_shape, shape((doc_rows // 2, LANES), F32), shape((doc_rows, LANES), F32)),
        7,
        smem=(0,),
        scratch=p_scratch,
        flops=half_flops,
    )(at, parts, w, f, c, tile, docs_all)
    from_other = lax.ppermute(for_other, "core", swap)
    for_own = call(final_own, part_shape, 5, smem=(0,), scratch=p_scratch, flops=half_flops)(at, u, c, tile, docs_all)
    sums = call(final_join, shape((n_y, 16, 2 * LANES * (chunk // 16) + LANES), BF16), 2)(for_own, from_other)
    sums = exchange(sums, "y")
    new = call(divide, shape((n_y * n_zl, chunk, 256), BF16), 2, smem=(0,), scratch=[pltpu.VMEM((LANES, LANES), F32)])(at, sums)
    own = exchange(new, ("y", "zl")).reshape(n_y * n_zl * chunk, 256)
    other = lax.ppermute(own, "core", swap)
    placed = shape((cents.shape[0], 256), BF16)
    new = call(place_own, placed, 2, in_specs=[smem, any_space], out_specs=any_space, scratch=[pltpu.SemaphoreType.DMA])(at, own)
    new = call(
        place_other, placed, 3, in_specs=[smem, any_space, any_space], out_specs=any_space, scratch=[pltpu.SemaphoreType.DMA], alias={2: 0}
    )(at, other, new)
    return new, pot.reshape(-1)


SIZES = (8, 2, 2, 4, 4)


def solution(mesh, sizes=SIZES):
    fine = Mesh(mesh.devices.reshape(sizes), ("y", "zl", "core", "zh", "x"))
    docs, cents = ("y", "zl", "core"), ("zh", "x")
    return jax.shard_map(
        functools.partial(per_device, sizes),
        mesh=fine,
        in_specs=(P(docs, None), P(cents, None), P(docs), P()),
        out_specs=(P(cents, None), P(docs)),
        check_vma=False,
    )
```

```python
import functools
import math

import jax
import jax.numpy as jnp
from jax import lax
from jax.experimental import pallas as pl
from jax.experimental.pallas import tpu as pltpu
from jax.sharding import Mesh
from jax.sharding import PartitionSpec as P

LOG2E = 1.4426950408889634
LN2 = 0.6931471805599453
LANES = 128
VMEM_LIMIT = 32 * 1024 * 1024
ROWS = ("zl", "zh", "x")
COLS = ("y", "core")
F32 = jnp.float32
BF16 = jnp.bfloat16


def call(kernel, out_shape, n_in, scratch=(), flops=0, out_specs=None, in_specs=None, alias=None):
    vmem = pl.BlockSpec(memory_space=pltpu.VMEM)
    if in_specs is None:
        in_specs = [vmem] * n_in
    if out_specs is None:
        out_specs = jax.tree.map(lambda _: vmem, out_shape)
    return pl.pallas_call(
        kernel,
        out_shape=out_shape,
        in_specs=in_specs,
        out_specs=out_specs,
        scratch_shapes=list(scratch),
        input_output_aliases=alias or {},
        compiler_params=pltpu.CompilerParams(vmem_limit_bytes=VMEM_LIMIT),
        cost_estimate=pl.CostEstimate(flops=flops, bytes_accessed=1 << 20, transcendentals=0),
    )


def lane_iota():
    return lax.broadcasted_iota(jnp.int32, (LANES, LANES), 1)


def to_columns(dense):
    return jnp.concatenate([dense] * (LANES // dense.shape[0]), axis=0).T


def nt_dot(a, b):
    return lax.dot_general(a, b, (((1,), (1,)), ((), ())), preferred_element_type=F32)


def weights_of(ids, mass_ref):
    def step(s, total):
        return jnp.where(ids == s, mass_ref[s].astype(F32), total)

    return lax.fori_loop(0, mass_ref.shape[0], step, jnp.zeros(ids.shape, F32), unroll=True) * 0.125


def first_rows(
    scale, mass_hbm, ids_hbm, docs_hbm, cents_hbm, out_ref, docs_ref, cents_ref, w_ref, mass_ref, ids_ref, sems
):
    n_doc, n_cent = docs_hbm.shape[0], cents_hbm.shape[0]
    block = 512
    steps = n_cent // block
    copies = [pltpu.make_async_copy(docs_hbm, docs_ref, sems.at[steps])]
    for q in range(steps):
        rows = pl.ds(q * block, block)
        copies.append(pltpu.make_async_copy(cents_hbm.at[rows, :], cents_ref.at[rows, :], sems.at[q]))
    copies.append(pltpu.make_async_copy(mass_hbm, mass_ref, sems.at[steps + 1]))
    copies.append(pltpu.make_async_copy(ids_hbm, ids_ref, sems.at[steps + 2]))
    for copy in copies[-2:] + copies[:-2]:
        copy.start()
    copies[steps + 1].wait()
    copies[steps + 2].wait()
    w_ref[...] = weights_of(ids_ref[...], mass_ref)
    copies[0].wait()
    groups = n_doc // 256
    tops = [jnp.full((8, 256), -jnp.inf, F32)] * groups
    totals = [jnp.zeros((8, 256), F32)] * groups
    for q in range(steps):
        copies[q + 1].wait()
        cents = cents_ref[q * block : (q + 1) * block, :]
        for g in range(groups):
            s = nt_dot(cents, docs_ref[g * 256 : (g + 1) * 256, :]).reshape(block // 8, 8, 256)
            top = jnp.maximum(tops[g], jnp.max(s, axis=0) * scale)
            totals[g] = totals[g] * jnp.exp2(tops[g] - top) + jnp.sum(jnp.exp2(s * scale - top[None]), axis=0)
            tops[g] = top
    rows = []
    for g in range(groups):
        top = jnp.max(tops[g], axis=0, keepdims=True)
        lse = top + jnp.log2(jnp.sum(totals[g] * jnp.exp2(tops[g] - top), axis=0, keepdims=True))
        rows += [lse[:, 0:LANES], lse[:, LANES:256]]
    out_ref[...] = jnp.broadcast_to(jnp.concatenate(rows, axis=0)[None], out_ref.shape)


def first_columns(
    scale, chunk, parts_ref, own_w_ref, other_w_ref, docs_ref, other_ref, cents_ref,
    out_ref, tile_ref, top_ref, f_ref, w_ref, docs_all_ref, half_ref,
):
    zl = lax.axis_index("zl")
    n_doc, n_cent = docs_ref.shape[0], cents_ref.shape[0] // 2
    groups = 2 * n_doc // LANES
    docs_all_ref[pl.ds(pl.multiple_of(zl * n_doc, n_doc), n_doc), :] = docs_ref[...]
    docs_all_ref[pl.ds(pl.multiple_of((1 - zl) * n_doc, n_doc), n_doc), :] = other_ref[...]
    for q in range(n_cent // chunk):
        rows = pl.ds(pl.multiple_of(q * 2 * chunk + zl * chunk, chunk), chunk)
        half_ref[q * chunk : (q + 1) * chunk, :] = cents_ref[rows, :]
    own, other = own_w_ref[...], other_w_ref[...]
    w_ref[0:8, :] = jnp.where(zl == 0, own, other)
    w_ref[8:16, :] = jnp.where(zl == 0, other, own)
    half = parts_ref.shape[0] // 2
    for z in range(2):
        parts = parts_ref[z * half : (z + 1) * half]
        top = jnp.max(parts, axis=0)
        lse = top + jnp.log2(jnp.sum(jnp.exp2(parts - top[None]), axis=0))
        f_ref[z * 8 : (z + 1) * 8, :] = jnp.log2(w_ref[z * 8 : (z + 1) * 8, :]) - lse

    for g in range(groups // 2):
        f = jnp.concatenate([f_ref[2 * g : 2 * g + 1, :], f_ref[2 * g + 1 : 2 * g + 2, :]], axis=1)
        docs = docs_all_ref[g * 256 : (g + 1) * 256, :]
        for q in range(n_cent // 256):
            cents = half_ref[q * 256 : (q + 1) * 256, :]
            tile_ref[q * 256 : (q + 1) * 256, g * 256 : (g + 1) * 256] = nt_dot(cents, docs) * scale + f
    lane = lane_iota()
    tops = jnp.zeros((LANES, LANES), F32)
    lses = jnp.zeros((LANES, LANES), F32)
    for r in range(n_cent // LANES):
        rows = slice(r * LANES, (r + 1) * LANES)
        top = tile_ref[rows, 0:LANES]
        for g in range(1, groups):
            top = jnp.maximum(top, tile_ref[rows, g * LANES : (g + 1) * LANES])
        top = jnp.broadcast_to(jnp.max(top, axis=1, keepdims=True), (LANES, LANES))
        total = jnp.zeros((LANES, LANES), F32)
        for g in range(groups):
            e = jnp.exp2(tile_ref[rows, g * LANES : (g + 1) * LANES] - top)
            tile_ref[rows, g * LANES : (g + 1) * LANES] = e
            total = total + e
        tops = jnp.where(lane == r, top, tops)
        lses = jnp.where(lane == r, top + jnp.log2(jnp.sum(total, axis=1, keepdims=True)), lses)
    top_ref[...] = tops.T[0:8, :]
    out_ref[...] = jnp.broadcast_to(lses.T[0:8, :][None], out_ref.shape)


def weigh_columns(c, tile_ref, out_ref):
    groups = tile_ref.shape[1] // LANES
    cols = to_columns(c)
    totals = [jnp.zeros((8, LANES), F32) for _ in range(groups)]
    for r in range(tile_ref.shape[0] // LANES):
        col = jnp.broadcast_to(cols[:, r : r + 1], (LANES, LANES))
        for g in range(groups):
            p = tile_ref[r * LANES : (r + 1) * LANES, g * LANES : (g + 1) * LANES] * col
            totals[g] = totals[g] + jnp.sum(p.reshape(LANES // 8, 8, LANES), axis=0)
    rows = jnp.concatenate([jnp.sum(t, axis=0, keepdims=True) for t in totals], axis=0)
    out_ref[...] = jnp.broadcast_to(rows[None], out_ref.shape).astype(out_ref.dtype)


def rows_after_first(log_target, parts_ref, top_ref, tile_ref, out_ref, c_ref):
    parts = parts_ref[...]
    top = jnp.max(parts, axis=0)
    lse = top + jnp.log2(jnp.sum(jnp.exp2(parts - top[None]), axis=0))
    c = jnp.exp2(top_ref[...] + (log_target - lse))
    c_ref[...] = c
    weigh_columns(c, tile_ref, out_ref)


def rows_after(target, parts_ref, last_ref, tile_ref, out_ref, c_ref):
    c = last_ref[...] * (target / jnp.sum(parts_ref[...].astype(F32), axis=0))
    c_ref[...] = c
    weigh_columns(c, tile_ref, out_ref)


def columns_after(parts_ref, w_ref, c_ref, tile_ref, out_ref):
    groups = tile_ref.shape[1] // LANES
    u = w_ref[...] / jnp.sum(parts_ref[...].astype(F32), axis=0)
    lane = lane_iota()
    sums = jnp.zeros((LANES, LANES), F32)
    for r in range(tile_ref.shape[0] // LANES):
        total = jnp.zeros((LANES, LANES), F32)
        for g in range(groups):
            total = total + tile_ref[r * LANES : (r + 1) * LANES, g * LANES : (g + 1) * LANES] * u[g : g + 1, :]
        sums = jnp.where(lane == r, jnp.sum(total, axis=1, keepdims=True), sums)
    out = sums.T[0:8, :] * c_ref[...]
    out_ref[...] = jnp.broadcast_to(out[None], out_ref.shape).astype(out_ref.dtype)


def half_sums(side, u, c_ref, tile_ref, docs_ref, out_ref, p_ref):
    n_half, n_doc = p_ref.shape
    groups = n_doc // LANES
    blocks = n_half // LANES
    cols = to_columns(c_ref[pl.ds(side * blocks, blocks), :])
    base = pl.multiple_of(side * n_half, n_half)
    lane = lane_iota()
    masses = jnp.zeros((LANES, LANES), F32)
    for r in range(blocks):
        rows = pl.ds(pl.multiple_of(base + r * LANES, LANES), LANES)
        col = jnp.broadcast_to(cols[:, r : r + 1], (LANES, LANES))
        total = jnp.zeros((LANES, LANES), F32)
        for g in range(groups):
            lanes = slice(g * LANES, (g + 1) * LANES)
            p = tile_ref[rows, lanes] * u[g : g + 1, :] * col
            total = total + p
            p_ref[r * LANES : (r + 1) * LANES, lanes] = p.astype(BF16)
        masses = jnp.where(lane == r, jnp.sum(total, axis=1, keepdims=True), masses)
    mass = masses.T[0:8, :]
    out_ref[n_half : n_half + 8, :] = jnp.concatenate([mass, mass], axis=1)
    for b in range(n_half // 256):
        rows = slice(b * 256, (b + 1) * 256)
        out_ref[rows, :] = jnp.dot(p_ref[rows, :], docs_ref[...], preferred_element_type=F32)


def final_other(parts_ref, w_ref, f_ref, c_ref, tile_ref, docs_ref, out_ref, pot_ref, u_ref, p_ref):
    u = w_ref[...] / jnp.sum(parts_ref[...].astype(F32), axis=0)
    u_ref[...] = u
    pot = (f_ref[...] + jnp.log2(u)) * LN2
    pot_ref[...] = jnp.where(lax.axis_index("zl") == 0, pot[0:8, :], pot[8:16, :])
    half_sums(1 - lax.axis_index("core"), u, c_ref, tile_ref, docs_ref, out_ref, p_ref)


def final_own(u_ref, c_ref, tile_ref, docs_ref, out_ref, p_ref):
    half_sums(lax.axis_index("core"), u_ref[...], c_ref, tile_ref, docs_ref, out_ref, p_ref)


def final_join(own_ref, other_ref, out_ref):
    peers = out_ref.shape[0]
    n_half = own_ref.shape[0] - 8
    chunk = n_half // peers
    mass = own_ref[n_half:, 0:LANES] + other_ref[n_half:, 0:LANES]
    high = mass.astype(BF16).astype(F32)
    low = mass - high
    for q in range(peers):
        for i in range(chunk // 16):
            rows = slice(q * chunk + i * 16, q * chunk + (i + 1) * 16)
            out_ref[q, :, i * 256 : (i + 1) * 256] = (own_ref[rows, :] + other_ref[rows, :]).astype(BF16)
        r = q * chunk // LANES
        pair = [jnp.broadcast_to(x[r : r + 1, :], (8, LANES)) for x in (high, low)]
        out_ref[q, :, 256 * (chunk // 16) :] = jnp.concatenate(pair, axis=0).astype(BF16)


def divide(parts_ref, out_ref, mass_ref):
    total = parts_ref[0].astype(F32)
    for p in range(1, parts_ref.shape[0]):
        total = total + parts_ref[p].astype(F32)
    tiles = total.shape[1] // LANES - 1
    chunk = tiles * 8
    mass = total[0:8, tiles * LANES :] + total[8:16, tiles * LANES :]
    mass_ref[...] = to_columns(mass)
    col = mass_ref[pl.ds(pl.multiple_of((lax.axis_index("y") & 1) * chunk, chunk), chunk), :]
    for i in range(chunk // 16):
        pair = [total[:, (i * 2 + h) * LANES : (i * 2 + h + 1) * LANES] / col[i * 16 : (i + 1) * 16, :] for h in range(2)]
        new = jnp.concatenate(pair, axis=1).astype(BF16)
        out_ref[:, i * 16 : (i + 1) * 16, :] = jnp.broadcast_to(new[None], (out_ref.shape[0], 16, 256))


def place_own(x_ref, out_ref, sem):
    rows = x_ref.shape[0]
    copy = pltpu.make_async_copy(x_ref, out_ref.at[pl.ds(pl.multiple_of(lax.axis_index("core") * rows, rows), rows), :], sem)
    copy.start()
    copy.wait()


def place_other(x_ref, _, out_ref, sem):
    rows = x_ref.shape[0]
    copy = pltpu.make_async_copy(x_ref, out_ref.at[pl.ds(pl.multiple_of((1 - lax.axis_index("core")) * rows, rows), rows), :], sem)
    copy.start()
    copy.wait()


def exchange(x, axes):
    return lax.all_to_all(x, axes, 0, 0)


def per_device(sizes, docs, cents, shard_ids, shard_mass):
    n_y, n_zl, n_core, n_zh, n_x = sizes
    row_peers, col_peers = n_zl * n_zh * n_x, n_y * n_core
    n_doc, n_cent = docs.shape[0] * 2, cents.shape[0] // 2
    doc_rows, cent_rows = n_doc // LANES, n_cent // LANES
    scale = 4.0 * docs.shape[1] ** -0.5 * LOG2E
    target = 0.5 * (docs.shape[0] * n_y * n_zl * n_core) / (cents.shape[0] * n_zh * n_x)
    swap = [(0, 1), (1, 0)]
    shape = jax.ShapeDtypeStruct
    tile_shape = pltpu.VMEM((n_cent, n_doc), F32)
    small = shape((cent_rows, LANES), F32)

    any_space = pl.BlockSpec(memory_space=pl.ANY)
    hbm = pl.BlockSpec(memory_space=pltpu.HBM)
    other_docs = lax.ppermute(docs, "zl", swap)
    parts, docs, cents, own_w = call(
        functools.partial(first_rows, scale),
        (
            shape((row_peers, doc_rows // 2, LANES), F32),
            pltpu.VMEM(docs.shape, BF16),
            pltpu.VMEM(cents.shape, BF16),
            shape((doc_rows // 2, LANES), F32),
        ),
        4,
        in_specs=[hbm] * 4,
        scratch=[pltpu.SMEM(shard_mass.shape, jnp.int32), pltpu.VMEM((doc_rows // 2, LANES), jnp.int32), pltpu.SemaphoreType.DMA((7,))],
        flops=2 * docs.shape[0] * cents.shape[0] * 256,
    )(*[pltpu.with_memory_space_constraint(x, pltpu.HBM) for x in (shard_mass, shard_ids.reshape(-1, LANES), docs, cents)])
    other_w = lax.ppermute(own_w, "zl", swap)
    parts = exchange(parts, ROWS)
    chunk = n_cent // col_peers
    parts, tile, top, f, w, docs_all = call(
        functools.partial(first_columns, scale, chunk),
        (
            shape((col_peers, cent_rows, LANES), F32),
            tile_shape,
            small,
            shape((doc_rows, LANES), F32),
            shape((doc_rows, LANES), F32),
            pltpu.VMEM((n_doc, 256), BF16),
        ),
        6,
        scratch=[pltpu.VMEM((n_cent, 256), BF16)],
        flops=2 * n_doc * n_cent * 256,
    )(parts, own_w, other_w, docs, other_docs, cents)

    rows_out = (shape((row_peers, doc_rows, LANES), BF16), small)
    parts = exchange(parts, COLS)
    log_target = math.log2(target)
    parts, c = call(functools.partial(rows_after_first, log_target), rows_out, 3, flops=2 * n_doc * n_cent)(parts, top, tile)
    for turn in range(2):
        parts = exchange(parts, ROWS)
        parts = call(columns_after, shape((col_peers, cent_rows, LANES), F32), 4, flops=2 * n_doc * n_cent)(parts, w, c, tile)
        parts = exchange(parts, COLS)
        parts, c = call(functools.partial(rows_after, target), rows_out, 3, flops=2 * n_doc * n_cent)(parts, c, tile)
    parts = exchange(parts, ROWS)
    n_half = n_cent // n_core
    half_flops = 2 * n_doc * n_half * 256
    part_shape = pltpu.VMEM((n_half + 8, 256), F32)
    p_scratch = [pltpu.VMEM((n_half, n_doc), BF16)]
    for_other, pot, u = call(
        final_other,
        (part_shape, shape((doc_rows // 2, LANES), F32), shape((doc_rows, LANES), F32)),
        6,
        scratch=p_scratch,
        flops=half_flops,
    )(parts, w, f, c, tile, docs_all)
    from_other = lax.ppermute(for_other, "core", swap)
    for_own = call(final_own, part_shape, 4, scratch=p_scratch, flops=half_flops)(u, c, tile, docs_all)
    sums = call(final_join, shape((n_y, 16, 2 * LANES * (chunk // 16) + LANES), BF16), 2)(for_own, from_other)
    sums = exchange(sums, "y")
    new = call(divide, shape((n_y * n_zl, chunk, 256), BF16), 1, scratch=[pltpu.VMEM((LANES, LANES), F32)])(sums)
    own = exchange(new, ("y", "zl")).reshape(n_y * n_zl * chunk, 256)
    other = lax.ppermute(own, "core", swap)
    placed = shape((cents.shape[0], 256), BF16)
    new = call(place_own, placed, 1, in_specs=[any_space], out_specs=any_space, scratch=[pltpu.SemaphoreType.DMA])(own)
    new = call(
        place_other, placed, 2, in_specs=[any_space, any_space], out_specs=any_space, scratch=[pltpu.SemaphoreType.DMA], alias={1: 0}
    )(other, new)
    return new, pot.reshape(-1)


SIZES = (8, 2, 2, 4, 4)


def solution(mesh, sizes=SIZES):
    fine = Mesh(mesh.devices.reshape(sizes), ("y", "zl", "core", "zh", "x"))
    docs, cents = ("y", "zl", "core"), ("zh", "x")
    return jax.shard_map(
        functools.partial(per_device, sizes),
        mesh=fine,
        in_specs=(P(docs, None), P(cents, None), P(docs), P()),
        out_specs=(P(cents, None), P(docs)),
        check_vma=False,
    )
```

```python
import functools
import math

import jax
import jax.numpy as jnp
from jax import lax
from jax.experimental import pallas as pl
from jax.experimental.pallas import tpu as pltpu
from jax.sharding import Mesh
from jax.sharding import PartitionSpec as P

LOG2E = 1.4426950408889634
LN2 = 0.6931471805599453
LANES = 128
VMEM_LIMIT = 32 * 1024 * 1024
ROWS = ("x", "zl", "zh")
COLS = ("y", "core")
F32 = jnp.float32
BF16 = jnp.bfloat16


def call(kernel, out_shape, n_in, scratch=(), flops=0, out_specs=None, in_specs=None, alias=None):
    vmem = pl.BlockSpec(memory_space=pltpu.VMEM)
    if in_specs is None:
        in_specs = [vmem] * n_in
    if out_specs is None:
        out_specs = jax.tree.map(lambda _: vmem, out_shape)
    return pl.pallas_call(
        kernel,
        out_shape=out_shape,
        in_specs=in_specs,
        out_specs=out_specs,
        scratch_shapes=list(scratch),
        input_output_aliases=alias or {},
        compiler_params=pltpu.CompilerParams(vmem_limit_bytes=VMEM_LIMIT),
        cost_estimate=pl.CostEstimate(flops=flops, bytes_accessed=1 << 20, transcendentals=0),
    )


def lane_iota():
    return lax.broadcasted_iota(jnp.int32, (LANES, LANES), 1)


def to_columns(dense):
    return jnp.concatenate([dense] * (LANES // dense.shape[0]), axis=0).T


def nt_dot(a, b):
    return lax.dot_general(a, b, (((1,), (1,)), ((), ())), preferred_element_type=F32)


def weights_of(ids, mass_ref):
    def step(s, total):
        return jnp.where(ids == s, mass_ref[s].astype(F32), total)

    return lax.fori_loop(0, mass_ref.shape[0], step, jnp.zeros(ids.shape, F32), unroll=True) * 0.125


def first_rows(
    scale, mass_hbm, ids_hbm, docs_hbm, cents_hbm, out_ref, docs_ref, cents_ref, w_ref, mass_ref, ids_ref, sems
):
    n_doc, n_cent = docs_hbm.shape[0], cents_hbm.shape[0]
    block = 512
    steps = n_cent // block
    copies = [pltpu.make_async_copy(docs_hbm, docs_ref, sems.at[steps])]
    for q in range(steps):
        rows = pl.ds(q * block, block)
        copies.append(pltpu.make_async_copy(cents_hbm.at[rows, :], cents_ref.at[rows, :], sems.at[q]))
    copies.append(pltpu.make_async_copy(mass_hbm, mass_ref, sems.at[steps + 1]))
    copies.append(pltpu.make_async_copy(ids_hbm, ids_ref, sems.at[steps + 2]))
    for copy in copies[-2:] + copies[:-2]:
        copy.start()
    copies[steps + 1].wait()
    copies[steps + 2].wait()
    w_ref[...] = weights_of(ids_ref[...], mass_ref)
    copies[0].wait()
    groups = n_doc // 256
    tops = [jnp.full((8, 256), -jnp.inf, F32)] * groups
    totals = [jnp.zeros((8, 256), F32)] * groups
    for q in range(steps):
        copies[q + 1].wait()
        cents = cents_ref[q * block : (q + 1) * block, :]
        for g in range(groups):
            s = nt_dot(cents, docs_ref[g * 256 : (g + 1) * 256, :]).reshape(block // 8, 8, 256)
            top = jnp.maximum(tops[g], jnp.max(s, axis=0) * scale)
            totals[g] = totals[g] * jnp.exp2(tops[g] - top) + jnp.sum(jnp.exp2(s * scale - top[None]), axis=0)
            tops[g] = top
    rows = []
    for g in range(groups):
        top = jnp.max(tops[g], axis=0, keepdims=True)
        lse = top + jnp.log2(jnp.sum(totals[g] * jnp.exp2(tops[g] - top), axis=0, keepdims=True))
        rows += [lse[:, 0:LANES], lse[:, LANES:256]]
    out_ref[...] = jnp.broadcast_to(jnp.concatenate(rows, axis=0)[None], out_ref.shape)


def first_columns(
    scale, n_x, chunk, parts_ref, own_w_ref, other_w_ref, docs_ref, other_ref, cents_ref,
    out_ref, tile_ref, top_ref, f_ref, w_ref, docs_all_ref, half_ref,
):
    zl = lax.axis_index("zl")
    n_doc, n_cent = docs_ref.shape[0], cents_ref.shape[0] // 2
    groups = 2 * n_doc // LANES
    docs_all_ref[pl.ds(pl.multiple_of(zl * n_doc, n_doc), n_doc), :] = docs_ref[...]
    docs_all_ref[pl.ds(pl.multiple_of((1 - zl) * n_doc, n_doc), n_doc), :] = other_ref[...]
    for q in range(n_cent // chunk):
        rows = pl.ds(pl.multiple_of(q * 2 * chunk + zl * chunk, chunk), chunk)
        half_ref[q * chunk : (q + 1) * chunk, :] = cents_ref[rows, :]
    own, other = own_w_ref[...], other_w_ref[...]
    w_ref[0:8, :] = jnp.where(zl == 0, own, other)
    w_ref[8:16, :] = jnp.where(zl == 0, other, own)
    by_zl = parts_ref[...].reshape(n_x, 2, parts_ref.shape[0] // (2 * n_x), 8, LANES)
    for z in range(2):
        parts = by_zl[:, z].reshape(parts_ref.shape[0] // 2, 8, LANES)
        top = jnp.max(parts, axis=0)
        lse = top + jnp.log2(jnp.sum(jnp.exp2(parts - top[None]), axis=0))
        f_ref[z * 8 : (z + 1) * 8, :] = jnp.log2(w_ref[z * 8 : (z + 1) * 8, :]) - lse

    for g in range(groups // 2):
        f = jnp.concatenate([f_ref[2 * g : 2 * g + 1, :], f_ref[2 * g + 1 : 2 * g + 2, :]], axis=1)
        docs = docs_all_ref[g * 256 : (g + 1) * 256, :]
        for q in range(n_cent // 256):
            cents = half_ref[q * 256 : (q + 1) * 256, :]
            tile_ref[q * 256 : (q + 1) * 256, g * 256 : (g + 1) * 256] = nt_dot(cents, docs) * scale + f
    lane = lane_iota()
    tops = jnp.zeros((LANES, LANES), F32)
    lses = jnp.zeros((LANES, LANES), F32)
    for r in range(n_cent // LANES):
        rows = slice(r * LANES, (r + 1) * LANES)
        top = tile_ref[rows, 0:LANES]
        for g in range(1, groups):
            top = jnp.maximum(top, tile_ref[rows, g * LANES : (g + 1) * LANES])
        top = jnp.broadcast_to(jnp.max(top, axis=1, keepdims=True), (LANES, LANES))
        total = jnp.zeros((LANES, LANES), F32)
        for g in range(groups):
            e = jnp.exp2(tile_ref[rows, g * LANES : (g + 1) * LANES] - top)
            tile_ref[rows, g * LANES : (g + 1) * LANES] = e
            total = total + e
        tops = jnp.where(lane == r, top, tops)
        lses = jnp.where(lane == r, top + jnp.log2(jnp.sum(total, axis=1, keepdims=True)), lses)
    top_ref[...] = tops.T[0:8, :]
    out_ref[...] = jnp.broadcast_to(lses.T[0:8, :][None], out_ref.shape)


def weigh_columns(c, tile_ref, out_ref):
    groups = tile_ref.shape[1] // LANES
    cols = to_columns(c)
    totals = [jnp.zeros((8, LANES), F32) for _ in range(groups)]
    for r in range(tile_ref.shape[0] // LANES):
        col = jnp.broadcast_to(cols[:, r : r + 1], (LANES, LANES))
        for g in range(groups):
            p = tile_ref[r * LANES : (r + 1) * LANES, g * LANES : (g + 1) * LANES] * col
            totals[g] = totals[g] + jnp.sum(p.reshape(LANES // 8, 8, LANES), axis=0)
    rows = jnp.concatenate([jnp.sum(t, axis=0, keepdims=True) for t in totals], axis=0)
    out_ref[...] = jnp.broadcast_to(rows[None], out_ref.shape).astype(out_ref.dtype)


def rows_after_first(log_target, parts_ref, top_ref, tile_ref, out_ref, c_ref):
    parts = parts_ref[...]
    top = jnp.max(parts, axis=0)
    lse = top + jnp.log2(jnp.sum(jnp.exp2(parts - top[None]), axis=0))
    c = jnp.exp2(top_ref[...] + (log_target - lse))
    c_ref[...] = c
    weigh_columns(c, tile_ref, out_ref)


def rows_after(target, parts_ref, last_ref, tile_ref, out_ref, c_ref):
    c = last_ref[...] * (target / jnp.sum(parts_ref[...].astype(F32), axis=0))
    c_ref[...] = c
    weigh_columns(c, tile_ref, out_ref)


def columns_after(parts_ref, w_ref, c_ref, tile_ref, out_ref):
    groups = tile_ref.shape[1] // LANES
    u = w_ref[...] / jnp.sum(parts_ref[...].astype(F32), axis=0)
    lane = lane_iota()
    sums = jnp.zeros((LANES, LANES), F32)
    for r in range(tile_ref.shape[0] // LANES):
        total = jnp.zeros((LANES, LANES), F32)
        for g in range(groups):
            total = total + tile_ref[r * LANES : (r + 1) * LANES, g * LANES : (g + 1) * LANES] * u[g : g + 1, :]
        sums = jnp.where(lane == r, jnp.sum(total, axis=1, keepdims=True), sums)
    out = sums.T[0:8, :] * c_ref[...]
    out_ref[...] = jnp.broadcast_to(out[None], out_ref.shape).astype(out_ref.dtype)


def half_sums(side, u, c_ref, tile_ref, docs_ref, out_ref, p_ref):
    n_half, n_doc = p_ref.shape
    groups = n_doc // LANES
    blocks = n_half // LANES
    cols = to_columns(c_ref[pl.ds(side * blocks, blocks), :])
    base = pl.multiple_of(side * n_half, n_half)
    lane = lane_iota()
    masses = jnp.zeros((LANES, LANES), F32)
    for r in range(blocks):
        rows = pl.ds(pl.multiple_of(base + r * LANES, LANES), LANES)
        col = jnp.broadcast_to(cols[:, r : r + 1], (LANES, LANES))
        total = jnp.zeros((LANES, LANES), F32)
        for g in range(groups):
            lanes = slice(g * LANES, (g + 1) * LANES)
            p = tile_ref[rows, lanes] * u[g : g + 1, :] * col
            total = total + p
            p_ref[r * LANES : (r + 1) * LANES, lanes] = p.astype(BF16)
        masses = jnp.where(lane == r, jnp.sum(total, axis=1, keepdims=True), masses)
    mass = masses.T[0:8, :]
    out_ref[n_half : n_half + 8, :] = jnp.concatenate([mass, mass], axis=1)
    for b in range(n_half // 256):
        rows = slice(b * 256, (b + 1) * 256)
        out_ref[rows, :] = jnp.dot(p_ref[rows, :], docs_ref[...], preferred_element_type=F32)


def final_other(parts_ref, w_ref, f_ref, c_ref, tile_ref, docs_ref, out_ref, pot_ref, u_ref, p_ref):
    u = w_ref[...] / jnp.sum(parts_ref[...].astype(F32), axis=0)
    u_ref[...] = u
    pot = (f_ref[...] + jnp.log2(u)) * LN2
    pot_ref[...] = jnp.where(lax.axis_index("zl") == 0, pot[0:8, :], pot[8:16, :])
    half_sums(1 - lax.axis_index("core"), u, c_ref, tile_ref, docs_ref, out_ref, p_ref)


def final_own(u_ref, c_ref, tile_ref, docs_ref, out_ref, p_ref):
    half_sums(lax.axis_index("core"), u_ref[...], c_ref, tile_ref, docs_ref, out_ref, p_ref)


def final_join(own_ref, other_ref, out_ref):
    peers = out_ref.shape[0]
    n_half = own_ref.shape[0] - 8
    chunk = n_half // peers
    mass = own_ref[n_half:, 0:LANES] + other_ref[n_half:, 0:LANES]
    high = mass.astype(BF16).astype(F32)
    low = mass - high
    for q in range(peers):
        for i in range(chunk // 16):
            rows = slice(q * chunk + i * 16, q * chunk + (i + 1) * 16)
            out_ref[q, :, i * 256 : (i + 1) * 256] = (own_ref[rows, :] + other_ref[rows, :]).astype(BF16)
        r = q * chunk // LANES
        pair = [jnp.broadcast_to(x[r : r + 1, :], (8, LANES)) for x in (high, low)]
        out_ref[q, :, 256 * (chunk // 16) :] = jnp.concatenate(pair, axis=0).astype(BF16)


def divide(parts_ref, out_ref, mass_ref):
    total = parts_ref[0].astype(F32)
    for p in range(1, parts_ref.shape[0]):
        total = total + parts_ref[p].astype(F32)
    tiles = total.shape[1] // LANES - 1
    chunk = tiles * 8
    mass = total[0:8, tiles * LANES :] + total[8:16, tiles * LANES :]
    mass_ref[...] = to_columns(mass)
    col = mass_ref[pl.ds(pl.multiple_of((lax.axis_index("y") & 1) * chunk, chunk), chunk), :]
    for i in range(chunk // 16):
        pair = [total[:, (i * 2 + h) * LANES : (i * 2 + h + 1) * LANES] / col[i * 16 : (i + 1) * 16, :] for h in range(2)]
        new = jnp.concatenate(pair, axis=1).astype(BF16)
        out_ref[:, i * 16 : (i + 1) * 16, :] = jnp.broadcast_to(new[None], (out_ref.shape[0], 16, 256))


def place_own(x_ref, out_ref, sem):
    rows = x_ref.shape[0]
    copy = pltpu.make_async_copy(x_ref, out_ref.at[pl.ds(pl.multiple_of(lax.axis_index("core") * rows, rows), rows), :], sem)
    copy.start()
    copy.wait()


def place_other(x_ref, _, out_ref, sem):
    rows = x_ref.shape[0]
    copy = pltpu.make_async_copy(x_ref, out_ref.at[pl.ds(pl.multiple_of((1 - lax.axis_index("core")) * rows, rows), rows), :], sem)
    copy.start()
    copy.wait()


def exchange(x, axes):
    return lax.all_to_all(x, axes, 0, 0)


def per_device(sizes, docs, cents, shard_ids, shard_mass):
    n_y, n_zl, n_core, n_zh, n_x = sizes
    row_peers, col_peers = n_zl * n_zh * n_x, n_y * n_core
    n_doc, n_cent = docs.shape[0] * 2, cents.shape[0] // 2
    doc_rows, cent_rows = n_doc // LANES, n_cent // LANES
    scale = 4.0 * docs.shape[1] ** -0.5 * LOG2E
    target = 0.5 * (docs.shape[0] * n_y * n_zl * n_core) / (cents.shape[0] * n_zh * n_x)
    swap = [(0, 1), (1, 0)]
    shape = jax.ShapeDtypeStruct
    tile_shape = pltpu.VMEM((n_cent, n_doc), F32)
    small = shape((cent_rows, LANES), F32)

    any_space = pl.BlockSpec(memory_space=pl.ANY)
    hbm = pl.BlockSpec(memory_space=pltpu.HBM)
    other_docs = lax.ppermute(docs, "zl", swap)
    parts, docs, cents, own_w = call(
        functools.partial(first_rows, scale),
        (
            shape((row_peers, doc_rows // 2, LANES), F32),
            pltpu.VMEM(docs.shape, BF16),
            pltpu.VMEM(cents.shape, BF16),
            shape((doc_rows // 2, LANES), F32),
        ),
        4,
        in_specs=[hbm] * 4,
        scratch=[pltpu.SMEM(shard_mass.shape, jnp.int32), pltpu.VMEM((doc_rows // 2, LANES), jnp.int32), pltpu.SemaphoreType.DMA((7,))],
        flops=2 * docs.shape[0] * cents.shape[0] * 256,
    )(*[pltpu.with_memory_space_constraint(x, pltpu.HBM) for x in (shard_mass, shard_ids.reshape(-1, LANES), docs, cents)])
    other_w = lax.ppermute(own_w, "zl", swap)
    parts = exchange(parts, ROWS)
    chunk = n_cent // col_peers
    parts, tile, top, f, w, docs_all = call(
        functools.partial(first_columns, scale, n_x, chunk),
        (
            shape((col_peers, cent_rows, LANES), F32),
            tile_shape,
            small,
            shape((doc_rows, LANES), F32),
            shape((doc_rows, LANES), F32),
            pltpu.VMEM((n_doc, 256), BF16),
        ),
        6,
        scratch=[pltpu.VMEM((n_cent, 256), BF16)],
        flops=2 * n_doc * n_cent * 256,
    )(parts, own_w, other_w, docs, other_docs, cents)

    rows_out = (shape((row_peers, doc_rows, LANES), BF16), small)
    parts = exchange(parts, COLS)
    log_target = math.log2(target)
    parts, c = call(functools.partial(rows_after_first, log_target), rows_out, 3, flops=2 * n_doc * n_cent)(parts, top, tile)
    for turn in range(2):
        parts = exchange(parts, ROWS)
        parts = call(columns_after, shape((col_peers, cent_rows, LANES), F32), 4, flops=2 * n_doc * n_cent)(parts, w, c, tile)
        parts = exchange(parts, COLS)
        parts, c = call(functools.partial(rows_after, target), rows_out, 3, flops=2 * n_doc * n_cent)(parts, c, tile)
    parts = exchange(parts, ROWS)
    n_half = n_cent // n_core
    half_flops = 2 * n_doc * n_half * 256
    part_shape = pltpu.VMEM((n_half + 8, 256), F32)
    p_scratch = [pltpu.VMEM((n_half, n_doc), BF16)]
    for_other, pot, u = call(
        final_other,
        (part_shape, shape((doc_rows // 2, LANES), F32), shape((doc_rows, LANES), F32)),
        6,
        scratch=p_scratch,
        flops=half_flops,
    )(parts, w, f, c, tile, docs_all)
    from_other = lax.ppermute(for_other, "core", swap)
    for_own = call(final_own, part_shape, 4, scratch=p_scratch, flops=half_flops)(u, c, tile, docs_all)
    sums = call(final_join, shape((n_y, 16, 2 * LANES * (chunk // 16) + LANES), BF16), 2)(for_own, from_other)
    sums = exchange(sums, "y")
    new = call(divide, shape((n_y * n_zl, chunk, 256), BF16), 1, scratch=[pltpu.VMEM((LANES, LANES), F32)])(sums)
    own = exchange(new, ("y", "zl")).reshape(n_y * n_zl * chunk, 256)
    other = lax.ppermute(own, "core", swap)
    placed = shape((cents.shape[0], 256), BF16)
    new = call(place_own, placed, 1, in_specs=[any_space], out_specs=any_space, scratch=[pltpu.SemaphoreType.DMA])(own)
    new = call(
        place_other, placed, 2, in_specs=[any_space, any_space], out_specs=any_space, scratch=[pltpu.SemaphoreType.DMA], alias={1: 0}
    )(other, new)
    return new, pot.reshape(-1)


SIZES = (8, 2, 2, 4, 4)


def solution(mesh, sizes=SIZES):
    fine = Mesh(mesh.devices.reshape(sizes), ("y", "zl", "core", "zh", "x"))
    docs, cents = ("y", "zl", "core"), ("zh", "x")
    return jax.shard_map(
        functools.partial(per_device, sizes),
        mesh=fine,
        in_specs=(P(docs, None), P(cents, None), P(docs), P()),
        out_specs=(P(cents, None), P(docs)),
        check_vma=False,
    )
```

```python
import functools
import math

import jax
import jax.numpy as jnp
from jax import lax
from jax.experimental import pallas as pl
from jax.experimental.pallas import tpu as pltpu
from jax.sharding import Mesh
from jax.sharding import PartitionSpec as P

LOG2E = 1.4426950408889634
LN2 = 0.6931471805599453
LANES = 128
VMEM_LIMIT = 32 * 1024 * 1024
ROWS = ("x", "zl", "zh")
COLS = ("y", "core")
F32 = jnp.float32
BF16 = jnp.bfloat16


def call(kernel, out_shape, n_in, scratch=(), flops=0, out_specs=None, in_specs=None, alias=None):
    vmem = pl.BlockSpec(memory_space=pltpu.VMEM)
    if in_specs is None:
        in_specs = [vmem] * n_in
    if out_specs is None:
        out_specs = jax.tree.map(lambda _: vmem, out_shape)
    return pl.pallas_call(
        kernel,
        out_shape=out_shape,
        in_specs=in_specs,
        out_specs=out_specs,
        scratch_shapes=list(scratch),
        input_output_aliases=alias or {},
        compiler_params=pltpu.CompilerParams(vmem_limit_bytes=VMEM_LIMIT),
        cost_estimate=pl.CostEstimate(flops=flops, bytes_accessed=1 << 20, transcendentals=0),
    )


def lane_iota():
    return lax.broadcasted_iota(jnp.int32, (LANES, LANES), 1)


def to_columns(dense):
    return jnp.concatenate([dense] * (LANES // dense.shape[0]), axis=0).T


def nt_dot(a, b):
    return lax.dot_general(a, b, (((1,), (1,)), ((), ())), preferred_element_type=F32)


def weights_of(ids, mass_ref):
    def step(s, total):
        return jnp.where(ids == s, mass_ref[s].astype(F32), total)

    return lax.fori_loop(0, mass_ref.shape[0], step, jnp.zeros(ids.shape, F32), unroll=True) * 0.125


def first_rows(
    scale, mass_hbm, ids_hbm, docs_hbm, cents_hbm, out_ref, docs_ref, cents_ref, w_ref, mass_ref, ids_ref, sems
):
    n_doc, n_cent = docs_hbm.shape[0], cents_hbm.shape[0]
    block = 512
    copies = [
        pltpu.make_async_copy(src, dst, sems.at[k])
        for k, (src, dst) in enumerate(((mass_hbm, mass_ref), (ids_hbm, ids_ref), (docs_hbm, docs_ref), (cents_hbm, cents_ref)))
    ]
    for copy in copies:
        copy.start()
    copies[0].wait()
    copies[1].wait()
    w = weights_of(ids_ref[...], mass_ref)
    w_ref[...] = w
    copies[2].wait()
    copies[3].wait()
    groups = n_doc // 256
    tops = [jnp.full((8, 256), -jnp.inf, F32)] * groups
    totals = [jnp.zeros((8, 256), F32)] * groups
    for q in range(n_cent // block):
        cents = cents_ref[q * block : (q + 1) * block, :]
        for g in range(groups):
            s = nt_dot(cents, docs_ref[g * 256 : (g + 1) * 256, :]).reshape(block // 8, 8, 256)
            top = jnp.maximum(tops[g], jnp.max(s, axis=0) * scale)
            totals[g] = totals[g] * jnp.exp2(tops[g] - top) + jnp.sum(jnp.exp2(s * scale - top[None]), axis=0)
            tops[g] = top
    rows = []
    for g in range(groups):
        top = jnp.max(tops[g], axis=0, keepdims=True)
        lse = top + jnp.log2(jnp.sum(totals[g] * jnp.exp2(tops[g] - top), axis=0, keepdims=True))
        rows += [lse[:, 0:LANES], lse[:, LANES:256]]
    out_ref[...] = jnp.broadcast_to((jnp.concatenate(rows, axis=0) - jnp.log2(w))[None], out_ref.shape)


def first_columns(
    scale, n_x, chunk, parts_ref, docs_ref, other_ref, cents_ref,
    out_ref, tile_ref, top_ref, f_ref, docs_all_ref, half_ref,
):
    zl = lax.axis_index("zl")
    n_doc, n_cent = docs_ref.shape[0], cents_ref.shape[0] // 2
    groups = 2 * n_doc // LANES
    docs_all_ref[pl.ds(pl.multiple_of(zl * n_doc, n_doc), n_doc), :] = docs_ref[...]
    docs_all_ref[pl.ds(pl.multiple_of((1 - zl) * n_doc, n_doc), n_doc), :] = other_ref[...]
    for q in range(n_cent // chunk):
        rows = pl.ds(pl.multiple_of(q * 2 * chunk + zl * chunk, chunk), chunk)
        half_ref[q * chunk : (q + 1) * chunk, :] = cents_ref[rows, :]
    by_zl = parts_ref[...].reshape(n_x, 2, parts_ref.shape[0] // (2 * n_x), 8, LANES)
    for z in range(2):
        parts = by_zl[:, z].reshape(parts_ref.shape[0] // 2, 8, LANES)
        top = jnp.max(parts, axis=0)
        f_ref[z * 8 : (z + 1) * 8, :] = -(top + jnp.log2(jnp.sum(jnp.exp2(parts - top[None]), axis=0)))

    for g in range(groups // 2):
        f = jnp.concatenate([f_ref[2 * g : 2 * g + 1, :], f_ref[2 * g + 1 : 2 * g + 2, :]], axis=1)
        docs = docs_all_ref[g * 256 : (g + 1) * 256, :]
        for q in range(n_cent // 256):
            cents = half_ref[q * 256 : (q + 1) * 256, :]
            tile_ref[q * 256 : (q + 1) * 256, g * 256 : (g + 1) * 256] = nt_dot(cents, docs) * scale + f
    lane = lane_iota()
    tops = jnp.zeros((LANES, LANES), F32)
    lses = jnp.zeros((LANES, LANES), F32)
    for r in range(n_cent // LANES):
        rows = slice(r * LANES, (r + 1) * LANES)
        top = tile_ref[rows, 0:LANES]
        for g in range(1, groups):
            top = jnp.maximum(top, tile_ref[rows, g * LANES : (g + 1) * LANES])
        top = jnp.broadcast_to(jnp.max(top, axis=1, keepdims=True), (LANES, LANES))
        total = jnp.zeros((LANES, LANES), F32)
        for g in range(groups):
            e = jnp.exp2(tile_ref[rows, g * LANES : (g + 1) * LANES] - top)
            tile_ref[rows, g * LANES : (g + 1) * LANES] = e
            total = total + e
        tops = jnp.where(lane == r, top, tops)
        lses = jnp.where(lane == r, top + jnp.log2(jnp.sum(total, axis=1, keepdims=True)), lses)
    top_ref[...] = tops.T[0:8, :]
    out_ref[...] = jnp.broadcast_to(lses.T[0:8, :][None], out_ref.shape)


def weigh_columns(c, tile_ref, out_ref):
    groups = tile_ref.shape[1] // LANES
    cols = to_columns(c)
    totals = [jnp.zeros((8, LANES), F32) for _ in range(groups)]
    for r in range(tile_ref.shape[0] // LANES):
        col = jnp.broadcast_to(cols[:, r : r + 1], (LANES, LANES))
        for g in range(groups):
            p = tile_ref[r * LANES : (r + 1) * LANES, g * LANES : (g + 1) * LANES] * col
            totals[g] = totals[g] + jnp.sum(p.reshape(LANES // 8, 8, LANES), axis=0)
    rows = jnp.concatenate([jnp.sum(t, axis=0, keepdims=True) for t in totals], axis=0)
    out_ref[...] = jnp.broadcast_to(rows[None], out_ref.shape).astype(out_ref.dtype)


def rows_after_first(log_target, parts_ref, top_ref, tile_ref, out_ref, c_ref):
    parts = parts_ref[...]
    top = jnp.max(parts, axis=0)
    lse = top + jnp.log2(jnp.sum(jnp.exp2(parts - top[None]), axis=0))
    c = jnp.exp2(top_ref[...] + (log_target - lse))
    c_ref[...] = c
    weigh_columns(c, tile_ref, out_ref)


def rows_after(target, parts_ref, last_ref, tile_ref, out_ref, c_ref):
    c = last_ref[...] * (target / jnp.sum(parts_ref[...].astype(F32), axis=0))
    c_ref[...] = c
    weigh_columns(c, tile_ref, out_ref)


def in_order(own, other):
    first = lax.axis_index("zl") == 0
    return jnp.concatenate([jnp.where(first, own, other), jnp.where(first, other, own)], axis=0)


def columns_after(parts_ref, w_ref, other_w_ref, c_ref, tile_ref, out_ref):
    groups = tile_ref.shape[1] // LANES
    u = in_order(w_ref[...], other_w_ref[...]) / jnp.sum(parts_ref[...].astype(F32), axis=0)
    lane = lane_iota()
    sums = jnp.zeros((LANES, LANES), F32)
    for r in range(tile_ref.shape[0] // LANES):
        total = jnp.zeros((LANES, LANES), F32)
        for g in range(groups):
            total = total + tile_ref[r * LANES : (r + 1) * LANES, g * LANES : (g + 1) * LANES] * u[g : g + 1, :]
        sums = jnp.where(lane == r, jnp.sum(total, axis=1, keepdims=True), sums)
    out = sums.T[0:8, :] * c_ref[...]
    out_ref[...] = jnp.broadcast_to(out[None], out_ref.shape).astype(out_ref.dtype)


def half_sums(side, u, c_ref, tile_ref, docs_ref, out_ref, p_ref):
    n_half, n_doc = p_ref.shape
    groups = n_doc // LANES
    blocks = n_half // LANES
    cols = to_columns(c_ref[pl.ds(side * blocks, blocks), :])
    base = pl.multiple_of(side * n_half, n_half)
    lane = lane_iota()
    masses = jnp.zeros((LANES, LANES), F32)
    for r in range(blocks):
        rows = pl.ds(pl.multiple_of(base + r * LANES, LANES), LANES)
        col = jnp.broadcast_to(cols[:, r : r + 1], (LANES, LANES))
        total = jnp.zeros((LANES, LANES), F32)
        for g in range(groups):
            lanes = slice(g * LANES, (g + 1) * LANES)
            p = tile_ref[rows, lanes] * u[g : g + 1, :] * col
            total = total + p
            p_ref[r * LANES : (r + 1) * LANES, lanes] = p.astype(BF16)
        masses = jnp.where(lane == r, jnp.sum(total, axis=1, keepdims=True), masses)
    mass = masses.T[0:8, :]
    out_ref[n_half : n_half + 8, :] = jnp.concatenate([mass, mass], axis=1)
    for b in range(n_half // 256):
        rows = slice(b * 256, (b + 1) * 256)
        out_ref[rows, :] = jnp.dot(p_ref[rows, :], docs_ref[...], preferred_element_type=F32)


def final_other(parts_ref, w_ref, other_w_ref, f_ref, c_ref, tile_ref, docs_ref, out_ref, pot_ref, u_ref, p_ref):
    u = in_order(w_ref[...], other_w_ref[...]) / jnp.sum(parts_ref[...].astype(F32), axis=0)
    u_ref[...] = u
    pot = (f_ref[...] + jnp.log2(u)) * LN2
    pot_ref[...] = jnp.where(lax.axis_index("zl") == 0, pot[0:8, :], pot[8:16, :])
    half_sums(1 - lax.axis_index("core"), u, c_ref, tile_ref, docs_ref, out_ref, p_ref)


def final_own(u_ref, c_ref, tile_ref, docs_ref, out_ref, p_ref):
    half_sums(lax.axis_index("core"), u_ref[...], c_ref, tile_ref, docs_ref, out_ref, p_ref)


def final_join(own_ref, other_ref, out_ref):
    peers = out_ref.shape[0]
    n_half = own_ref.shape[0] - 8
    chunk = n_half // peers
    mass = own_ref[n_half:, 0:LANES] + other_ref[n_half:, 0:LANES]
    high = mass.astype(BF16).astype(F32)
    low = mass - high
    for q in range(peers):
        for i in range(chunk // 16):
            rows = slice(q * chunk + i * 16, q * chunk + (i + 1) * 16)
            out_ref[q, :, i * 256 : (i + 1) * 256] = (own_ref[rows, :] + other_ref[rows, :]).astype(BF16)
        r = q * chunk // LANES
        pair = [jnp.broadcast_to(x[r : r + 1, :], (8, LANES)) for x in (high, low)]
        out_ref[q, :, 256 * (chunk // 16) :] = jnp.concatenate(pair, axis=0).astype(BF16)


def divide(parts_ref, out_ref, mass_ref):
    total = parts_ref[0].astype(F32)
    for p in range(1, parts_ref.shape[0]):
        total = total + parts_ref[p].astype(F32)
    tiles = total.shape[1] // LANES - 1
    chunk = tiles * 8
    mass = total[0:8, tiles * LANES :] + total[8:16, tiles * LANES :]
    mass_ref[...] = to_columns(mass)
    col = mass_ref[pl.ds(pl.multiple_of((lax.axis_index("y") & 1) * chunk, chunk), chunk), :]
    for i in range(chunk // 16):
        pair = [total[:, (i * 2 + h) * LANES : (i * 2 + h + 1) * LANES] / col[i * 16 : (i + 1) * 16, :] for h in range(2)]
        new = jnp.concatenate(pair, axis=1).astype(BF16)
        out_ref[:, i * 16 : (i + 1) * 16, :] = jnp.broadcast_to(new[None], (out_ref.shape[0], 16, 256))


def place_own(x_ref, out_ref, sem):
    rows = x_ref.shape[0]
    copy = pltpu.make_async_copy(x_ref, out_ref.at[pl.ds(pl.multiple_of(lax.axis_index("core") * rows, rows), rows), :], sem)
    copy.start()
    copy.wait()


def place_other(x_ref, _, out_ref, sem):
    rows = x_ref.shape[0]
    copy = pltpu.make_async_copy(x_ref, out_ref.at[pl.ds(pl.multiple_of((1 - lax.axis_index("core")) * rows, rows), rows), :], sem)
    copy.start()
    copy.wait()


def exchange(x, axes):
    return lax.all_to_all(x, axes, 0, 0)


def per_device(sizes, docs, cents, shard_ids, shard_mass):
    n_y, n_zl, n_core, n_zh, n_x = sizes
    row_peers, col_peers = n_zl * n_zh * n_x, n_y * n_core
    n_doc, n_cent = docs.shape[0] * 2, cents.shape[0] // 2
    doc_rows, cent_rows = n_doc // LANES, n_cent // LANES
    scale = 4.0 * docs.shape[1] ** -0.5 * LOG2E
    target = 0.5 * (docs.shape[0] * n_y * n_zl * n_core) / (cents.shape[0] * n_zh * n_x)
    swap = [(0, 1), (1, 0)]
    shape = jax.ShapeDtypeStruct
    tile_shape = pltpu.VMEM((n_cent, n_doc), F32)
    small = shape((cent_rows, LANES), F32)

    any_space = pl.BlockSpec(memory_space=pl.ANY)
    hbm = pl.BlockSpec(memory_space=pltpu.HBM)
    other_docs = lax.ppermute(docs, "zl", swap)
    parts, docs, cents, own_w = call(
        functools.partial(first_rows, scale),
        (
            shape((row_peers, doc_rows // 2, LANES), F32),
            pltpu.VMEM(docs.shape, BF16),
            pltpu.VMEM(cents.shape, BF16),
            shape((doc_rows // 2, LANES), F32),
        ),
        4,
        in_specs=[hbm] * 4,
        scratch=[pltpu.SMEM(shard_mass.shape, jnp.int32), pltpu.VMEM((doc_rows // 2, LANES), jnp.int32), pltpu.SemaphoreType.DMA((4,))],
        flops=2 * docs.shape[0] * cents.shape[0] * 256,
    )(*[pltpu.with_memory_space_constraint(x, pltpu.HBM) for x in (shard_mass, shard_ids.reshape(-1, LANES), docs, cents)])
    other_w = lax.ppermute(own_w, "zl", swap)
    parts = exchange(parts, ROWS)
    chunk = n_cent // col_peers
    parts, tile, top, f, docs_all = call(
        functools.partial(first_columns, scale, n_x, chunk),
        (
            shape((col_peers, cent_rows, LANES), F32),
            tile_shape,
            small,
            shape((doc_rows, LANES), F32),
            pltpu.VMEM((n_doc, 256), BF16),
        ),
        4,
        scratch=[pltpu.VMEM((n_cent, 256), BF16)],
        flops=2 * n_doc * n_cent * 256,
    )(parts, docs, other_docs, cents)

    rows_out = (shape((row_peers, doc_rows, LANES), BF16), small)
    parts = exchange(parts, COLS)
    log_target = math.log2(target)
    parts, c = call(functools.partial(rows_after_first, log_target), rows_out, 3, flops=2 * n_doc * n_cent)(parts, top, tile)
    for turn in range(2):
        parts = exchange(parts, ROWS)
        parts = call(columns_after, shape((col_peers, cent_rows, LANES), F32), 5, flops=2 * n_doc * n_cent)(parts, own_w, other_w, c, tile)
        parts = exchange(parts, COLS)
        parts, c = call(functools.partial(rows_after, target), rows_out, 3, flops=2 * n_doc * n_cent)(parts, c, tile)
    parts = exchange(parts, ROWS)
    n_half = n_cent // n_core
    half_flops = 2 * n_doc * n_half * 256
    part_shape = pltpu.VMEM((n_half + 8, 256), F32)
    p_scratch = [pltpu.VMEM((n_half, n_doc), BF16)]
    for_other, pot, u = call(
        final_other,
        (part_shape, shape((doc_rows // 2, LANES), F32), shape((doc_rows, LANES), F32)),
        7,
        scratch=p_scratch,
        flops=half_flops,
    )(parts, own_w, other_w, f, c, tile, docs_all)
    from_other = lax.ppermute(for_other, "core", swap)
    for_own = call(final_own, part_shape, 4, scratch=p_scratch, flops=half_flops)(u, c, tile, docs_all)
    sums = call(final_join, shape((n_y, 16, 2 * LANES * (chunk // 16) + LANES), BF16), 2)(for_own, from_other)
    sums = exchange(sums, "y")
    new = call(divide, shape((n_y * n_zl, chunk, 256), BF16), 1, scratch=[pltpu.VMEM((LANES, LANES), F32)])(sums)
    own = exchange(new, ("y", "zl")).reshape(n_y * n_zl * chunk, 256)
    other = lax.ppermute(own, "core", swap)
    placed = shape((cents.shape[0], 256), BF16)
    new = call(place_own, placed, 1, in_specs=[any_space], out_specs=any_space, scratch=[pltpu.SemaphoreType.DMA])(own)
    new = call(
        place_other, placed, 2, in_specs=[any_space, any_space], out_specs=any_space, scratch=[pltpu.SemaphoreType.DMA], alias={1: 0}
    )(other, new)
    return new, pot.reshape(-1)


SIZES = (8, 2, 2, 4, 4)


def solution(mesh, sizes=SIZES):
    fine = Mesh(mesh.devices.reshape(sizes), ("y", "zl", "core", "zh", "x"))
    docs, cents = ("y", "zl", "core"), ("zh", "x")
    return jax.shard_map(
        functools.partial(per_device, sizes),
        mesh=fine,
        in_specs=(P(docs, None), P(cents, None), P(docs), P()),
        out_specs=(P(cents, None), P(docs)),
        check_vma=False,
    )
```

```python
import functools
import math

import jax
import jax.numpy as jnp
from jax import lax
from jax.experimental import pallas as pl
from jax.experimental.pallas import tpu as pltpu
from jax.sharding import Mesh
from jax.sharding import PartitionSpec as P

LOG2E = 1.4426950408889634
LN2 = 0.6931471805599453
LANES = 128
VMEM_LIMIT = 32 * 1024 * 1024
ROWS = ("x", "zl", "zh")
COLS = ("y", "core")
F32 = jnp.float32
BF16 = jnp.bfloat16


def call(kernel, out_shape, n_in, scratch=(), flops=0, out_specs=None, in_specs=None, alias=None):
    vmem = pl.BlockSpec(memory_space=pltpu.VMEM)
    if in_specs is None:
        in_specs = [vmem] * n_in
    if out_specs is None:
        out_specs = jax.tree.map(lambda _: vmem, out_shape)
    return pl.pallas_call(
        kernel,
        out_shape=out_shape,
        in_specs=in_specs,
        out_specs=out_specs,
        scratch_shapes=list(scratch),
        input_output_aliases=alias or {},
        compiler_params=pltpu.CompilerParams(vmem_limit_bytes=VMEM_LIMIT),
        cost_estimate=pl.CostEstimate(flops=flops, bytes_accessed=1 << 20, transcendentals=0),
    )


def lane_iota():
    return lax.broadcasted_iota(jnp.int32, (LANES, LANES), 1)


def to_columns(dense):
    return jnp.concatenate([dense] * (LANES // dense.shape[0]), axis=0).T


def nt_dot(a, b):
    return lax.dot_general(a, b, (((1,), (1,)), ((), ())), preferred_element_type=F32)


def weights_of(ids, mass_ref):
    def step(s, total):
        return jnp.where(ids == s, mass_ref[s].astype(F32), total)

    return lax.fori_loop(0, mass_ref.shape[0], step, jnp.zeros(ids.shape, F32), unroll=True) * 0.125


def first_rows(
    scale, mass_hbm, ids_hbm, docs_hbm, cents_hbm, out_ref, docs_ref, cents_ref, w_ref, mass_ref, ids_ref, sems
):
    n_doc, n_cent = docs_hbm.shape[0], cents_hbm.shape[0]
    block = 512
    copies = [
        pltpu.make_async_copy(src, dst, sems.at[k])
        for k, (src, dst) in enumerate(((mass_hbm, mass_ref), (ids_hbm, ids_ref), (docs_hbm, docs_ref), (cents_hbm, cents_ref)))
    ]
    for copy in copies:
        copy.start()
    copies[0].wait()
    copies[1].wait()
    w_ref[...] = weights_of(ids_ref[...], mass_ref)
    copies[2].wait()
    copies[3].wait()
    groups = n_doc // 256
    tops = [jnp.full((8, 256), -jnp.inf, F32)] * groups
    totals = [jnp.zeros((8, 256), F32)] * groups
    for q in range(n_cent // block):
        cents = cents_ref[q * block : (q + 1) * block, :]
        for g in range(groups):
            s = nt_dot(cents, docs_ref[g * 256 : (g + 1) * 256, :]).reshape(block // 8, 8, 256)
            top = jnp.maximum(tops[g], jnp.max(s, axis=0) * scale)
            totals[g] = totals[g] * jnp.exp2(tops[g] - top) + jnp.sum(jnp.exp2(s * scale - top[None]), axis=0)
            tops[g] = top
    rows = []
    for g in range(groups):
        top = jnp.max(tops[g], axis=0, keepdims=True)
        lse = top + jnp.log2(jnp.sum(totals[g] * jnp.exp2(tops[g] - top), axis=0, keepdims=True))
        rows += [lse[:, 0:LANES], lse[:, LANES:256]]
    out_ref[...] = jnp.broadcast_to(jnp.concatenate(rows, axis=0)[None], out_ref.shape)


def first_columns(
    scale, n_x, chunk, parts_ref, own_w_ref, other_w_ref, docs_ref, other_ref, cents_ref,
    out_ref, tile_ref, top_ref, f_ref, w_ref, docs_all_ref, half_ref,
):
    zl = lax.axis_index("zl")
    n_doc, n_cent = docs_ref.shape[0], cents_ref.shape[0] // 2
    groups = 2 * n_doc // LANES
    docs_all_ref[pl.ds(pl.multiple_of(zl * n_doc, n_doc), n_doc), :] = docs_ref[...]
    docs_all_ref[pl.ds(pl.multiple_of((1 - zl) * n_doc, n_doc), n_doc), :] = other_ref[...]
    for q in range(n_cent // chunk):
        rows = pl.ds(pl.multiple_of(q * 2 * chunk + zl * chunk, chunk), chunk)
        half_ref[q * chunk : (q + 1) * chunk, :] = cents_ref[rows, :]
    own, other = own_w_ref[...], other_w_ref[...]
    w_ref[0:8, :] = jnp.where(zl == 0, own, other)
    w_ref[8:16, :] = jnp.where(zl == 0, other, own)
    by_zl = parts_ref[...].reshape(n_x, 2, parts_ref.shape[0] // (2 * n_x), 8, LANES)
    for z in range(2):
        parts = by_zl[:, z].reshape(parts_ref.shape[0] // 2, 8, LANES)
        top = jnp.max(parts, axis=0)
        lse = top + jnp.log2(jnp.sum(jnp.exp2(parts - top[None]), axis=0))
        f_ref[z * 8 : (z + 1) * 8, :] = jnp.log2(w_ref[z * 8 : (z + 1) * 8, :]) - lse

    for g in range(groups // 2):
        f = jnp.concatenate([f_ref[2 * g : 2 * g + 1, :], f_ref[2 * g + 1 : 2 * g + 2, :]], axis=1)
        docs = docs_all_ref[g * 256 : (g + 1) * 256, :]
        for q in range(n_cent // 256):
            cents = half_ref[q * 256 : (q + 1) * 256, :]
            tile_ref[q * 256 : (q + 1) * 256, g * 256 : (g + 1) * 256] = nt_dot(cents, docs) * scale + f
    lane = lane_iota()
    tops = jnp.zeros((LANES, LANES), F32)
    lses = jnp.zeros((LANES, LANES), F32)
    for r in range(n_cent // LANES):
        rows = slice(r * LANES, (r + 1) * LANES)
        top = tile_ref[rows, 0:LANES]
        for g in range(1, groups):
            top = jnp.maximum(top, tile_ref[rows, g * LANES : (g + 1) * LANES])
        top = jnp.broadcast_to(jnp.max(top, axis=1, keepdims=True), (LANES, LANES))
        total = jnp.zeros((LANES, LANES), F32)
        for g in range(groups):
            e = jnp.exp2(tile_ref[rows, g * LANES : (g + 1) * LANES] - top)
            tile_ref[rows, g * LANES : (g + 1) * LANES] = e
            total = total + e
        tops = jnp.where(lane == r, top, tops)
        lses = jnp.where(lane == r, top + jnp.log2(jnp.sum(total, axis=1, keepdims=True)), lses)
    top_ref[...] = tops.T[0:8, :]
    out_ref[...] = jnp.broadcast_to(lses.T[0:8, :][None], out_ref.shape)


def weigh_columns(c, tile_ref, out_ref):
    groups = tile_ref.shape[1] // LANES
    cols = to_columns(c)
    totals = [jnp.zeros((8, LANES), F32) for _ in range(groups)]
    for r in range(tile_ref.shape[0] // LANES):
        col = jnp.broadcast_to(cols[:, r : r + 1], (LANES, LANES))
        for g in range(groups):
            p = tile_ref[r * LANES : (r + 1) * LANES, g * LANES : (g + 1) * LANES] * col
            totals[g] = totals[g] + jnp.sum(p.reshape(LANES // 8, 8, LANES), axis=0)
    rows = jnp.concatenate([jnp.sum(t, axis=0, keepdims=True) for t in totals], axis=0)
    out_ref[...] = jnp.broadcast_to(rows[None], out_ref.shape).astype(out_ref.dtype)


def rows_after_first(log_target, parts_ref, top_ref, tile_ref, out_ref, c_ref):
    parts = parts_ref[...]
    top = jnp.max(parts, axis=0)
    lse = top + jnp.log2(jnp.sum(jnp.exp2(parts - top[None]), axis=0))
    c = jnp.exp2(top_ref[...] + (log_target - lse))
    c_ref[...] = c
    weigh_columns(c, tile_ref, out_ref)


def rows_after(target, parts_ref, last_ref, tile_ref, out_ref, c_ref):
    c = last_ref[...] * (target / jnp.sum(parts_ref[...].astype(F32), axis=0))
    c_ref[...] = c
    weigh_columns(c, tile_ref, out_ref)


def columns_after(parts_ref, w_ref, c_ref, tile_ref, out_ref):
    groups = tile_ref.shape[1] // LANES
    u = w_ref[...] / jnp.sum(parts_ref[...].astype(F32), axis=0)
    lane = lane_iota()
    sums = jnp.zeros((LANES, LANES), F32)
    for r in range(tile_ref.shape[0] // LANES):
        total = jnp.zeros((LANES, LANES), F32)
        for g in range(groups):
            total = total + tile_ref[r * LANES : (r + 1) * LANES, g * LANES : (g + 1) * LANES] * u[g : g + 1, :]
        sums = jnp.where(lane == r, jnp.sum(total, axis=1, keepdims=True), sums)
    out = sums.T[0:8, :] * c_ref[...]
    out_ref[...] = jnp.broadcast_to(out[None], out_ref.shape).astype(out_ref.dtype)


def half_sums(side, u, c_ref, tile_ref, docs_ref, out_ref, p_ref):
    n_half, n_doc = p_ref.shape
    groups = n_doc // LANES
    blocks = n_half // LANES
    cols = to_columns(c_ref[pl.ds(side * blocks, blocks), :])
    base = pl.multiple_of(side * n_half, n_half)
    lane = lane_iota()
    masses = jnp.zeros((LANES, LANES), F32)
    for r in range(blocks):
        rows = pl.ds(pl.multiple_of(base + r * LANES, LANES), LANES)
        col = jnp.broadcast_to(cols[:, r : r + 1], (LANES, LANES))
        total = jnp.zeros((LANES, LANES), F32)
        for g in range(groups):
            lanes = slice(g * LANES, (g + 1) * LANES)
            p = tile_ref[rows, lanes] * u[g : g + 1, :] * col
            total = total + p
            p_ref[r * LANES : (r + 1) * LANES, lanes] = p.astype(BF16)
        masses = jnp.where(lane == r, jnp.sum(total, axis=1, keepdims=True), masses)
    mass = masses.T[0:8, :]
    out_ref[n_half : n_half + 8, :] = jnp.concatenate([mass, mass], axis=1)
    for b in range(n_half // 256):
        rows = slice(b * 256, (b + 1) * 256)
        out_ref[rows, :] = jnp.dot(p_ref[rows, :], docs_ref[...], preferred_element_type=F32)


def final_other(parts_ref, w_ref, f_ref, c_ref, tile_ref, docs_ref, out_ref, pot_ref, u_ref, p_ref):
    u = w_ref[...] / jnp.sum(parts_ref[...].astype(F32), axis=0)
    u_ref[...] = u
    pot = (f_ref[...] + jnp.log2(u)) * LN2
    pot_ref[...] = jnp.where(lax.axis_index("zl") == 0, pot[0:8, :], pot[8:16, :])
    half_sums(1 - lax.axis_index("core"), u, c_ref, tile_ref, docs_ref, out_ref, p_ref)


def final_own(u_ref, c_ref, tile_ref, docs_ref, out_ref, p_ref):
    half_sums(lax.axis_index("core"), u_ref[...], c_ref, tile_ref, docs_ref, out_ref, p_ref)


def final_join(own_ref, other_ref, out_ref):
    peers = out_ref.shape[0]
    n_half = own_ref.shape[0] - 8
    chunk = n_half // peers
    mass = own_ref[n_half:, 0:LANES] + other_ref[n_half:, 0:LANES]
    high = mass.astype(BF16).astype(F32)
    low = mass - high
    for q in range(peers):
        for i in range(chunk // 16):
            rows = slice(q * chunk + i * 16, q * chunk + (i + 1) * 16)
            out_ref[q, :, i * 256 : (i + 1) * 256] = (own_ref[rows, :] + other_ref[rows, :]).astype(BF16)
        r = q * chunk // LANES
        pair = [jnp.broadcast_to(x[r : r + 1, :], (8, LANES)) for x in (high, low)]
        out_ref[q, :, 256 * (chunk // 16) :] = jnp.concatenate(pair, axis=0).astype(BF16)


def divide(parts_ref, out_ref, mass_ref):
    total = parts_ref[0].astype(F32)
    for p in range(1, parts_ref.shape[0]):
        total = total + parts_ref[p].astype(F32)
    tiles = total.shape[1] // LANES - 1
    chunk = tiles * 8
    mass = total[0:8, tiles * LANES :] + total[8:16, tiles * LANES :]
    mass_ref[...] = to_columns(mass)
    col = mass_ref[pl.ds(pl.multiple_of((lax.axis_index("y") & 1) * chunk, chunk), chunk), :]
    for i in range(chunk // 16):
        pair = [total[:, (i * 2 + h) * LANES : (i * 2 + h + 1) * LANES] / col[i * 16 : (i + 1) * 16, :] for h in range(2)]
        new = jnp.concatenate(pair, axis=1).astype(BF16)
        out_ref[:, i * 16 : (i + 1) * 16, :] = jnp.broadcast_to(new[None], (out_ref.shape[0], 16, 256))


def place_own(x_ref, out_ref, sem):
    rows = x_ref.shape[0]
    copy = pltpu.make_async_copy(x_ref, out_ref.at[pl.ds(pl.multiple_of(lax.axis_index("core") * rows, rows), rows), :], sem)
    copy.start()
    copy.wait()


def place_other(x_ref, _, out_ref, sem):
    rows = x_ref.shape[0]
    copy = pltpu.make_async_copy(x_ref, out_ref.at[pl.ds(pl.multiple_of((1 - lax.axis_index("core")) * rows, rows), rows), :], sem)
    copy.start()
    copy.wait()


def exchange(x, axes):
    return lax.all_to_all(x, axes, 0, 0)


def per_device(sizes, docs, cents, shard_ids, shard_mass):
    n_y, n_zl, n_core, n_zh, n_x = sizes
    row_peers, col_peers = n_zl * n_zh * n_x, n_y * n_core
    n_doc, n_cent = docs.shape[0] * 2, cents.shape[0] // 2
    doc_rows, cent_rows = n_doc // LANES, n_cent // LANES
    scale = 4.0 * docs.shape[1] ** -0.5 * LOG2E
    target = 0.5 * (docs.shape[0] * n_y * n_zl * n_core) / (cents.shape[0] * n_zh * n_x)
    swap = [(0, 1), (1, 0)]
    shape = jax.ShapeDtypeStruct
    tile_shape = pltpu.VMEM((n_cent, n_doc), F32)
    small = shape((cent_rows, LANES), F32)

    any_space = pl.BlockSpec(memory_space=pl.ANY)
    hbm = pl.BlockSpec(memory_space=pltpu.HBM)
    other_docs = lax.ppermute(docs, "zl", swap)
    parts, docs, cents, own_w = call(
        functools.partial(first_rows, scale),
        (
            shape((row_peers, doc_rows // 2, LANES), F32),
            pltpu.VMEM(docs.shape, BF16),
            pltpu.VMEM(cents.shape, BF16),
            shape((doc_rows // 2, LANES), F32),
        ),
        4,
        in_specs=[hbm] * 4,
        scratch=[pltpu.SMEM(shard_mass.shape, jnp.int32), pltpu.VMEM((doc_rows // 2, LANES), jnp.int32), pltpu.SemaphoreType.DMA((4,))],
        flops=2 * docs.shape[0] * cents.shape[0] * 256,
    )(*[pltpu.with_memory_space_constraint(x, pltpu.HBM) for x in (shard_mass, shard_ids.reshape(-1, LANES), docs, cents)])
    other_w = lax.ppermute(own_w, "zl", swap)
    parts = exchange(parts, ROWS)
    chunk = n_cent // col_peers
    parts, tile, top, f, w, docs_all = call(
        functools.partial(first_columns, scale, n_x, chunk),
        (
            shape((col_peers, cent_rows, LANES), F32),
            tile_shape,
            small,
            shape((doc_rows, LANES), F32),
            shape((doc_rows, LANES), F32),
            pltpu.VMEM((n_doc, 256), BF16),
        ),
        6,
        scratch=[pltpu.VMEM((n_cent, 256), BF16)],
        flops=2 * n_doc * n_cent * 256,
    )(parts, own_w, other_w, docs, other_docs, cents)

    rows_out = (shape((row_peers, doc_rows, LANES), BF16), small)
    parts = exchange(parts, COLS)
    log_target = math.log2(target)
    parts, c = call(functools.partial(rows_after_first, log_target), rows_out, 3, flops=2 * n_doc * n_cent)(parts, top, tile)
    for turn in range(2):
        parts = exchange(parts, ROWS)
        parts = call(columns_after, shape((col_peers, cent_rows, LANES), BF16), 4, flops=2 * n_doc * n_cent)(parts, w, c, tile)
        parts = exchange(parts, COLS)
        parts, c = call(functools.partial(rows_after, target), rows_out, 3, flops=2 * n_doc * n_cent)(parts, c, tile)
    parts = exchange(parts, ROWS)
    n_half = n_cent // n_core
    half_flops = 2 * n_doc * n_half * 256
    part_shape = pltpu.VMEM((n_half + 8, 256), F32)
    p_scratch = [pltpu.VMEM((n_half, n_doc), BF16)]
    for_other, pot, u = call(
        final_other,
        (part_shape, shape((doc_rows // 2, LANES), F32), shape((doc_rows, LANES), F32)),
        6,
        scratch=p_scratch,
        flops=half_flops,
    )(parts, w, f, c, tile, docs_all)
    from_other = lax.ppermute(for_other, "core", swap)
    for_own = call(final_own, part_shape, 4, scratch=p_scratch, flops=half_flops)(u, c, tile, docs_all)
    sums = call(final_join, shape((n_y, 16, 2 * LANES * (chunk // 16) + LANES), BF16), 2)(for_own, from_other)
    sums = exchange(sums, "y")
    new = call(divide, shape((n_y * n_zl, chunk, 256), BF16), 1, scratch=[pltpu.VMEM((LANES, LANES), F32)])(sums)
    own = exchange(new, ("y", "zl")).reshape(n_y * n_zl * chunk, 256)
    other = lax.ppermute(own, "core", swap)
    placed = shape((cents.shape[0], 256), BF16)
    new = call(place_own, placed, 1, in_specs=[any_space], out_specs=any_space, scratch=[pltpu.SemaphoreType.DMA])(own)
    new = call(
        place_other, placed, 2, in_specs=[any_space, any_space], out_specs=any_space, scratch=[pltpu.SemaphoreType.DMA], alias={1: 0}
    )(other, new)
    return new, pot.reshape(-1)


SIZES = (8, 2, 2, 4, 4)


def solution(mesh, sizes=SIZES):
    fine = Mesh(mesh.devices.reshape(sizes), ("y", "zl", "core", "zh", "x"))
    docs, cents = ("y", "zl", "core"), ("zh", "x")
    return jax.shard_map(
        functools.partial(per_device, sizes),
        mesh=fine,
        in_specs=(P(docs, None), P(cents, None), P(docs), P()),
        out_specs=(P(cents, None), P(docs)),
        check_vma=False,
    )
```

```python
import functools
import math

import jax
import jax.numpy as jnp
from jax import lax
from jax.experimental import pallas as pl
from jax.experimental.pallas import tpu as pltpu
from jax.sharding import Mesh
from jax.sharding import PartitionSpec as P

LOG2E = 1.4426950408889634
LN2 = 0.6931471805599453
LANES = 128
VMEM_LIMIT = 32 * 1024 * 1024
ROWS = ("x", "zl", "zh")
COLS = ("y", "core")
F32 = jnp.float32
BF16 = jnp.bfloat16


def call(kernel, out_shape, n_in, scratch=(), flops=0, out_specs=None, in_specs=None, alias=None):
    vmem = pl.BlockSpec(memory_space=pltpu.VMEM)
    if in_specs is None:
        in_specs = [vmem] * n_in
    if out_specs is None:
        out_specs = jax.tree.map(lambda _: vmem, out_shape)
    return pl.pallas_call(
        kernel,
        out_shape=out_shape,
        in_specs=in_specs,
        out_specs=out_specs,
        scratch_shapes=list(scratch),
        input_output_aliases=alias or {},
        compiler_params=pltpu.CompilerParams(vmem_limit_bytes=VMEM_LIMIT),
        cost_estimate=pl.CostEstimate(flops=flops, bytes_accessed=1 << 20, transcendentals=0),
    )


def lane_iota():
    return lax.broadcasted_iota(jnp.int32, (LANES, LANES), 1)


def to_columns(dense):
    return jnp.concatenate([dense] * (LANES // dense.shape[0]), axis=0).T


def nt_dot(a, b):
    return lax.dot_general(a, b, (((1,), (1,)), ((), ())), preferred_element_type=F32)


def weights_of(ids, mass_ref):
    def step(s, total):
        return jnp.where(ids == s, mass_ref[s].astype(F32), total)

    return lax.fori_loop(0, mass_ref.shape[0], step, jnp.zeros(ids.shape, F32), unroll=True) * 0.125


def first_rows(
    scale, mass_hbm, ids_hbm, docs_hbm, cents_hbm, out_ref, docs_ref, cents_ref, w_ref, mass_ref, ids_ref, sems
):
    n_doc, n_cent = docs_hbm.shape[0], cents_hbm.shape[0]
    block = 512
    copies = [
        pltpu.make_async_copy(src, dst, sems.at[k])
        for k, (src, dst) in enumerate(((mass_hbm, mass_ref), (ids_hbm, ids_ref), (docs_hbm, docs_ref), (cents_hbm, cents_ref)))
    ]
    for copy in copies:
        copy.start()
    copies[0].wait()
    copies[1].wait()
    w = weights_of(ids_ref[...], mass_ref)
    w_ref[...] = w
    copies[2].wait()
    copies[3].wait()
    groups = n_doc // 256
    tops = [jnp.full((8, 256), -jnp.inf, F32)] * groups
    totals = [jnp.zeros((8, 256), F32)] * groups
    for q in range(n_cent // block):
        cents = cents_ref[q * block : (q + 1) * block, :]
        for g in range(groups):
            s = nt_dot(cents, docs_ref[g * 256 : (g + 1) * 256, :]).reshape(block // 8, 8, 256)
            top = jnp.maximum(tops[g], jnp.max(s, axis=0) * scale)
            totals[g] = totals[g] * jnp.exp2(tops[g] - top) + jnp.sum(jnp.exp2(s * scale - top[None]), axis=0)
            tops[g] = top
    rows = []
    for g in range(groups):
        top = jnp.max(tops[g], axis=0, keepdims=True)
        lse = top + jnp.log2(jnp.sum(totals[g] * jnp.exp2(tops[g] - top), axis=0, keepdims=True))
        rows += [lse[:, 0:LANES], lse[:, LANES:256]]
    out_ref[...] = jnp.broadcast_to((jnp.concatenate(rows, axis=0) - jnp.log2(w))[None], out_ref.shape)


def first_columns(
    scale, n_x, chunk, parts_ref, docs_ref, other_ref, cents_ref,
    out_ref, tile_ref, top_ref, f_ref, docs_all_ref, half_ref,
):
    zl = lax.axis_index("zl")
    n_doc, n_cent = docs_ref.shape[0], cents_ref.shape[0] // 2
    groups = 2 * n_doc // LANES
    docs_all_ref[pl.ds(pl.multiple_of(zl * n_doc, n_doc), n_doc), :] = docs_ref[...]
    docs_all_ref[pl.ds(pl.multiple_of((1 - zl) * n_doc, n_doc), n_doc), :] = other_ref[...]
    for q in range(n_cent // chunk):
        rows = pl.ds(pl.multiple_of(q * 2 * chunk + zl * chunk, chunk), chunk)
        half_ref[q * chunk : (q + 1) * chunk, :] = cents_ref[rows, :]
    by_zl = parts_ref[...].reshape(n_x, 2, parts_ref.shape[0] // (2 * n_x), 8, LANES)
    for z in range(2):
        parts = by_zl[:, z].reshape(parts_ref.shape[0] // 2, 8, LANES)
        top = jnp.max(parts, axis=0)
        f_ref[z * 8 : (z + 1) * 8, :] = -(top + jnp.log2(jnp.sum(jnp.exp2(parts - top[None]), axis=0)))

    for g in range(groups // 2):
        f = jnp.concatenate([f_ref[2 * g : 2 * g + 1, :], f_ref[2 * g + 1 : 2 * g + 2, :]], axis=1)
        docs = docs_all_ref[g * 256 : (g + 1) * 256, :]
        for q in range(n_cent // 256):
            cents = half_ref[q * 256 : (q + 1) * 256, :]
            tile_ref[q * 256 : (q + 1) * 256, g * 256 : (g + 1) * 256] = nt_dot(cents, docs) * scale + f
    lane = lane_iota()
    tops = jnp.zeros((LANES, LANES), F32)
    lses = jnp.zeros((LANES, LANES), F32)
    for r in range(n_cent // LANES):
        rows = slice(r * LANES, (r + 1) * LANES)
        top = tile_ref[rows, 0:LANES]
        for g in range(1, groups):
            top = jnp.maximum(top, tile_ref[rows, g * LANES : (g + 1) * LANES])
        top = jnp.broadcast_to(jnp.max(top, axis=1, keepdims=True), (LANES, LANES))
        total = jnp.zeros((LANES, LANES), F32)
        for g in range(groups):
            e = jnp.exp2(tile_ref[rows, g * LANES : (g + 1) * LANES] - top)
            tile_ref[rows, g * LANES : (g + 1) * LANES] = e
            total = total + e
        tops = jnp.where(lane == r, top, tops)
        lses = jnp.where(lane == r, top + jnp.log2(jnp.sum(total, axis=1, keepdims=True)), lses)
    top_ref[...] = tops.T[0:8, :]
    out_ref[...] = jnp.broadcast_to(lses.T[0:8, :][None], out_ref.shape)


def weigh_columns(c, tile_ref, out_ref):
    groups = tile_ref.shape[1] // LANES
    cols = to_columns(c)
    totals = [jnp.zeros((8, LANES), F32) for _ in range(groups)]
    for r in range(tile_ref.shape[0] // LANES):
        col = jnp.broadcast_to(cols[:, r : r + 1], (LANES, LANES))
        for g in range(groups):
            p = tile_ref[r * LANES : (r + 1) * LANES, g * LANES : (g + 1) * LANES] * col
            totals[g] = totals[g] + jnp.sum(p.reshape(LANES // 8, 8, LANES), axis=0)
    rows = jnp.concatenate([jnp.sum(t, axis=0, keepdims=True) for t in totals], axis=0)
    out_ref[:, 0:groups, :] = jnp.broadcast_to(rows[None], (out_ref.shape[0], groups, LANES)).astype(out_ref.dtype)


def rows_after_first(log_target, parts_ref, top_ref, w_ref, tile_ref, out_ref, c_ref):
    parts = parts_ref[...]
    top = jnp.max(parts, axis=0)
    lse = top + jnp.log2(jnp.sum(jnp.exp2(parts - top[None]), axis=0))
    c = jnp.exp2(top_ref[...] + (log_target - lse))
    c_ref[...] = c
    weigh_columns(c, tile_ref, out_ref)
    w = w_ref[...]
    groups = out_ref.shape[1] - w.shape[0]
    out_ref[:, groups:, :] = jnp.broadcast_to(w[None], (out_ref.shape[0], *w.shape)).astype(out_ref.dtype)


def rows_after(target, parts_ref, last_ref, tile_ref, out_ref, c_ref):
    c = last_ref[...] * (target / jnp.sum(parts_ref[...].astype(F32), axis=0))
    c_ref[...] = c
    weigh_columns(c, tile_ref, out_ref)


def columns_after_first(n_zh, parts_ref, c_ref, tile_ref, out_ref, w_ref):
    groups = w_ref.shape[0]
    w = jnp.concatenate([parts_ref[z * n_zh, groups:, :].astype(F32) for z in range(2)], axis=0)
    w_ref[...] = w
    weigh_rows(w / jnp.sum(parts_ref[:, 0:groups, :].astype(F32), axis=0), c_ref, tile_ref, out_ref)


def columns_after(parts_ref, w_ref, c_ref, tile_ref, out_ref):
    weigh_rows(w_ref[...] / jnp.sum(parts_ref[...].astype(F32), axis=0), c_ref, tile_ref, out_ref)


def weigh_rows(u, c_ref, tile_ref, out_ref):
    groups = tile_ref.shape[1] // LANES
    lane = lane_iota()
    sums = jnp.zeros((LANES, LANES), F32)
    for r in range(tile_ref.shape[0] // LANES):
        total = jnp.zeros((LANES, LANES), F32)
        for g in range(groups):
            total = total + tile_ref[r * LANES : (r + 1) * LANES, g * LANES : (g + 1) * LANES] * u[g : g + 1, :]
        sums = jnp.where(lane == r, jnp.sum(total, axis=1, keepdims=True), sums)
    out = sums.T[0:8, :] * c_ref[...]
    out_ref[...] = jnp.broadcast_to(out[None], out_ref.shape).astype(out_ref.dtype)


def half_sums(side, u, c_ref, tile_ref, docs_ref, out_ref, p_ref):
    n_half, n_doc = p_ref.shape
    groups = n_doc // LANES
    blocks = n_half // LANES
    cols = to_columns(c_ref[pl.ds(side * blocks, blocks), :])
    base = pl.multiple_of(side * n_half, n_half)
    lane = lane_iota()
    masses = jnp.zeros((LANES, LANES), F32)
    for r in range(blocks):
        rows = pl.ds(pl.multiple_of(base + r * LANES, LANES), LANES)
        col = jnp.broadcast_to(cols[:, r : r + 1], (LANES, LANES))
        total = jnp.zeros((LANES, LANES), F32)
        for g in range(groups):
            lanes = slice(g * LANES, (g + 1) * LANES)
            p = tile_ref[rows, lanes] * u[g : g + 1, :] * col
            total = total + p
            p_ref[r * LANES : (r + 1) * LANES, lanes] = p.astype(BF16)
        masses = jnp.where(lane == r, jnp.sum(total, axis=1, keepdims=True), masses)
    mass = masses.T[0:8, :]
    out_ref[n_half : n_half + 8, :] = jnp.concatenate([mass, mass], axis=1)
    for b in range(n_half // 256):
        rows = slice(b * 256, (b + 1) * 256)
        out_ref[rows, :] = jnp.dot(p_ref[rows, :], docs_ref[...], preferred_element_type=F32)


def final_other(parts_ref, w_ref, f_ref, c_ref, tile_ref, docs_ref, out_ref, pot_ref, u_ref, p_ref):
    u = w_ref[...] / jnp.sum(parts_ref[...].astype(F32), axis=0)
    u_ref[...] = u
    pot = (f_ref[...] + jnp.log2(u)) * LN2
    pot_ref[...] = jnp.where(lax.axis_index("zl") == 0, pot[0:8, :], pot[8:16, :])
    half_sums(1 - lax.axis_index("core"), u, c_ref, tile_ref, docs_ref, out_ref, p_ref)


def final_own(u_ref, c_ref, tile_ref, docs_ref, out_ref, p_ref):
    half_sums(lax.axis_index("core"), u_ref[...], c_ref, tile_ref, docs_ref, out_ref, p_ref)


def final_join(own_ref, other_ref, out_ref):
    peers = out_ref.shape[0]
    n_half = own_ref.shape[0] - 8
    chunk = n_half // peers
    mass = own_ref[n_half:, 0:LANES] + other_ref[n_half:, 0:LANES]
    high = mass.astype(BF16).astype(F32)
    low = mass - high
    for q in range(peers):
        for i in range(chunk // 16):
            rows = slice(q * chunk + i * 16, q * chunk + (i + 1) * 16)
            out_ref[q, :, i * 256 : (i + 1) * 256] = (own_ref[rows, :] + other_ref[rows, :]).astype(BF16)
        r = q * chunk // LANES
        pair = [jnp.broadcast_to(x[r : r + 1, :], (8, LANES)) for x in (high, low)]
        out_ref[q, :, 256 * (chunk // 16) :] = jnp.concatenate(pair, axis=0).astype(BF16)


def divide(parts_ref, out_ref, mass_ref):
    total = parts_ref[0].astype(F32)
    for p in range(1, parts_ref.shape[0]):
        total = total + parts_ref[p].astype(F32)
    tiles = total.shape[1] // LANES - 1
    chunk = tiles * 8
    mass = total[0:8, tiles * LANES :] + total[8:16, tiles * LANES :]
    mass_ref[...] = to_columns(mass)
    col = mass_ref[pl.ds(pl.multiple_of((lax.axis_index("y") & 1) * chunk, chunk), chunk), :]
    for i in range(chunk // 16):
        pair = [total[:, (i * 2 + h) * LANES : (i * 2 + h + 1) * LANES] / col[i * 16 : (i + 1) * 16, :] for h in range(2)]
        new = jnp.concatenate(pair, axis=1).astype(BF16)
        out_ref[:, i * 16 : (i + 1) * 16, :] = jnp.broadcast_to(new[None], (out_ref.shape[0], 16, 256))


def place_own(x_ref, pot_ref, out_ref, pot_out_ref, sems):
    rows = x_ref.shape[0]
    place = pl.ds(pl.multiple_of(lax.axis_index("core") * rows, rows), rows)
    copies = [pltpu.make_async_copy(x_ref, out_ref.at[place, :], sems.at[0]), pltpu.make_async_copy(pot_ref, pot_out_ref, sems.at[1])]
    for copy in copies:
        copy.start()
    for copy in copies:
        copy.wait()


def place_other(x_ref, _, out_ref, sem):
    rows = x_ref.shape[0]
    copy = pltpu.make_async_copy(x_ref, out_ref.at[pl.ds(pl.multiple_of((1 - lax.axis_index("core")) * rows, rows), rows), :], sem)
    copy.start()
    copy.wait()


def exchange(x, axes):
    return lax.all_to_all(x, axes, 0, 0)


def per_device(sizes, docs, cents, shard_ids, shard_mass):
    n_y, n_zl, n_core, n_zh, n_x = sizes
    row_peers, col_peers = n_zl * n_zh * n_x, n_y * n_core
    n_doc, n_cent = docs.shape[0] * 2, cents.shape[0] // 2
    doc_rows, cent_rows = n_doc // LANES, n_cent // LANES
    scale = 4.0 * docs.shape[1] ** -0.5 * LOG2E
    target = 0.5 * (docs.shape[0] * n_y * n_zl * n_core) / (cents.shape[0] * n_zh * n_x)
    swap = [(0, 1), (1, 0)]
    shape = jax.ShapeDtypeStruct
    tile_shape = pltpu.VMEM((n_cent, n_doc), F32)
    small = shape((cent_rows, LANES), F32)

    any_space = pl.BlockSpec(memory_space=pl.ANY)
    hbm = pl.BlockSpec(memory_space=pltpu.HBM)
    other_docs = lax.ppermute(docs, "zl", swap)
    parts, docs, cents, own_w = call(
        functools.partial(first_rows, scale),
        (
            shape((row_peers, doc_rows // 2, LANES), F32),
            pltpu.VMEM(docs.shape, BF16),
            pltpu.VMEM(cents.shape, BF16),
            shape((doc_rows // 2, LANES), F32),
        ),
        4,
        in_specs=[hbm] * 4,
        scratch=[pltpu.SMEM(shard_mass.shape, jnp.int32), pltpu.VMEM((doc_rows // 2, LANES), jnp.int32), pltpu.SemaphoreType.DMA((4,))],
        flops=2 * docs.shape[0] * cents.shape[0] * 256,
    )(*[pltpu.with_memory_space_constraint(x, pltpu.HBM) for x in (shard_mass, shard_ids.reshape(-1, LANES), docs, cents)])
    parts = exchange(parts, ROWS)
    chunk = n_cent // col_peers
    parts, tile, top, f, docs_all = call(
        functools.partial(first_columns, scale, n_x, chunk),
        (
            shape((col_peers, cent_rows, LANES), F32),
            tile_shape,
            small,
            shape((doc_rows, LANES), F32),
            pltpu.VMEM((n_doc, 256), BF16),
        ),
        4,
        scratch=[pltpu.VMEM((n_cent, 256), BF16)],
        flops=2 * n_doc * n_cent * 256,
    )(parts, docs, other_docs, cents)

    rows_out = (shape((row_peers, doc_rows, LANES), BF16), small)
    parts = exchange(parts, COLS)
    log_target = math.log2(target)
    first_out = (shape((row_peers, doc_rows + doc_rows // 2, LANES), BF16), small)
    parts, c = call(functools.partial(rows_after_first, log_target), first_out, 4, flops=2 * n_doc * n_cent)(parts, top, own_w, tile)
    col_out = shape((col_peers, cent_rows, LANES), BF16)
    for turn in range(2):
        parts = exchange(parts, ROWS)
        if turn == 0:
            out = (col_out, shape((doc_rows, LANES), F32))
            parts, w = call(functools.partial(columns_after_first, n_zh), out, 3, flops=2 * n_doc * n_cent)(parts, c, tile)
        else:
            parts = call(columns_after, col_out, 4, flops=2 * n_doc * n_cent)(parts, w, c, tile)
        parts = exchange(parts, COLS)
        parts, c = call(functools.partial(rows_after, target), rows_out, 3, flops=2 * n_doc * n_cent)(parts, c, tile)
    parts = exchange(parts, ROWS)
    n_half = n_cent // n_core
    half_flops = 2 * n_doc * n_half * 256
    part_shape = pltpu.VMEM((n_half + 8, 256), F32)
    p_scratch = [pltpu.VMEM((n_half, n_doc), BF16)]
    for_other, pot, u = call(
        final_other,
        (part_shape, pltpu.VMEM((doc_rows // 2, LANES), F32), shape((doc_rows, LANES), F32)),
        6,
        scratch=p_scratch,
        flops=half_flops,
    )(parts, w, f, c, tile, docs_all)
    from_other = lax.ppermute(for_other, "core", swap)
    for_own = call(final_own, part_shape, 4, scratch=p_scratch, flops=half_flops)(u, c, tile, docs_all)
    sums = call(final_join, shape((n_y, 16, 2 * LANES * (chunk // 16) + LANES), BF16), 2)(for_own, from_other)
    sums = exchange(sums, "y")
    new = call(divide, shape((n_y * n_zl, chunk, 256), BF16), 1, scratch=[pltpu.VMEM((LANES, LANES), F32)])(sums)
    own = exchange(new, ("y", "zl")).reshape(n_y * n_zl * chunk, 256)
    other = lax.ppermute(own, "core", swap)
    placed = shape((cents.shape[0], 256), BF16)
    new, pot = call(
        place_own,
        (placed, shape((doc_rows // 2, LANES), F32)),
        2,
        in_specs=[any_space, pl.BlockSpec(memory_space=pltpu.VMEM)],
        out_specs=(any_space, any_space),
        scratch=[pltpu.SemaphoreType.DMA((2,))],
    )(own, pot)
    new = call(
        place_other, placed, 2, in_specs=[any_space, any_space], out_specs=any_space, scratch=[pltpu.SemaphoreType.DMA], alias={1: 0}
    )(other, new)
    return new, pot.reshape(-1)


SIZES = (8, 2, 2, 4, 4)


def solution(mesh, sizes=SIZES):
    fine = Mesh(mesh.devices.reshape(sizes), ("y", "zl", "core", "zh", "x"))
    docs, cents = ("y", "zl", "core"), ("zh", "x")
    return jax.shard_map(
        functools.partial(per_device, sizes),
        mesh=fine,
        in_specs=(P(docs, None), P(cents, None), P(docs), P()),
        out_specs=(P(cents, None), P(docs)),
        check_vma=False,
    )
```

```python
import functools
import math

import jax
import jax.numpy as jnp
from jax import lax
from jax.experimental import pallas as pl
from jax.experimental.pallas import tpu as pltpu
from jax.sharding import Mesh
from jax.sharding import PartitionSpec as P

LOG2E = 1.4426950408889634
LN2 = 0.6931471805599453
LANES = 128
VMEM_LIMIT = 32 * 1024 * 1024
ROWS = ("x", "zl", "zh")
COLS = ("y", "core")
F32 = jnp.float32
BF16 = jnp.bfloat16


def call(kernel, out_shape, n_in, scratch=(), flops=0, out_specs=None, in_specs=None, alias=None):
    vmem = pl.BlockSpec(memory_space=pltpu.VMEM)
    if in_specs is None:
        in_specs = [vmem] * n_in
    if out_specs is None:
        out_specs = jax.tree.map(lambda _: vmem, out_shape)
    return pl.pallas_call(
        kernel,
        out_shape=out_shape,
        in_specs=in_specs,
        out_specs=out_specs,
        scratch_shapes=list(scratch),
        input_output_aliases=alias or {},
        compiler_params=pltpu.CompilerParams(vmem_limit_bytes=VMEM_LIMIT),
        cost_estimate=pl.CostEstimate(flops=flops, bytes_accessed=1 << 20, transcendentals=0),
    )


def lane_iota():
    return lax.broadcasted_iota(jnp.int32, (LANES, LANES), 1)


def to_columns(dense):
    return jnp.concatenate([dense] * (LANES // dense.shape[0]), axis=0).T


def nt_dot(a, b):
    return lax.dot_general(a, b, (((1,), (1,)), ((), ())), preferred_element_type=F32)


def weights_of(ids, mass_ref):
    def step(s, total):
        return jnp.where(ids == s, mass_ref[s].astype(F32), total)

    return lax.fori_loop(0, mass_ref.shape[0], step, jnp.zeros(ids.shape, F32), unroll=True) * 0.125


def first_rows(
    scale, mass_hbm, ids_hbm, docs_hbm, cents_hbm, out_ref, docs_ref, cents_ref, w_ref, mass_ref, ids_ref, sems
):
    n_doc, n_cent = docs_hbm.shape[0], cents_hbm.shape[0]
    block = 512
    copies = [
        pltpu.make_async_copy(src, dst, sems.at[k])
        for k, (src, dst) in enumerate(((mass_hbm, mass_ref), (ids_hbm, ids_ref), (docs_hbm, docs_ref), (cents_hbm, cents_ref)))
    ]
    for copy in copies:
        copy.start()
    copies[0].wait()
    copies[1].wait()
    w = weights_of(ids_ref[...], mass_ref)
    w_ref[...] = w
    copies[2].wait()
    copies[3].wait()
    groups = n_doc // 256
    tops = [jnp.full((8, 256), -jnp.inf, F32)] * groups
    totals = [jnp.zeros((8, 256), F32)] * groups
    for q in range(n_cent // block):
        cents = cents_ref[q * block : (q + 1) * block, :]
        for g in range(groups):
            s = nt_dot(cents, docs_ref[g * 256 : (g + 1) * 256, :]).reshape(block // 8, 8, 256)
            top = jnp.maximum(tops[g], jnp.max(s, axis=0) * scale)
            totals[g] = totals[g] * jnp.exp2(tops[g] - top) + jnp.sum(jnp.exp2(s * scale - top[None]), axis=0)
            tops[g] = top
    rows = []
    for g in range(groups):
        top = jnp.max(tops[g], axis=0, keepdims=True)
        lse = top + jnp.log2(jnp.sum(totals[g] * jnp.exp2(tops[g] - top), axis=0, keepdims=True))
        rows += [lse[:, 0:LANES], lse[:, LANES:256]]
    out_ref[...] = jnp.broadcast_to((jnp.concatenate(rows, axis=0) - jnp.log2(w))[None], out_ref.shape)


def first_columns(
    scale, n_x, chunk, parts_ref, docs_ref, other_ref, cents_ref,
    out_ref, tile_ref, top_ref, f_ref, docs_all_ref, half_ref,
):
    zl = lax.axis_index("zl")
    n_doc, n_cent = docs_ref.shape[0], cents_ref.shape[0] // 2
    groups = 2 * n_doc // LANES
    docs_all_ref[pl.ds(pl.multiple_of(zl * n_doc, n_doc), n_doc), :] = docs_ref[...]
    docs_all_ref[pl.ds(pl.multiple_of((1 - zl) * n_doc, n_doc), n_doc), :] = other_ref[...]
    for q in range(n_cent // chunk):
        rows = pl.ds(pl.multiple_of(q * 2 * chunk + zl * chunk, chunk), chunk)
        half_ref[q * chunk : (q + 1) * chunk, :] = cents_ref[rows, :]
    by_zl = parts_ref[...].reshape(n_x, 2, parts_ref.shape[0] // (2 * n_x), 8, LANES)
    for z in range(2):
        parts = by_zl[:, z].reshape(parts_ref.shape[0] // 2, 8, LANES)
        top = jnp.max(parts, axis=0)
        f_ref[z * 8 : (z + 1) * 8, :] = -(top + jnp.log2(jnp.sum(jnp.exp2(parts - top[None]), axis=0)))

    for g in range(groups // 2):
        f = jnp.concatenate([f_ref[2 * g : 2 * g + 1, :], f_ref[2 * g + 1 : 2 * g + 2, :]], axis=1)
        docs = docs_all_ref[g * 256 : (g + 1) * 256, :]
        for q in range(n_cent // 256):
            cents = half_ref[q * 256 : (q + 1) * 256, :]
            tile_ref[q * 256 : (q + 1) * 256, g * 256 : (g + 1) * 256] = nt_dot(cents, docs) * scale + f
    lane = lane_iota()
    tops = jnp.zeros((LANES, LANES), F32)
    lses = jnp.zeros((LANES, LANES), F32)
    for r in range(n_cent // LANES):
        rows = slice(r * LANES, (r + 1) * LANES)
        top = tile_ref[rows, 0:LANES]
        for g in range(1, groups):
            top = jnp.maximum(top, tile_ref[rows, g * LANES : (g + 1) * LANES])
        top = jnp.broadcast_to(jnp.max(top, axis=1, keepdims=True), (LANES, LANES))
        total = jnp.zeros((LANES, LANES), F32)
        for g in range(groups):
            e = jnp.exp2(tile_ref[rows, g * LANES : (g + 1) * LANES] - top)
            tile_ref[rows, g * LANES : (g + 1) * LANES] = e
            total = total + e
        tops = jnp.where(lane == r, top, tops)
        lses = jnp.where(lane == r, top + jnp.log2(jnp.sum(total, axis=1, keepdims=True)), lses)
    top_ref[...] = tops.T[0:8, :]
    out_ref[...] = jnp.broadcast_to(lses.T[0:8, :][None], out_ref.shape)


def weigh_columns(c, tile_ref, out_ref):
    groups = tile_ref.shape[1] // LANES
    totals = [jnp.zeros((8, LANES), F32) for _ in range(groups)]
    for r in range(tile_ref.shape[0] // LANES):
        col = jnp.broadcast_to(c[r : r + 1, :], (LANES, LANES)).T
        for g in range(groups):
            p = tile_ref[r * LANES : (r + 1) * LANES, g * LANES : (g + 1) * LANES] * col
            totals[g] = totals[g] + jnp.sum(p.reshape(LANES // 8, 8, LANES), axis=0)
    rows = jnp.concatenate([jnp.sum(t, axis=0, keepdims=True) for t in totals], axis=0)
    out_ref[:, 0:groups, :] = jnp.broadcast_to(rows[None], (out_ref.shape[0], groups, LANES)).astype(out_ref.dtype)


def rows_after_first(log_target, parts_ref, top_ref, w_ref, tile_ref, out_ref, c_ref):
    parts = parts_ref[...]
    top = jnp.max(parts, axis=0)
    lse = top + jnp.log2(jnp.sum(jnp.exp2(parts - top[None]), axis=0))
    c = jnp.exp2(top_ref[...] + (log_target - lse))
    c_ref[...] = c
    weigh_columns(c, tile_ref, out_ref)
    w = w_ref[...]
    groups = out_ref.shape[1] - w.shape[0]
    out_ref[:, groups:, :] = jnp.broadcast_to(w[None], (out_ref.shape[0], *w.shape)).astype(out_ref.dtype)


def rows_after(target, parts_ref, last_ref, tile_ref, out_ref, c_ref):
    c = last_ref[...] * (target / jnp.sum(parts_ref[...].astype(F32), axis=0))
    c_ref[...] = c
    weigh_columns(c, tile_ref, out_ref)


def columns_after_first(n_zh, parts_ref, c_ref, tile_ref, out_ref, w_ref):
    groups = w_ref.shape[0]
    w = jnp.concatenate([parts_ref[z * n_zh, groups:, :].astype(F32) for z in range(2)], axis=0)
    w_ref[...] = w
    weigh_rows(w / jnp.sum(parts_ref[:, 0:groups, :].astype(F32), axis=0), c_ref, tile_ref, out_ref)


def columns_after(parts_ref, w_ref, c_ref, tile_ref, out_ref):
    weigh_rows(w_ref[...] / jnp.sum(parts_ref[...].astype(F32), axis=0), c_ref, tile_ref, out_ref)


def weigh_rows(u, c_ref, tile_ref, out_ref):
    groups = tile_ref.shape[1] // LANES
    lane = lane_iota()
    sums = jnp.zeros((LANES, LANES), F32)
    for r in range(tile_ref.shape[0] // LANES):
        total = jnp.zeros((LANES, LANES), F32)
        for g in range(groups):
            total = total + tile_ref[r * LANES : (r + 1) * LANES, g * LANES : (g + 1) * LANES] * u[g : g + 1, :]
        sums = jnp.where(lane == r, jnp.sum(total, axis=1, keepdims=True), sums)
    out = sums.T[0:8, :] * c_ref[...]
    out_ref[...] = jnp.broadcast_to(out[None], out_ref.shape).astype(out_ref.dtype)


def half_sums(side, u, c_ref, tile_ref, docs_ref, out_ref, p_ref):
    n_half, n_doc = p_ref.shape
    groups = n_doc // LANES
    blocks = n_half // LANES
    cols = to_columns(c_ref[pl.ds(side * blocks, blocks), :])
    base = pl.multiple_of(side * n_half, n_half)
    lane = lane_iota()
    masses = jnp.zeros((LANES, LANES), F32)
    for r in range(blocks):
        rows = pl.ds(pl.multiple_of(base + r * LANES, LANES), LANES)
        col = jnp.broadcast_to(cols[:, r : r + 1], (LANES, LANES))
        total = jnp.zeros((LANES, LANES), F32)
        for g in range(groups):
            lanes = slice(g * LANES, (g + 1) * LANES)
            p = tile_ref[rows, lanes] * u[g : g + 1, :] * col
            total = total + p
            p_ref[r * LANES : (r + 1) * LANES, lanes] = p.astype(BF16)
        masses = jnp.where(lane == r, jnp.sum(total, axis=1, keepdims=True), masses)
    mass = masses.T[0:8, :]
    out_ref[n_half : n_half + 8, :] = jnp.concatenate([mass, mass], axis=1)
    for b in range(n_half // 256):
        rows = slice(b * 256, (b + 1) * 256)
        out_ref[rows, :] = jnp.dot(p_ref[rows, :], docs_ref[...], preferred_element_type=F32)


def final_other(parts_ref, w_ref, f_ref, c_ref, tile_ref, docs_ref, out_ref, pot_ref, u_ref, p_ref):
    u = w_ref[...] / jnp.sum(parts_ref[...].astype(F32), axis=0)
    u_ref[...] = u
    pot = (f_ref[...] + jnp.log2(u)) * LN2
    pot_ref[...] = jnp.where(lax.axis_index("zl") == 0, pot[0:8, :], pot[8:16, :])
    half_sums(1 - lax.axis_index("core"), u, c_ref, tile_ref, docs_ref, out_ref, p_ref)


def final_own(u_ref, c_ref, tile_ref, docs_ref, out_ref, p_ref):
    half_sums(lax.axis_index("core"), u_ref[...], c_ref, tile_ref, docs_ref, out_ref, p_ref)


def final_join(own_ref, other_ref, out_ref):
    peers = out_ref.shape[0]
    n_half = own_ref.shape[0] - 8
    chunk = n_half // peers
    mass = own_ref[n_half:, 0:LANES] + other_ref[n_half:, 0:LANES]
    high = mass.astype(BF16).astype(F32)
    low = mass - high
    for q in range(peers):
        for i in range(chunk // 16):
            rows = slice(q * chunk + i * 16, q * chunk + (i + 1) * 16)
            out_ref[q, :, i * 256 : (i + 1) * 256] = (own_ref[rows, :] + other_ref[rows, :]).astype(BF16)
        r = q * chunk // LANES
        pair = [jnp.broadcast_to(x[r : r + 1, :], (8, LANES)) for x in (high, low)]
        out_ref[q, :, 256 * (chunk // 16) :] = jnp.concatenate(pair, axis=0).astype(BF16)


def divide(parts_ref, out_ref, mass_ref):
    total = parts_ref[0].astype(F32)
    for p in range(1, parts_ref.shape[0]):
        total = total + parts_ref[p].astype(F32)
    tiles = total.shape[1] // LANES - 1
    chunk = tiles * 8
    mass = total[0:8, tiles * LANES :] + total[8:16, tiles * LANES :]
    mass_ref[...] = to_columns(mass)
    col = mass_ref[pl.ds(pl.multiple_of((lax.axis_index("y") & 1) * chunk, chunk), chunk), :]
    for i in range(chunk // 16):
        pair = [total[:, (i * 2 + h) * LANES : (i * 2 + h + 1) * LANES] / col[i * 16 : (i + 1) * 16, :] for h in range(2)]
        new = jnp.concatenate(pair, axis=1).astype(BF16)
        out_ref[:, i * 16 : (i + 1) * 16, :] = jnp.broadcast_to(new[None], (out_ref.shape[0], 16, 256))


def place_own(x_ref, pot_ref, out_ref, pot_out_ref, sems):
    rows = x_ref.shape[0]
    place = pl.ds(pl.multiple_of(lax.axis_index("core") * rows, rows), rows)
    copies = [pltpu.make_async_copy(x_ref, out_ref.at[place, :], sems.at[0]), pltpu.make_async_copy(pot_ref, pot_out_ref, sems.at[1])]
    for copy in copies:
        copy.start()
    for copy in copies:
        copy.wait()


def place_other(x_ref, _, out_ref, sem):
    rows = x_ref.shape[0]
    copy = pltpu.make_async_copy(x_ref, out_ref.at[pl.ds(pl.multiple_of((1 - lax.axis_index("core")) * rows, rows), rows), :], sem)
    copy.start()
    copy.wait()


def exchange(x, axes):
    return lax.all_to_all(x, axes, 0, 0)


def per_device(sizes, docs, cents, shard_ids, shard_mass):
    n_y, n_zl, n_core, n_zh, n_x = sizes
    row_peers, col_peers = n_zl * n_zh * n_x, n_y * n_core
    n_doc, n_cent = docs.shape[0] * 2, cents.shape[0] // 2
    doc_rows, cent_rows = n_doc // LANES, n_cent // LANES
    scale = 4.0 * docs.shape[1] ** -0.5 * LOG2E
    target = 0.5 * (docs.shape[0] * n_y * n_zl * n_core) / (cents.shape[0] * n_zh * n_x)
    swap = [(0, 1), (1, 0)]
    shape = jax.ShapeDtypeStruct
    tile_shape = pltpu.VMEM((n_cent, n_doc), F32)
    small = shape((cent_rows, LANES), F32)

    any_space = pl.BlockSpec(memory_space=pl.ANY)
    hbm = pl.BlockSpec(memory_space=pltpu.HBM)
    other_docs = lax.ppermute(docs, "zl", swap)
    parts, docs, cents, own_w = call(
        functools.partial(first_rows, scale),
        (
            shape((row_peers, doc_rows // 2, LANES), F32),
            pltpu.VMEM(docs.shape, BF16),
            pltpu.VMEM(cents.shape, BF16),
            shape((doc_rows // 2, LANES), F32),
        ),
        4,
        in_specs=[hbm] * 4,
        scratch=[pltpu.SMEM(shard_mass.shape, jnp.int32), pltpu.VMEM((doc_rows // 2, LANES), jnp.int32), pltpu.SemaphoreType.DMA((4,))],
        flops=2 * docs.shape[0] * cents.shape[0] * 256,
    )(*[pltpu.with_memory_space_constraint(x, pltpu.HBM) for x in (shard_mass, shard_ids.reshape(-1, LANES), docs, cents)])
    parts = exchange(parts, ROWS)
    chunk = n_cent // col_peers
    parts, tile, top, f, docs_all = call(
        functools.partial(first_columns, scale, n_x, chunk),
        (
            shape((col_peers, cent_rows, LANES), F32),
            tile_shape,
            small,
            shape((doc_rows, LANES), F32),
            pltpu.VMEM((n_doc, 256), BF16),
        ),
        4,
        scratch=[pltpu.VMEM((n_cent, 256), BF16)],
        flops=2 * n_doc * n_cent * 256,
    )(parts, docs, other_docs, cents)

    rows_out = (shape((row_peers, doc_rows, LANES), BF16), small)
    parts = exchange(parts, COLS)
    log_target = math.log2(target)
    first_out = (shape((row_peers, doc_rows + doc_rows // 2, LANES), BF16), small)
    parts, c = call(functools.partial(rows_after_first, log_target), first_out, 4, flops=2 * n_doc * n_cent)(parts, top, own_w, tile)
    col_out = shape((col_peers, cent_rows, LANES), BF16)
    for turn in range(2):
        parts = exchange(parts, ROWS)
        if turn == 0:
            out = (col_out, shape((doc_rows, LANES), F32))
            parts, w = call(functools.partial(columns_after_first, n_zh), out, 3, flops=2 * n_doc * n_cent)(parts, c, tile)
        else:
            parts = call(columns_after, col_out, 4, flops=2 * n_doc * n_cent)(parts, w, c, tile)
        parts = exchange(parts, COLS)
        parts, c = call(functools.partial(rows_after, target), rows_out, 3, flops=2 * n_doc * n_cent)(parts, c, tile)
    parts = exchange(parts, ROWS)
    n_half = n_cent // n_core
    half_flops = 2 * n_doc * n_half * 256
    part_shape = pltpu.VMEM((n_half + 8, 256), F32)
    p_scratch = [pltpu.VMEM((n_half, n_doc), BF16)]
    for_other, pot, u = call(
        final_other,
        (part_shape, pltpu.VMEM((doc_rows // 2, LANES), F32), shape((doc_rows, LANES), F32)),
        6,
        scratch=p_scratch,
        flops=half_flops,
    )(parts, w, f, c, tile, docs_all)
    from_other = lax.ppermute(for_other, "core", swap)
    for_own = call(final_own, part_shape, 4, scratch=p_scratch, flops=half_flops)(u, c, tile, docs_all)
    sums = call(final_join, shape((n_y, 16, 2 * LANES * (chunk // 16) + LANES), BF16), 2)(for_own, from_other)
    sums = exchange(sums, "y")
    new = call(divide, shape((n_y * n_zl, chunk, 256), BF16), 1, scratch=[pltpu.VMEM((LANES, LANES), F32)])(sums)
    own = exchange(new, ("y", "zl")).reshape(n_y * n_zl * chunk, 256)
    other = lax.ppermute(own, "core", swap)
    placed = shape((cents.shape[0], 256), BF16)
    new, pot = call(
        place_own,
        (placed, shape((doc_rows // 2, LANES), F32)),
        2,
        in_specs=[any_space, pl.BlockSpec(memory_space=pltpu.VMEM)],
        out_specs=(any_space, any_space),
        scratch=[pltpu.SemaphoreType.DMA((2,))],
    )(own, pot)
    new = call(
        place_other, placed, 2, in_specs=[any_space, any_space], out_specs=any_space, scratch=[pltpu.SemaphoreType.DMA], alias={1: 0}
    )(other, new)
    return new, pot.reshape(-1)


SIZES = (8, 2, 2, 4, 4)


def solution(mesh, sizes=SIZES):
    fine = Mesh(mesh.devices.reshape(sizes), ("y", "zl", "core", "zh", "x"))
    docs, cents = ("y", "zl", "core"), ("zh", "x")
    return jax.shard_map(
        functools.partial(per_device, sizes),
        mesh=fine,
        in_specs=(P(docs, None), P(cents, None), P(docs), P()),
        out_specs=(P(cents, None), P(docs)),
        check_vma=False,
    )
```

```python
import functools
import math

import jax
import jax.numpy as jnp
from jax import lax
from jax.experimental import pallas as pl
from jax.experimental.pallas import tpu as pltpu
from jax.sharding import Mesh
from jax.sharding import PartitionSpec as P

LOG2E = 1.4426950408889634
LN2 = 0.6931471805599453
LANES = 128
VMEM_LIMIT = 32 * 1024 * 1024
ROWS = ("x", "zl", "zh")
COLS = ("y", "core")
F32 = jnp.float32
BF16 = jnp.bfloat16


def call(kernel, out_shape, n_in, scratch=(), flops=0, out_specs=None, in_specs=None, alias=None):
    vmem = pl.BlockSpec(memory_space=pltpu.VMEM)
    if in_specs is None:
        in_specs = [vmem] * n_in
    if out_specs is None:
        out_specs = jax.tree.map(lambda _: vmem, out_shape)
    return pl.pallas_call(
        kernel,
        out_shape=out_shape,
        in_specs=in_specs,
        out_specs=out_specs,
        scratch_shapes=list(scratch),
        input_output_aliases=alias or {},
        compiler_params=pltpu.CompilerParams(vmem_limit_bytes=VMEM_LIMIT),
        cost_estimate=pl.CostEstimate(flops=flops, bytes_accessed=1 << 20, transcendentals=0),
    )


def lane_iota():
    return lax.broadcasted_iota(jnp.int32, (LANES, LANES), 1)


def to_columns(dense):
    return jnp.concatenate([dense] * (LANES // dense.shape[0]), axis=0).T


def nt_dot(a, b):
    return lax.dot_general(a, b, (((1,), (1,)), ((), ())), preferred_element_type=F32)


def weights_of(ids, mass_ref):
    def step(s, total):
        return jnp.where(ids == s, mass_ref[s].astype(F32), total)

    return lax.fori_loop(0, mass_ref.shape[0], step, jnp.zeros(ids.shape, F32), unroll=True) * 0.125


def first_rows(
    scale, mass_hbm, ids_hbm, docs_hbm, cents_hbm, out_ref, docs_ref, cents_ref, w_ref, mass_ref, ids_ref, sems
):
    n_doc, n_cent = docs_hbm.shape[0], cents_hbm.shape[0]
    block = 512
    copies = [
        pltpu.make_async_copy(src, dst, sems.at[k])
        for k, (src, dst) in enumerate(((mass_hbm, mass_ref), (ids_hbm, ids_ref), (docs_hbm, docs_ref), (cents_hbm, cents_ref)))
    ]
    for copy in copies:
        copy.start()
    copies[0].wait()
    copies[1].wait()
    w = weights_of(ids_ref[...], mass_ref)
    w_ref[...] = w
    copies[2].wait()
    copies[3].wait()
    groups = n_doc // 256
    tops = [jnp.full((8, 256), -jnp.inf, F32)] * groups
    totals = [jnp.zeros((8, 256), F32)] * groups
    for q in range(n_cent // block):
        cents = cents_ref[q * block : (q + 1) * block, :]
        for g in range(groups):
            s = nt_dot(cents, docs_ref[g * 256 : (g + 1) * 256, :]).reshape(block // 8, 8, 256)
            top = jnp.maximum(tops[g], jnp.max(s, axis=0) * scale)
            totals[g] = totals[g] * jnp.exp2(tops[g] - top) + jnp.sum(jnp.exp2(s * scale - top[None]), axis=0)
            tops[g] = top
    rows = []
    for g in range(groups):
        top = jnp.max(tops[g], axis=0, keepdims=True)
        lse = top + jnp.log2(jnp.sum(totals[g] * jnp.exp2(tops[g] - top), axis=0, keepdims=True))
        rows += [lse[:, 0:LANES], lse[:, LANES:256]]
    out_ref[...] = jnp.broadcast_to((jnp.concatenate(rows, axis=0) - jnp.log2(w))[None], out_ref.shape)


def first_columns(
    scale, n_x, parts_ref, docs_ref, other_ref, cents_ref,
    out_ref, tile_ref, top_ref, f_ref, docs_all_ref, half_ref,
):
    zl = lax.axis_index("zl")
    n_doc, n_cent = docs_ref.shape[0], cents_ref.shape[0] // 2
    groups = 2 * n_doc // LANES
    docs_all_ref[pl.ds(pl.multiple_of(zl * n_doc, n_doc), n_doc), :] = docs_ref[...]
    docs_all_ref[pl.ds(pl.multiple_of((1 - zl) * n_doc, n_doc), n_doc), :] = other_ref[...]
    run = n_cent // 2
    for q in range(2):
        rows = pl.ds(pl.multiple_of(q * n_cent + zl * run, run), run)
        half_ref[q * run : (q + 1) * run, :] = cents_ref[rows, :]
    by_zl = parts_ref[...].reshape(n_x, 2, parts_ref.shape[0] // (2 * n_x), 8, LANES)
    for z in range(2):
        parts = by_zl[:, z].reshape(parts_ref.shape[0] // 2, 8, LANES)
        top = jnp.max(parts, axis=0)
        f_ref[z * 8 : (z + 1) * 8, :] = -(top + jnp.log2(jnp.sum(jnp.exp2(parts - top[None]), axis=0)))

    for g in range(groups // 2):
        f = jnp.concatenate([f_ref[2 * g : 2 * g + 1, :], f_ref[2 * g + 1 : 2 * g + 2, :]], axis=1)
        docs = docs_all_ref[g * 256 : (g + 1) * 256, :]
        for q in range(n_cent // 256):
            cents = half_ref[q * 256 : (q + 1) * 256, :]
            tile_ref[q * 256 : (q + 1) * 256, g * 256 : (g + 1) * 256] = nt_dot(cents, docs) * scale + f
    lane = lane_iota()
    tops = jnp.zeros((LANES, LANES), F32)
    lses = jnp.zeros((LANES, LANES), F32)
    for r in range(n_cent // LANES):
        rows = slice(r * LANES, (r + 1) * LANES)
        top = tile_ref[rows, 0:LANES]
        for g in range(1, groups):
            top = jnp.maximum(top, tile_ref[rows, g * LANES : (g + 1) * LANES])
        top = jnp.broadcast_to(jnp.max(top, axis=1, keepdims=True), (LANES, LANES))
        total = jnp.zeros((LANES, LANES), F32)
        for g in range(groups):
            e = jnp.exp2(tile_ref[rows, g * LANES : (g + 1) * LANES] - top)
            tile_ref[rows, g * LANES : (g + 1) * LANES] = e
            total = total + e
        tops = jnp.where(lane == r, top, tops)
        lses = jnp.where(lane == r, top + jnp.log2(jnp.sum(total, axis=1, keepdims=True)), lses)
    top_ref[...] = tops.T[0:8, :]
    out_ref[...] = jnp.broadcast_to(lses.T[0:8, :][None], out_ref.shape)


def weigh_columns(c, tile_ref, out_ref):
    groups = tile_ref.shape[1] // LANES
    totals = [jnp.zeros((8, LANES), F32) for _ in range(groups)]
    for r in range(tile_ref.shape[0] // LANES):
        col = jnp.broadcast_to(c[r : r + 1, :], (LANES, LANES)).T
        for g in range(groups):
            p = tile_ref[r * LANES : (r + 1) * LANES, g * LANES : (g + 1) * LANES] * col
            totals[g] = totals[g] + jnp.sum(p.reshape(LANES // 8, 8, LANES), axis=0)
    rows = jnp.concatenate([jnp.sum(t, axis=0, keepdims=True) for t in totals], axis=0)
    out_ref[:, 0:groups, :] = jnp.broadcast_to(rows[None], (out_ref.shape[0], groups, LANES)).astype(out_ref.dtype)


def rows_after_first(log_target, parts_ref, top_ref, w_ref, tile_ref, out_ref, c_ref):
    parts = parts_ref[...]
    top = jnp.max(parts, axis=0)
    lse = top + jnp.log2(jnp.sum(jnp.exp2(parts - top[None]), axis=0))
    c = jnp.exp2(top_ref[...] + (log_target - lse))
    c_ref[...] = c
    weigh_columns(c, tile_ref, out_ref)
    w = w_ref[...]
    groups = out_ref.shape[1] - w.shape[0]
    out_ref[:, groups:, :] = jnp.broadcast_to(w[None], (out_ref.shape[0], *w.shape)).astype(out_ref.dtype)


def rows_after(target, parts_ref, last_ref, tile_ref, out_ref, c_ref):
    c = last_ref[...] * (target / jnp.sum(parts_ref[...].astype(F32), axis=0))
    c_ref[...] = c
    weigh_columns(c, tile_ref, out_ref)


def columns_after_first(n_zh, parts_ref, c_ref, tile_ref, out_ref, w_ref):
    groups = w_ref.shape[0]
    w = jnp.concatenate([parts_ref[z * n_zh, groups:, :].astype(F32) for z in range(2)], axis=0)
    w_ref[...] = w
    weigh_rows(w / jnp.sum(parts_ref[:, 0:groups, :].astype(F32), axis=0), c_ref, tile_ref, out_ref)


def columns_after(parts_ref, w_ref, c_ref, tile_ref, out_ref):
    weigh_rows(w_ref[...] / jnp.sum(parts_ref[...].astype(F32), axis=0), c_ref, tile_ref, out_ref)


def weigh_rows(u, c_ref, tile_ref, out_ref):
    groups = tile_ref.shape[1] // LANES
    lane = lane_iota()
    sums = jnp.zeros((LANES, LANES), F32)
    for r in range(tile_ref.shape[0] // LANES):
        total = jnp.zeros((LANES, LANES), F32)
        for g in range(groups):
            total = total + tile_ref[r * LANES : (r + 1) * LANES, g * LANES : (g + 1) * LANES] * u[g : g + 1, :]
        sums = jnp.where(lane == r, jnp.sum(total, axis=1, keepdims=True), sums)
    out = sums.T[0:8, :] * c_ref[...]
    out_ref[...] = jnp.broadcast_to(out[None], out_ref.shape).astype(out_ref.dtype)


def half_sums(side, u, c_ref, tile_ref, docs_ref, out_ref, p_ref):
    n_half, n_doc = p_ref.shape
    groups = n_doc // LANES
    blocks = n_half // LANES
    cols = to_columns(c_ref[pl.ds(side * blocks, blocks), :])
    base = pl.multiple_of(side * n_half, n_half)
    lane = lane_iota()
    masses = jnp.zeros((LANES, LANES), F32)
    for r in range(blocks):
        rows = pl.ds(pl.multiple_of(base + r * LANES, LANES), LANES)
        col = jnp.broadcast_to(cols[:, r : r + 1], (LANES, LANES))
        total = jnp.zeros((LANES, LANES), F32)
        for g in range(groups):
            lanes = slice(g * LANES, (g + 1) * LANES)
            p = tile_ref[rows, lanes] * u[g : g + 1, :] * col
            total = total + p
            p_ref[r * LANES : (r + 1) * LANES, lanes] = p.astype(BF16)
        masses = jnp.where(lane == r, jnp.sum(total, axis=1, keepdims=True), masses)
    mass = masses.T[0:8, :]
    out_ref[n_half : n_half + 8, :] = jnp.concatenate([mass, mass], axis=1)
    for b in range(n_half // 256):
        rows = slice(b * 256, (b + 1) * 256)
        out_ref[rows, :] = jnp.dot(p_ref[rows, :], docs_ref[...], preferred_element_type=F32)


def final_other(parts_ref, w_ref, f_ref, c_ref, tile_ref, docs_ref, out_ref, pot_ref, u_ref, p_ref):
    u = w_ref[...] / jnp.sum(parts_ref[...].astype(F32), axis=0)
    u_ref[...] = u
    pot = (f_ref[...] + jnp.log2(u)) * LN2
    pot_ref[...] = jnp.where(lax.axis_index("zl") == 0, pot[0:8, :], pot[8:16, :])
    half_sums(1 - lax.axis_index("core"), u, c_ref, tile_ref, docs_ref, out_ref, p_ref)


def final_own(u_ref, c_ref, tile_ref, docs_ref, out_ref, p_ref):
    half_sums(lax.axis_index("core"), u_ref[...], c_ref, tile_ref, docs_ref, out_ref, p_ref)


def final_join(own_ref, other_ref, out_ref):
    peers = out_ref.shape[0]
    n_half = own_ref.shape[0] - 8
    chunk = n_half // peers
    mass = own_ref[n_half:, 0:LANES] + other_ref[n_half:, 0:LANES]
    high = mass.astype(BF16).astype(F32)
    low = mass - high
    for q in range(peers):
        for i in range(chunk // 16):
            rows = slice(q * chunk + i * 16, q * chunk + (i + 1) * 16)
            out_ref[q, :, i * 256 : (i + 1) * 256] = (own_ref[rows, :] + other_ref[rows, :]).astype(BF16)
        r = q * chunk // LANES
        pair = [jnp.broadcast_to(x[r : r + 1, :], (8, LANES)) for x in (high, low)]
        out_ref[q, :, 256 * (chunk // 16) :] = jnp.concatenate(pair, axis=0).astype(BF16)


def divide(parts_ref, out_ref, mass_ref):
    total = parts_ref[0].astype(F32)
    for p in range(1, parts_ref.shape[0]):
        total = total + parts_ref[p].astype(F32)
    tiles = total.shape[1] // LANES - 1
    chunk = tiles * 8
    mass = total[0:8, tiles * LANES :] + total[8:16, tiles * LANES :]
    mass_ref[...] = to_columns(mass)
    col = mass_ref[pl.ds(pl.multiple_of((lax.axis_index("y") & 1) * chunk, chunk), chunk), :]
    for i in range(chunk // 16):
        pair = [total[:, (i * 2 + h) * LANES : (i * 2 + h + 1) * LANES] / col[i * 16 : (i + 1) * 16, :] for h in range(2)]
        new = jnp.concatenate(pair, axis=1).astype(BF16)
        out_ref[:, i * 16 : (i + 1) * 16, :] = jnp.broadcast_to(new[None], (out_ref.shape[0], 16, 256))


def place_own(x_ref, pot_ref, out_ref, pot_out_ref, sems):
    rows = x_ref.shape[0]
    place = pl.ds(pl.multiple_of(lax.axis_index("core") * rows, rows), rows)
    copies = [pltpu.make_async_copy(x_ref, out_ref.at[place, :], sems.at[0]), pltpu.make_async_copy(pot_ref, pot_out_ref, sems.at[1])]
    for copy in copies:
        copy.start()
    for copy in copies:
        copy.wait()


def place_other(x_ref, _, out_ref, sem):
    rows = x_ref.shape[0]
    copy = pltpu.make_async_copy(x_ref, out_ref.at[pl.ds(pl.multiple_of((1 - lax.axis_index("core")) * rows, rows), rows), :], sem)
    copy.start()
    copy.wait()


def exchange(x, axes):
    return lax.all_to_all(x, axes, 0, 0)


def per_device(sizes, docs, cents, shard_ids, shard_mass):
    n_y, n_zl, n_core, n_zh, n_x = sizes
    row_peers, col_peers = n_zl * n_zh * n_x, n_y * n_core
    n_doc, n_cent = docs.shape[0] * 2, cents.shape[0] // 2
    doc_rows, cent_rows = n_doc // LANES, n_cent // LANES
    scale = 4.0 * docs.shape[1] ** -0.5 * LOG2E
    target = 0.5 * (docs.shape[0] * n_y * n_zl * n_core) / (cents.shape[0] * n_zh * n_x)
    swap = [(0, 1), (1, 0)]
    shape = jax.ShapeDtypeStruct
    tile_shape = pltpu.VMEM((n_cent, n_doc), F32)
    small = shape((cent_rows, LANES), F32)

    any_space = pl.BlockSpec(memory_space=pl.ANY)
    hbm = pl.BlockSpec(memory_space=pltpu.HBM)
    other_docs = lax.ppermute(docs, "zl", swap)
    parts, docs, cents, own_w = call(
        functools.partial(first_rows, scale),
        (
            shape((row_peers, doc_rows // 2, LANES), F32),
            pltpu.VMEM(docs.shape, BF16),
            pltpu.VMEM(cents.shape, BF16),
            shape((doc_rows // 2, LANES), F32),
        ),
        4,
        in_specs=[hbm] * 4,
        scratch=[pltpu.SMEM(shard_mass.shape, jnp.int32), pltpu.VMEM((doc_rows // 2, LANES), jnp.int32), pltpu.SemaphoreType.DMA((4,))],
        flops=2 * docs.shape[0] * cents.shape[0] * 256,
    )(*[pltpu.with_memory_space_constraint(x, pltpu.HBM) for x in (shard_mass, shard_ids.reshape(-1, LANES), docs, cents)])
    parts = exchange(parts, ROWS)
    chunk = n_cent // col_peers
    parts, tile, top, f, docs_all = call(
        functools.partial(first_columns, scale, n_x),
        (
            shape((col_peers, cent_rows, LANES), F32),
            tile_shape,
            small,
            shape((doc_rows, LANES), F32),
            pltpu.VMEM((n_doc, 256), BF16),
        ),
        4,
        scratch=[pltpu.VMEM((n_cent, 256), BF16)],
        flops=2 * n_doc * n_cent * 256,
    )(parts, docs, other_docs, cents)

    rows_out = (shape((row_peers, doc_rows, LANES), BF16), small)
    parts = exchange(parts, COLS)
    log_target = math.log2(target)
    first_out = (shape((row_peers, doc_rows + doc_rows // 2, LANES), BF16), small)
    parts, c = call(functools.partial(rows_after_first, log_target), first_out, 4, flops=2 * n_doc * n_cent)(parts, top, own_w, tile)
    col_out = shape((col_peers, cent_rows, LANES), BF16)
    for turn in range(2):
        parts = exchange(parts, ROWS)
        if turn == 0:
            out = (col_out, shape((doc_rows, LANES), F32))
            parts, w = call(functools.partial(columns_after_first, n_zh), out, 3, flops=2 * n_doc * n_cent)(parts, c, tile)
        else:
            parts = call(columns_after, col_out, 4, flops=2 * n_doc * n_cent)(parts, w, c, tile)
        parts = exchange(parts, COLS)
        parts, c = call(functools.partial(rows_after, target), rows_out, 3, flops=2 * n_doc * n_cent)(parts, c, tile)
    parts = exchange(parts, ROWS)
    n_half = n_cent // n_core
    half_flops = 2 * n_doc * n_half * 256
    part_shape = pltpu.VMEM((n_half + 8, 256), F32)
    p_scratch = [pltpu.VMEM((n_half, n_doc), BF16)]
    for_other, pot, u = call(
        final_other,
        (part_shape, pltpu.VMEM((doc_rows // 2, LANES), F32), shape((doc_rows, LANES), F32)),
        6,
        scratch=p_scratch,
        flops=half_flops,
    )(parts, w, f, c, tile, docs_all)
    from_other = lax.ppermute(for_other, "core", swap)
    for_own = call(final_own, part_shape, 4, scratch=p_scratch, flops=half_flops)(u, c, tile, docs_all)
    sums = call(final_join, shape((n_y, 16, 2 * LANES * (chunk // 16) + LANES), BF16), 2)(for_own, from_other)
    sums = exchange(sums, "y")
    new = call(divide, shape((n_y * n_zl, chunk, 256), BF16), 1, scratch=[pltpu.VMEM((LANES, LANES), F32)])(sums)
    own = exchange(new, ("zl", "y")).reshape(n_y * n_zl * chunk, 256)
    other = lax.ppermute(own, "core", swap)
    placed = shape((cents.shape[0], 256), BF16)
    new, pot = call(
        place_own,
        (placed, shape((doc_rows // 2, LANES), F32)),
        2,
        in_specs=[any_space, pl.BlockSpec(memory_space=pltpu.VMEM)],
        out_specs=(any_space, any_space),
        scratch=[pltpu.SemaphoreType.DMA((2,))],
    )(own, pot)
    new = call(
        place_other, placed, 2, in_specs=[any_space, any_space], out_specs=any_space, scratch=[pltpu.SemaphoreType.DMA], alias={1: 0}
    )(other, new)
    return new, pot.reshape(-1)


SIZES = (8, 2, 2, 4, 4)


def solution(mesh, sizes=SIZES):
    fine = Mesh(mesh.devices.reshape(sizes), ("y", "zl", "core", "zh", "x"))
    docs, cents = ("y", "zl", "core"), ("zh", "x")
    return jax.shard_map(
        functools.partial(per_device, sizes),
        mesh=fine,
        in_specs=(P(docs, None), P(cents, None), P(docs), P()),
        out_specs=(P(cents, None), P(docs)),
        check_vma=False,
    )
```

```python
import functools
import math

import jax
import jax.numpy as jnp
from jax import lax
from jax.experimental import pallas as pl
from jax.experimental.pallas import tpu as pltpu
from jax.sharding import Mesh
from jax.sharding import PartitionSpec as P

LOG2E = 1.4426950408889634
LN2 = 0.6931471805599453
LANES = 128
VMEM_LIMIT = 32 * 1024 * 1024
ROWS = ("x", "zl", "zh")
COLS = ("yc", "yb", "ya", "core")
SUMS = ("yb", "ya", "yc")
F32 = jnp.float32
BF16 = jnp.bfloat16


def call(kernel, out_shape, n_in, scratch=(), flops=0, out_specs=None, in_specs=None, alias=None):
    vmem = pl.BlockSpec(memory_space=pltpu.VMEM)
    if in_specs is None:
        in_specs = [vmem] * n_in
    if out_specs is None:
        out_specs = jax.tree.map(lambda _: vmem, out_shape)
    return pl.pallas_call(
        kernel,
        out_shape=out_shape,
        in_specs=in_specs,
        out_specs=out_specs,
        scratch_shapes=list(scratch),
        input_output_aliases=alias or {},
        compiler_params=pltpu.CompilerParams(vmem_limit_bytes=VMEM_LIMIT),
        cost_estimate=pl.CostEstimate(flops=flops, bytes_accessed=1 << 20, transcendentals=0),
    )


def lane_iota():
    return lax.broadcasted_iota(jnp.int32, (LANES, LANES), 1)


def to_columns(dense):
    return jnp.concatenate([dense] * (LANES // dense.shape[0]), axis=0).T


def nt_dot(a, b):
    return lax.dot_general(a, b, (((1,), (1,)), ((), ())), preferred_element_type=F32)


def weights_of(ids, mass_ref):
    def step(s, total):
        return jnp.where(ids == s, mass_ref[s].astype(F32), total)

    return lax.fori_loop(0, mass_ref.shape[0], step, jnp.zeros(ids.shape, F32), unroll=True) * 0.125


def first_rows(
    scale, mass_hbm, ids_hbm, docs_hbm, cents_hbm, out_ref, docs_ref, cents_ref, w_ref, mass_ref, ids_ref, sems
):
    n_doc, n_cent = docs_hbm.shape[0], cents_hbm.shape[0]
    block = 512
    copies = [
        pltpu.make_async_copy(src, dst, sems.at[k])
        for k, (src, dst) in enumerate(((mass_hbm, mass_ref), (ids_hbm, ids_ref), (docs_hbm, docs_ref), (cents_hbm, cents_ref)))
    ]
    for copy in copies:
        copy.start()
    copies[0].wait()
    copies[1].wait()
    w = weights_of(ids_ref[...], mass_ref)
    w_ref[...] = w
    copies[2].wait()
    copies[3].wait()
    groups = n_doc // 256
    tops = [jnp.full((8, 256), -jnp.inf, F32)] * groups
    totals = [jnp.zeros((8, 256), F32)] * groups
    for q in range(n_cent // block):
        cents = cents_ref[q * block : (q + 1) * block, :]
        for g in range(groups):
            s = nt_dot(cents, docs_ref[g * 256 : (g + 1) * 256, :]).reshape(block // 8, 8, 256)
            top = jnp.maximum(tops[g], jnp.max(s, axis=0) * scale)
            totals[g] = totals[g] * jnp.exp2(tops[g] - top) + jnp.sum(jnp.exp2(s * scale - top[None]), axis=0)
            tops[g] = top
    rows = []
    for g in range(groups):
        top = jnp.max(tops[g], axis=0, keepdims=True)
        lse = top + jnp.log2(jnp.sum(totals[g] * jnp.exp2(tops[g] - top), axis=0, keepdims=True))
        rows += [lse[:, 0:LANES], lse[:, LANES:256]]
    out_ref[...] = jnp.broadcast_to((jnp.concatenate(rows, axis=0) - jnp.log2(w))[None], out_ref.shape)


def first_columns(
    scale, n_x, parts_ref, docs_ref, other_ref, cents_ref,
    out_ref, tile_ref, top_ref, f_ref, docs_all_ref, half_ref,
):
    zl = lax.axis_index("zl")
    n_doc, n_cent = docs_ref.shape[0], cents_ref.shape[0] // 2
    groups = 2 * n_doc // LANES
    docs_all_ref[pl.ds(pl.multiple_of(zl * n_doc, n_doc), n_doc), :] = docs_ref[...]
    docs_all_ref[pl.ds(pl.multiple_of((1 - zl) * n_doc, n_doc), n_doc), :] = other_ref[...]
    run = n_cent // 2
    for q in range(2):
        rows = pl.ds(pl.multiple_of(q * n_cent + zl * run, run), run)
        half_ref[q * run : (q + 1) * run, :] = cents_ref[rows, :]
    by_zl = parts_ref[...].reshape(n_x, 2, parts_ref.shape[0] // (2 * n_x), 8, LANES)
    for z in range(2):
        parts = by_zl[:, z].reshape(parts_ref.shape[0] // 2, 8, LANES)
        top = jnp.max(parts, axis=0)
        f_ref[z * 8 : (z + 1) * 8, :] = -(top + jnp.log2(jnp.sum(jnp.exp2(parts - top[None]), axis=0)))

    for g in range(groups // 2):
        f = jnp.concatenate([f_ref[2 * g : 2 * g + 1, :], f_ref[2 * g + 1 : 2 * g + 2, :]], axis=1)
        docs = docs_all_ref[g * 256 : (g + 1) * 256, :]
        for q in range(n_cent // 256):
            cents = half_ref[q * 256 : (q + 1) * 256, :]
            tile_ref[q * 256 : (q + 1) * 256, g * 256 : (g + 1) * 256] = nt_dot(cents, docs) * scale + f
    lane = lane_iota()
    tops = jnp.zeros((LANES, LANES), F32)
    lses = jnp.zeros((LANES, LANES), F32)
    for r in range(n_cent // LANES):
        rows = slice(r * LANES, (r + 1) * LANES)
        top = tile_ref[rows, 0:LANES]
        for g in range(1, groups):
            top = jnp.maximum(top, tile_ref[rows, g * LANES : (g + 1) * LANES])
        top = jnp.broadcast_to(jnp.max(top, axis=1, keepdims=True), (LANES, LANES))
        total = jnp.zeros((LANES, LANES), F32)
        for g in range(groups):
            e = jnp.exp2(tile_ref[rows, g * LANES : (g + 1) * LANES] - top)
            tile_ref[rows, g * LANES : (g + 1) * LANES] = e
            total = total + e
        tops = jnp.where(lane == r, top, tops)
        lses = jnp.where(lane == r, top + jnp.log2(jnp.sum(total, axis=1, keepdims=True)), lses)
    top_ref[...] = tops.T[0:8, :]
    out_ref[...] = jnp.broadcast_to(lses.T[0:8, :][None], out_ref.shape)


def weigh_columns(c, tile_ref, out_ref):
    groups = tile_ref.shape[1] // LANES
    totals = [jnp.zeros((8, LANES), F32) for _ in range(groups)]
    for r in range(tile_ref.shape[0] // LANES):
        col = jnp.broadcast_to(c[r : r + 1, :], (LANES, LANES)).T
        for g in range(groups):
            p = tile_ref[r * LANES : (r + 1) * LANES, g * LANES : (g + 1) * LANES] * col
            totals[g] = totals[g] + jnp.sum(p.reshape(LANES // 8, 8, LANES), axis=0)
    rows = jnp.concatenate([jnp.sum(t, axis=0, keepdims=True) for t in totals], axis=0)
    out_ref[:, 0:groups, :] = jnp.broadcast_to(rows[None], (out_ref.shape[0], groups, LANES)).astype(out_ref.dtype)


def rows_after_first(log_target, parts_ref, top_ref, w_ref, tile_ref, out_ref, c_ref):
    parts = parts_ref[...]
    top = jnp.max(parts, axis=0)
    lse = top + jnp.log2(jnp.sum(jnp.exp2(parts - top[None]), axis=0))
    c = jnp.exp2(top_ref[...] + (log_target - lse))
    c_ref[...] = c
    weigh_columns(c, tile_ref, out_ref)
    w = w_ref[...]
    groups = out_ref.shape[1] - w.shape[0]
    out_ref[:, groups:, :] = jnp.broadcast_to(w[None], (out_ref.shape[0], *w.shape)).astype(out_ref.dtype)


def rows_after(target, parts_ref, last_ref, tile_ref, out_ref, c_ref):
    c = last_ref[...] * (target / jnp.sum(parts_ref[...].astype(F32), axis=0))
    c_ref[...] = c
    weigh_columns(c, tile_ref, out_ref)


def columns_after_first(n_zh, parts_ref, c_ref, tile_ref, out_ref, w_ref):
    groups = w_ref.shape[0]
    w = jnp.concatenate([parts_ref[z * n_zh, groups:, :].astype(F32) for z in range(2)], axis=0)
    w_ref[...] = w
    weigh_rows(w / jnp.sum(parts_ref[:, 0:groups, :].astype(F32), axis=0), c_ref, tile_ref, out_ref)


def columns_after(parts_ref, w_ref, c_ref, tile_ref, out_ref):
    weigh_rows(w_ref[...] / jnp.sum(parts_ref[...].astype(F32), axis=0), c_ref, tile_ref, out_ref)


def weigh_rows(u, c_ref, tile_ref, out_ref):
    groups = tile_ref.shape[1] // LANES
    lane = lane_iota()
    sums = jnp.zeros((LANES, LANES), F32)
    for r in range(tile_ref.shape[0] // LANES):
        total = jnp.zeros((LANES, LANES), F32)
        for g in range(groups):
            total = total + tile_ref[r * LANES : (r + 1) * LANES, g * LANES : (g + 1) * LANES] * u[g : g + 1, :]
        sums = jnp.where(lane == r, jnp.sum(total, axis=1, keepdims=True), sums)
    out = sums.T[0:8, :] * c_ref[...]
    out_ref[...] = jnp.broadcast_to(out[None], out_ref.shape).astype(out_ref.dtype)


def half_sums(side, u, c_ref, tile_ref, docs_ref, out_ref, p_ref):
    n_half, n_doc = p_ref.shape
    groups = n_doc // LANES
    blocks = n_half // LANES
    cols = to_columns(c_ref[pl.ds(side * blocks, blocks), :])
    base = pl.multiple_of(side * n_half, n_half)
    lane = lane_iota()
    masses = jnp.zeros((LANES, LANES), F32)
    for r in range(blocks):
        rows = pl.ds(pl.multiple_of(base + r * LANES, LANES), LANES)
        col = jnp.broadcast_to(cols[:, r : r + 1], (LANES, LANES))
        total = jnp.zeros((LANES, LANES), F32)
        for g in range(groups):
            lanes = slice(g * LANES, (g + 1) * LANES)
            p = tile_ref[rows, lanes] * u[g : g + 1, :] * col
            total = total + p
            p_ref[r * LANES : (r + 1) * LANES, lanes] = p.astype(BF16)
        masses = jnp.where(lane == r, jnp.sum(total, axis=1, keepdims=True), masses)
    mass = masses.T[0:8, :]
    out_ref[n_half : n_half + 8, :] = jnp.concatenate([mass, mass], axis=1)
    for b in range(n_half // 256):
        rows = slice(b * 256, (b + 1) * 256)
        out_ref[rows, :] = jnp.dot(p_ref[rows, :], docs_ref[...], preferred_element_type=F32)


def final_other(parts_ref, w_ref, f_ref, c_ref, tile_ref, docs_ref, out_ref, pot_ref, u_ref, p_ref):
    u = w_ref[...] / jnp.sum(parts_ref[...].astype(F32), axis=0)
    u_ref[...] = u
    pot = (f_ref[...] + jnp.log2(u)) * LN2
    pot_ref[...] = jnp.where(lax.axis_index("zl") == 0, pot[0:8, :], pot[8:16, :])
    half_sums(1 - lax.axis_index("core"), u, c_ref, tile_ref, docs_ref, out_ref, p_ref)


def final_own(u_ref, c_ref, tile_ref, docs_ref, out_ref, p_ref):
    half_sums(lax.axis_index("core"), u_ref[...], c_ref, tile_ref, docs_ref, out_ref, p_ref)


def final_join(own_ref, other_ref, out_ref):
    peers = out_ref.shape[0]
    n_half = own_ref.shape[0] - 8
    chunk = n_half // peers
    mass = own_ref[n_half:, 0:LANES] + other_ref[n_half:, 0:LANES]
    high = mass.astype(BF16).astype(F32)
    low = mass - high
    for q in range(peers):
        for i in range(chunk // 16):
            rows = slice(q * chunk + i * 16, q * chunk + (i + 1) * 16)
            out_ref[q, :, i * 256 : (i + 1) * 256] = (own_ref[rows, :] + other_ref[rows, :]).astype(BF16)
        r = q * chunk // LANES
        pair = [jnp.broadcast_to(x[r : r + 1, :], (8, LANES)) for x in (high, low)]
        out_ref[q, :, 256 * (chunk // 16) :] = jnp.concatenate(pair, axis=0).astype(BF16)


def divide(parts_ref, out_ref, mass_ref):
    total = parts_ref[0].astype(F32)
    for p in range(1, parts_ref.shape[0]):
        total = total + parts_ref[p].astype(F32)
    tiles = total.shape[1] // LANES - 1
    chunk = tiles * 8
    mass = total[0:8, tiles * LANES :] + total[8:16, tiles * LANES :]
    mass_ref[...] = to_columns(mass)
    col = mass_ref[pl.ds(pl.multiple_of((lax.axis_index("yc")) * chunk, chunk), chunk), :]
    for i in range(chunk // 16):
        pair = [total[:, (i * 2 + h) * LANES : (i * 2 + h + 1) * LANES] / col[i * 16 : (i + 1) * 16, :] for h in range(2)]
        new = jnp.concatenate(pair, axis=1).astype(BF16)
        out_ref[:, i * 16 : (i + 1) * 16, :] = jnp.broadcast_to(new[None], (out_ref.shape[0], 16, 256))


def place_own(x_ref, pot_ref, out_ref, pot_out_ref, sems):
    rows = x_ref.shape[0]
    place = pl.ds(pl.multiple_of(lax.axis_index("core") * rows, rows), rows)
    copies = [pltpu.make_async_copy(x_ref, out_ref.at[place, :], sems.at[0]), pltpu.make_async_copy(pot_ref, pot_out_ref, sems.at[1])]
    for copy in copies:
        copy.start()
    for copy in copies:
        copy.wait()


def place_other(x_ref, _, out_ref, sem):
    rows = x_ref.shape[0]
    copy = pltpu.make_async_copy(x_ref, out_ref.at[pl.ds(pl.multiple_of((1 - lax.axis_index("core")) * rows, rows), rows), :], sem)
    copy.start()
    copy.wait()


def exchange(x, axes):
    return lax.all_to_all(x, axes, 0, 0)


def per_device(sizes, docs, cents, shard_ids, shard_mass):
    *y_bits, n_zl, n_core, n_zh, n_x = sizes
    n_y = math.prod(y_bits)
    row_peers, col_peers = n_zl * n_zh * n_x, n_y * n_core
    n_doc, n_cent = docs.shape[0] * 2, cents.shape[0] // 2
    doc_rows, cent_rows = n_doc // LANES, n_cent // LANES
    scale = 4.0 * docs.shape[1] ** -0.5 * LOG2E
    target = 0.5 * (docs.shape[0] * n_y * n_zl * n_core) / (cents.shape[0] * n_zh * n_x)
    swap = [(0, 1), (1, 0)]
    shape = jax.ShapeDtypeStruct
    tile_shape = pltpu.VMEM((n_cent, n_doc), F32)
    small = shape((cent_rows, LANES), F32)

    any_space = pl.BlockSpec(memory_space=pl.ANY)
    hbm = pl.BlockSpec(memory_space=pltpu.HBM)
    other_docs = lax.ppermute(docs, "zl", swap)
    parts, docs, cents, own_w = call(
        functools.partial(first_rows, scale),
        (
            shape((row_peers, doc_rows // 2, LANES), F32),
            pltpu.VMEM(docs.shape, BF16),
            pltpu.VMEM(cents.shape, BF16),
            shape((doc_rows // 2, LANES), F32),
        ),
        4,
        in_specs=[hbm] * 4,
        scratch=[pltpu.SMEM(shard_mass.shape, jnp.int32), pltpu.VMEM((doc_rows // 2, LANES), jnp.int32), pltpu.SemaphoreType.DMA((4,))],
        flops=2 * docs.shape[0] * cents.shape[0] * 256,
    )(*[pltpu.with_memory_space_constraint(x, pltpu.HBM) for x in (shard_mass, shard_ids.reshape(-1, LANES), docs, cents)])
    parts = exchange(parts, ROWS)
    chunk = n_cent // col_peers
    parts, tile, top, f, docs_all = call(
        functools.partial(first_columns, scale, n_x),
        (
            shape((col_peers, cent_rows, LANES), F32),
            tile_shape,
            small,
            shape((doc_rows, LANES), F32),
            pltpu.VMEM((n_doc, 256), BF16),
        ),
        4,
        scratch=[pltpu.VMEM((n_cent, 256), BF16)],
        flops=2 * n_doc * n_cent * 256,
    )(parts, docs, other_docs, cents)

    rows_out = (shape((row_peers, doc_rows, LANES), BF16), small)
    parts = exchange(parts, COLS)
    log_target = math.log2(target)
    first_out = (shape((row_peers, doc_rows + doc_rows // 2, LANES), BF16), small)
    parts, c = call(functools.partial(rows_after_first, log_target), first_out, 4, flops=2 * n_doc * n_cent)(parts, top, own_w, tile)
    col_out = shape((col_peers, cent_rows, LANES), BF16)
    for turn in range(2):
        parts = exchange(parts, ROWS)
        if turn == 0:
            out = (col_out, shape((doc_rows, LANES), F32))
            parts, w = call(functools.partial(columns_after_first, n_zh), out, 3, flops=2 * n_doc * n_cent)(parts, c, tile)
        else:
            parts = call(columns_after, col_out, 4, flops=2 * n_doc * n_cent)(parts, w, c, tile)
        parts = exchange(parts, COLS)
        parts, c = call(functools.partial(rows_after, target), rows_out, 3, flops=2 * n_doc * n_cent)(parts, c, tile)
    parts = exchange(parts, ROWS)
    n_half = n_cent // n_core
    half_flops = 2 * n_doc * n_half * 256
    part_shape = pltpu.VMEM((n_half + 8, 256), F32)
    p_scratch = [pltpu.VMEM((n_half, n_doc), BF16)]
    for_other, pot, u = call(
        final_other,
        (part_shape, pltpu.VMEM((doc_rows // 2, LANES), F32), shape((doc_rows, LANES), F32)),
        6,
        scratch=p_scratch,
        flops=half_flops,
    )(parts, w, f, c, tile, docs_all)
    from_other = lax.ppermute(for_other, "core", swap)
    for_own = call(final_own, part_shape, 4, scratch=p_scratch, flops=half_flops)(u, c, tile, docs_all)
    sums = call(final_join, shape((n_y, 16, 2 * LANES * (chunk // 16) + LANES), BF16), 2)(for_own, from_other)
    sums = exchange(sums, SUMS)
    new = call(divide, shape((n_y * n_zl, chunk, 256), BF16), 1, scratch=[pltpu.VMEM((LANES, LANES), F32)])(sums)
    own = exchange(new, ("zl", *SUMS)).reshape(n_y * n_zl * chunk, 256)
    other = lax.ppermute(own, "core", swap)
    placed = shape((cents.shape[0], 256), BF16)
    new, pot = call(
        place_own,
        (placed, shape((doc_rows // 2, LANES), F32)),
        2,
        in_specs=[any_space, pl.BlockSpec(memory_space=pltpu.VMEM)],
        out_specs=(any_space, any_space),
        scratch=[pltpu.SemaphoreType.DMA((2,))],
    )(own, pot)
    new = call(
        place_other, placed, 2, in_specs=[any_space, any_space], out_specs=any_space, scratch=[pltpu.SemaphoreType.DMA], alias={1: 0}
    )(other, new)
    return new, pot.reshape(-1)


SIZES = (2, 2, 2, 2, 2, 4, 4)


def solution(mesh, sizes=SIZES):
    fine = Mesh(mesh.devices.reshape(sizes), ("ya", "yb", "yc", "zl", "core", "zh", "x"))
    docs, cents = ("ya", "yb", "yc", "zl", "core"), ("zh", "x")
    return jax.shard_map(
        functools.partial(per_device, sizes),
        mesh=fine,
        in_specs=(P(docs, None), P(cents, None), P(docs), P()),
        out_specs=(P(cents, None), P(docs)),
        check_vma=False,
    )
```

```python
import functools
import math

import jax
import jax.numpy as jnp
from jax import lax
from jax.experimental import pallas as pl
from jax.experimental.pallas import tpu as pltpu
from jax.sharding import Mesh
from jax.sharding import PartitionSpec as P

LOG2E = 1.4426950408889634
LN2 = 0.6931471805599453
LANES = 128
VMEM_LIMIT = 32 * 1024 * 1024
ROWS = ("zb", "za", "zl", "xb", "xa")
COLS = ("yc", "yb", "ya", "core")
SUMS = ("yb", "ya", "yc")
F32 = jnp.float32
BF16 = jnp.bfloat16


def call(kernel, out_shape, n_in, scratch=(), flops=0, out_specs=None, in_specs=None, alias=None):
    vmem = pl.BlockSpec(memory_space=pltpu.VMEM)
    if in_specs is None:
        in_specs = [vmem] * n_in
    if out_specs is None:
        out_specs = jax.tree.map(lambda _: vmem, out_shape)
    return pl.pallas_call(
        kernel,
        out_shape=out_shape,
        in_specs=in_specs,
        out_specs=out_specs,
        scratch_shapes=list(scratch),
        input_output_aliases=alias or {},
        compiler_params=pltpu.CompilerParams(vmem_limit_bytes=VMEM_LIMIT),
        cost_estimate=pl.CostEstimate(flops=flops, bytes_accessed=1 << 20, transcendentals=0),
    )


def lane_iota():
    return lax.broadcasted_iota(jnp.int32, (LANES, LANES), 1)


def to_columns(dense):
    return jnp.concatenate([dense] * (LANES // dense.shape[0]), axis=0).T


def nt_dot(a, b):
    return lax.dot_general(a, b, (((1,), (1,)), ((), ())), preferred_element_type=F32)


def weights_of(ids, mass_ref):
    def step(s, total):
        return jnp.where(ids == s, mass_ref[s].astype(F32), total)

    return lax.fori_loop(0, mass_ref.shape[0], step, jnp.zeros(ids.shape, F32), unroll=True) * 0.125


def first_rows(
    scale, mass_hbm, ids_hbm, docs_hbm, cents_hbm, out_ref, docs_ref, cents_ref, w_ref, mass_ref, ids_ref, sems
):
    n_doc, n_cent = docs_hbm.shape[0], cents_hbm.shape[0]
    block = 512
    copies = [
        pltpu.make_async_copy(src, dst, sems.at[k])
        for k, (src, dst) in enumerate(((mass_hbm, mass_ref), (ids_hbm, ids_ref), (docs_hbm, docs_ref), (cents_hbm, cents_ref)))
    ]
    for copy in copies:
        copy.start()
    copies[0].wait()
    copies[1].wait()
    w = weights_of(ids_ref[...], mass_ref)
    w_ref[...] = w
    copies[2].wait()
    copies[3].wait()
    groups = n_doc // 256
    tops = [jnp.full((8, 256), -jnp.inf, F32)] * groups
    totals = [jnp.zeros((8, 256), F32)] * groups
    for q in range(n_cent // block):
        cents = cents_ref[q * block : (q + 1) * block, :]
        for g in range(groups):
            s = nt_dot(cents, docs_ref[g * 256 : (g + 1) * 256, :]).reshape(block // 8, 8, 256)
            top = jnp.maximum(tops[g], jnp.max(s, axis=0) * scale)
            totals[g] = totals[g] * jnp.exp2(tops[g] - top) + jnp.sum(jnp.exp2(s * scale - top[None]), axis=0)
            tops[g] = top
    rows = []
    for g in range(groups):
        top = jnp.max(tops[g], axis=0, keepdims=True)
        lse = top + jnp.log2(jnp.sum(totals[g] * jnp.exp2(tops[g] - top), axis=0, keepdims=True))
        rows += [lse[:, 0:LANES], lse[:, LANES:256]]
    out_ref[...] = jnp.broadcast_to((jnp.concatenate(rows, axis=0) - jnp.log2(w))[None], out_ref.shape)


def first_columns(
    scale, n_zh, parts_ref, docs_ref, other_ref, cents_ref,
    out_ref, tile_ref, top_ref, f_ref, docs_all_ref, half_ref,
):
    zl = lax.axis_index("zl")
    n_doc, n_cent = docs_ref.shape[0], cents_ref.shape[0] // 2
    groups = 2 * n_doc // LANES
    docs_all_ref[pl.ds(pl.multiple_of(zl * n_doc, n_doc), n_doc), :] = docs_ref[...]
    docs_all_ref[pl.ds(pl.multiple_of((1 - zl) * n_doc, n_doc), n_doc), :] = other_ref[...]
    run = n_cent // 2
    for q in range(2):
        rows = pl.ds(pl.multiple_of(q * n_cent + zl * run, run), run)
        half_ref[q * run : (q + 1) * run, :] = cents_ref[rows, :]
    by_zl = parts_ref[...].reshape(n_zh, 2, parts_ref.shape[0] // (2 * n_zh), 8, LANES)
    for z in range(2):
        parts = by_zl[:, z].reshape(parts_ref.shape[0] // 2, 8, LANES)
        top = jnp.max(parts, axis=0)
        f_ref[z * 8 : (z + 1) * 8, :] = -(top + jnp.log2(jnp.sum(jnp.exp2(parts - top[None]), axis=0)))

    for g in range(groups // 2):
        f = jnp.concatenate([f_ref[2 * g : 2 * g + 1, :], f_ref[2 * g + 1 : 2 * g + 2, :]], axis=1)
        docs = docs_all_ref[g * 256 : (g + 1) * 256, :]
        for q in range(n_cent // 256):
            cents = half_ref[q * 256 : (q + 1) * 256, :]
            tile_ref[q * 256 : (q + 1) * 256, g * 256 : (g + 1) * 256] = nt_dot(cents, docs) * scale + f
    lane = lane_iota()
    tops = jnp.zeros((LANES, LANES), F32)
    lses = jnp.zeros((LANES, LANES), F32)
    for r in range(n_cent // LANES):
        rows = slice(r * LANES, (r + 1) * LANES)
        top = tile_ref[rows, 0:LANES]
        for g in range(1, groups):
            top = jnp.maximum(top, tile_ref[rows, g * LANES : (g + 1) * LANES])
        top = jnp.broadcast_to(jnp.max(top, axis=1, keepdims=True), (LANES, LANES))
        total = jnp.zeros((LANES, LANES), F32)
        for g in range(groups):
            e = jnp.exp2(tile_ref[rows, g * LANES : (g + 1) * LANES] - top)
            tile_ref[rows, g * LANES : (g + 1) * LANES] = e
            total = total + e
        tops = jnp.where(lane == r, top, tops)
        lses = jnp.where(lane == r, top + jnp.log2(jnp.sum(total, axis=1, keepdims=True)), lses)
    top_ref[...] = tops.T[0:8, :]
    out_ref[...] = jnp.broadcast_to(lses.T[0:8, :][None], out_ref.shape)


def weigh_columns(c, tile_ref, out_ref):
    groups = tile_ref.shape[1] // LANES
    totals = [jnp.zeros((8, LANES), F32) for _ in range(groups)]
    for r in range(tile_ref.shape[0] // LANES):
        col = jnp.broadcast_to(c[r : r + 1, :], (LANES, LANES)).T
        for g in range(groups):
            p = tile_ref[r * LANES : (r + 1) * LANES, g * LANES : (g + 1) * LANES] * col
            totals[g] = totals[g] + jnp.sum(p.reshape(LANES // 8, 8, LANES), axis=0)
    rows = jnp.concatenate([jnp.sum(t, axis=0, keepdims=True) for t in totals], axis=0)
    out_ref[:, 0:groups, :] = jnp.broadcast_to(rows[None], (out_ref.shape[0], groups, LANES)).astype(out_ref.dtype)


def rows_after_first(log_target, parts_ref, top_ref, w_ref, tile_ref, out_ref, c_ref):
    parts = parts_ref[...]
    top = jnp.max(parts, axis=0)
    lse = top + jnp.log2(jnp.sum(jnp.exp2(parts - top[None]), axis=0))
    c = jnp.exp2(top_ref[...] + (log_target - lse))
    c_ref[...] = c
    weigh_columns(c, tile_ref, out_ref)
    w = w_ref[...]
    groups = out_ref.shape[1] - w.shape[0]
    out_ref[:, groups:, :] = jnp.broadcast_to(w[None], (out_ref.shape[0], *w.shape)).astype(out_ref.dtype)


def rows_after(target, parts_ref, last_ref, tile_ref, out_ref, c_ref):
    c = last_ref[...] * (target / jnp.sum(parts_ref[...].astype(F32), axis=0))
    c_ref[...] = c
    weigh_columns(c, tile_ref, out_ref)


def columns_after_first(n_x, parts_ref, c_ref, tile_ref, out_ref, w_ref):
    groups = w_ref.shape[0]
    w = jnp.concatenate([parts_ref[z * n_x, groups:, :].astype(F32) for z in range(2)], axis=0)
    w_ref[...] = w
    weigh_rows(w / jnp.sum(parts_ref[:, 0:groups, :].astype(F32), axis=0), c_ref, tile_ref, out_ref)


def columns_after(parts_ref, w_ref, c_ref, tile_ref, out_ref):
    weigh_rows(w_ref[...] / jnp.sum(parts_ref[...].astype(F32), axis=0), c_ref, tile_ref, out_ref)


def weigh_rows(u, c_ref, tile_ref, out_ref):
    groups = tile_ref.shape[1] // LANES
    lane = lane_iota()
    sums = jnp.zeros((LANES, LANES), F32)
    for r in range(tile_ref.shape[0] // LANES):
        total = jnp.zeros((LANES, LANES), F32)
        for g in range(groups):
            total = total + tile_ref[r * LANES : (r + 1) * LANES, g * LANES : (g + 1) * LANES] * u[g : g + 1, :]
        sums = jnp.where(lane == r, jnp.sum(total, axis=1, keepdims=True), sums)
    out = sums.T[0:8, :] * c_ref[...]
    out_ref[...] = jnp.broadcast_to(out[None], out_ref.shape).astype(out_ref.dtype)


def half_sums(side, u, c_ref, tile_ref, docs_ref, out_ref, p_ref):
    n_half, n_doc = p_ref.shape
    groups = n_doc // LANES
    blocks = n_half // LANES
    cols = to_columns(c_ref[pl.ds(side * blocks, blocks), :])
    base = pl.multiple_of(side * n_half, n_half)
    lane = lane_iota()
    masses = jnp.zeros((LANES, LANES), F32)
    for r in range(blocks):
        rows = pl.ds(pl.multiple_of(base + r * LANES, LANES), LANES)
        col = jnp.broadcast_to(cols[:, r : r + 1], (LANES, LANES))
        total = jnp.zeros((LANES, LANES), F32)
        for g in range(groups):
            lanes = slice(g * LANES, (g + 1) * LANES)
            p = tile_ref[rows, lanes] * u[g : g + 1, :] * col
            total = total + p
            p_ref[r * LANES : (r + 1) * LANES, lanes] = p.astype(BF16)
        masses = jnp.where(lane == r, jnp.sum(total, axis=1, keepdims=True), masses)
    mass = masses.T[0:8, :]
    out_ref[n_half : n_half + 8, :] = jnp.concatenate([mass, mass], axis=1)
    for b in range(n_half // 256):
        rows = slice(b * 256, (b + 1) * 256)
        out_ref[rows, :] = jnp.dot(p_ref[rows, :], docs_ref[...], preferred_element_type=F32)


def final_other(parts_ref, w_ref, f_ref, c_ref, tile_ref, docs_ref, out_ref, pot_ref, u_ref, p_ref):
    u = w_ref[...] / jnp.sum(parts_ref[...].astype(F32), axis=0)
    u_ref[...] = u
    pot = (f_ref[...] + jnp.log2(u)) * LN2
    pot_ref[...] = jnp.where(lax.axis_index("zl") == 0, pot[0:8, :], pot[8:16, :])
    half_sums(1 - lax.axis_index("core"), u, c_ref, tile_ref, docs_ref, out_ref, p_ref)


def final_own(u_ref, c_ref, tile_ref, docs_ref, out_ref, p_ref):
    half_sums(lax.axis_index("core"), u_ref[...], c_ref, tile_ref, docs_ref, out_ref, p_ref)


def final_join(own_ref, other_ref, out_ref):
    peers = out_ref.shape[0]
    n_half = own_ref.shape[0] - 8
    chunk = n_half // peers
    mass = own_ref[n_half:, 0:LANES] + other_ref[n_half:, 0:LANES]
    high = mass.astype(BF16).astype(F32)
    low = mass - high
    for q in range(peers):
        for i in range(chunk // 16):
            rows = slice(q * chunk + i * 16, q * chunk + (i + 1) * 16)
            out_ref[q, :, i * 256 : (i + 1) * 256] = (own_ref[rows, :] + other_ref[rows, :]).astype(BF16)
        r = q * chunk // LANES
        pair = [jnp.broadcast_to(x[r : r + 1, :], (8, LANES)) for x in (high, low)]
        out_ref[q, :, 256 * (chunk // 16) :] = jnp.concatenate(pair, axis=0).astype(BF16)


def divide(parts_ref, out_ref, mass_ref):
    total = parts_ref[0].astype(F32)
    for p in range(1, parts_ref.shape[0]):
        total = total + parts_ref[p].astype(F32)
    tiles = total.shape[1] // LANES - 1
    chunk = tiles * 8
    mass = total[0:8, tiles * LANES :] + total[8:16, tiles * LANES :]
    mass_ref[...] = to_columns(mass)
    col = mass_ref[pl.ds(pl.multiple_of((lax.axis_index("yc")) * chunk, chunk), chunk), :]
    for i in range(chunk // 16):
        pair = [total[:, (i * 2 + h) * LANES : (i * 2 + h + 1) * LANES] / col[i * 16 : (i + 1) * 16, :] for h in range(2)]
        new = jnp.concatenate(pair, axis=1).astype(BF16)
        out_ref[:, i * 16 : (i + 1) * 16, :] = jnp.broadcast_to(new[None], (out_ref.shape[0], 16, 256))


def place_own(x_ref, pot_ref, out_ref, pot_out_ref, sems):
    rows = x_ref.shape[0]
    place = pl.ds(pl.multiple_of(lax.axis_index("core") * rows, rows), rows)
    copies = [pltpu.make_async_copy(x_ref, out_ref.at[place, :], sems.at[0]), pltpu.make_async_copy(pot_ref, pot_out_ref, sems.at[1])]
    for copy in copies:
        copy.start()
    for copy in copies:
        copy.wait()


def place_other(x_ref, _, out_ref, sem):
    rows = x_ref.shape[0]
    copy = pltpu.make_async_copy(x_ref, out_ref.at[pl.ds(pl.multiple_of((1 - lax.axis_index("core")) * rows, rows), rows), :], sem)
    copy.start()
    copy.wait()


def exchange(x, axes):
    return lax.all_to_all(x, axes, 0, 0)


def per_device(sizes, docs, cents, shard_ids, shard_mass):
    n_y, n_zl, n_core = math.prod(sizes[0:3]), sizes[3], sizes[4]
    n_zh, n_x = math.prod(sizes[5:7]), math.prod(sizes[7:9])
    row_peers, col_peers = n_zl * n_zh * n_x, n_y * n_core
    n_doc, n_cent = docs.shape[0] * 2, cents.shape[0] // 2
    doc_rows, cent_rows = n_doc // LANES, n_cent // LANES
    scale = 4.0 * docs.shape[1] ** -0.5 * LOG2E
    target = 0.5 * (docs.shape[0] * n_y * n_zl * n_core) / (cents.shape[0] * n_zh * n_x)
    swap = [(0, 1), (1, 0)]
    shape = jax.ShapeDtypeStruct
    tile_shape = pltpu.VMEM((n_cent, n_doc), F32)
    small = shape((cent_rows, LANES), F32)

    any_space = pl.BlockSpec(memory_space=pl.ANY)
    hbm = pl.BlockSpec(memory_space=pltpu.HBM)
    other_docs = lax.ppermute(docs, "zl", swap)
    parts, docs, cents, own_w = call(
        functools.partial(first_rows, scale),
        (
            shape((row_peers, doc_rows // 2, LANES), F32),
            pltpu.VMEM(docs.shape, BF16),
            pltpu.VMEM(cents.shape, BF16),
            shape((doc_rows // 2, LANES), F32),
        ),
        4,
        in_specs=[hbm] * 4,
        scratch=[pltpu.SMEM(shard_mass.shape, jnp.int32), pltpu.VMEM((doc_rows // 2, LANES), jnp.int32), pltpu.SemaphoreType.DMA((4,))],
        flops=2 * docs.shape[0] * cents.shape[0] * 256,
    )(*[pltpu.with_memory_space_constraint(x, pltpu.HBM) for x in (shard_mass, shard_ids.reshape(-1, LANES), docs, cents)])
    parts = exchange(parts, ROWS)
    chunk = n_cent // col_peers
    parts, tile, top, f, docs_all = call(
        functools.partial(first_columns, scale, n_zh),
        (
            shape((col_peers, cent_rows, LANES), F32),
            tile_shape,
            small,
            shape((doc_rows, LANES), F32),
            pltpu.VMEM((n_doc, 256), BF16),
        ),
        4,
        scratch=[pltpu.VMEM((n_cent, 256), BF16)],
        flops=2 * n_doc * n_cent * 256,
    )(parts, docs, other_docs, cents)

    rows_out = (shape((row_peers, doc_rows, LANES), BF16), small)
    parts = exchange(parts, COLS)
    log_target = math.log2(target)
    first_out = (shape((row_peers, doc_rows + doc_rows // 2, LANES), BF16), small)
    parts, c = call(functools.partial(rows_after_first, log_target), first_out, 4, flops=2 * n_doc * n_cent)(parts, top, own_w, tile)
    col_out = shape((col_peers, cent_rows, LANES), BF16)
    for turn in range(2):
        parts = exchange(parts, ROWS)
        if turn == 0:
            out = (col_out, shape((doc_rows, LANES), F32))
            parts, w = call(functools.partial(columns_after_first, n_x), out, 3, flops=2 * n_doc * n_cent)(parts, c, tile)
        else:
            parts = call(columns_after, col_out, 4, flops=2 * n_doc * n_cent)(parts, w, c, tile)
        parts = exchange(parts, COLS)
        parts, c = call(functools.partial(rows_after, target), rows_out, 3, flops=2 * n_doc * n_cent)(parts, c, tile)
    parts = exchange(parts, ROWS)
    n_half = n_cent // n_core
    half_flops = 2 * n_doc * n_half * 256
    part_shape = pltpu.VMEM((n_half + 8, 256), F32)
    p_scratch = [pltpu.VMEM((n_half, n_doc), BF16)]
    for_other, pot, u = call(
        final_other,
        (part_shape, pltpu.VMEM((doc_rows // 2, LANES), F32), shape((doc_rows, LANES), F32)),
        6,
        scratch=p_scratch,
        flops=half_flops,
    )(parts, w, f, c, tile, docs_all)
    from_other = lax.ppermute(for_other, "core", swap)
    for_own = call(final_own, part_shape, 4, scratch=p_scratch, flops=half_flops)(u, c, tile, docs_all)
    sums = call(final_join, shape((n_y, 16, 2 * LANES * (chunk // 16) + LANES), BF16), 2)(for_own, from_other)
    sums = exchange(sums, SUMS)
    new = call(divide, shape((n_y * n_zl, chunk, 256), BF16), 1, scratch=[pltpu.VMEM((LANES, LANES), F32)])(sums)
    own = exchange(new, ("zl", *SUMS)).reshape(n_y * n_zl * chunk, 256)
    other = lax.ppermute(own, "core", swap)
    placed = shape((cents.shape[0], 256), BF16)
    new, pot = call(
        place_own,
        (placed, shape((doc_rows // 2, LANES), F32)),
        2,
        in_specs=[any_space, pl.BlockSpec(memory_space=pltpu.VMEM)],
        out_specs=(any_space, any_space),
        scratch=[pltpu.SemaphoreType.DMA((2,))],
    )(own, pot)
    new = call(
        place_other, placed, 2, in_specs=[any_space, any_space], out_specs=any_space, scratch=[pltpu.SemaphoreType.DMA], alias={1: 0}
    )(other, new)
    return new, pot.reshape(-1)


SIZES = (2, 2, 2, 2, 2, 2, 2, 2, 2)


def solution(mesh, sizes=SIZES):
    fine = Mesh(mesh.devices.reshape(sizes), ("ya", "yb", "yc", "zl", "core", "za", "zb", "xa", "xb"))
    docs, cents = ("ya", "yb", "yc", "zl", "core"), ("za", "zb", "xa", "xb")
    return jax.shard_map(
        functools.partial(per_device, sizes),
        mesh=fine,
        in_specs=(P(docs, None), P(cents, None), P(docs), P()),
        out_specs=(P(cents, None), P(docs)),
        check_vma=False,
    )
```

```python
import functools
import math

import jax
import jax.numpy as jnp
from jax import lax
from jax.experimental import pallas as pl
from jax.experimental.pallas import tpu as pltpu
from jax.sharding import Mesh
from jax.sharding import PartitionSpec as P

LOG2E = 1.4426950408889634
LN2 = 0.6931471805599453
LANES = 128
VMEM_LIMIT = 32 * 1024 * 1024
ROWS = ("zb", "za", "zl", "xb", "xa")
COLS = ("yc", "yb", "ya", "core")
SUMS = ("yb", "ya", "yc")
F32 = jnp.float32
BF16 = jnp.bfloat16


def call(kernel, out_shape, n_in, scratch=(), flops=0, out_specs=None, in_specs=None, alias=None):
    vmem = pl.BlockSpec(memory_space=pltpu.VMEM)
    if in_specs is None:
        in_specs = [vmem] * n_in
    if out_specs is None:
        out_specs = jax.tree.map(lambda _: vmem, out_shape)
    return pl.pallas_call(
        kernel,
        out_shape=out_shape,
        in_specs=in_specs,
        out_specs=out_specs,
        scratch_shapes=list(scratch),
        input_output_aliases=alias or {},
        compiler_params=pltpu.CompilerParams(vmem_limit_bytes=VMEM_LIMIT),
        cost_estimate=pl.CostEstimate(flops=flops, bytes_accessed=1 << 20, transcendentals=0),
    )


def lane_iota():
    return lax.broadcasted_iota(jnp.int32, (LANES, LANES), 1)


def to_columns(dense):
    return jnp.concatenate([dense] * (LANES // dense.shape[0]), axis=0).T


def nt_dot(a, b):
    return lax.dot_general(a, b, (((1,), (1,)), ((), ())), preferred_element_type=F32)


def weights_of(ids, mass_ref):
    def step(s, total):
        return jnp.where(ids == s, mass_ref[s].astype(F32), total)

    return lax.fori_loop(0, mass_ref.shape[0], step, jnp.zeros(ids.shape, F32), unroll=True) * 0.125


def first_rows(
    scale, mass_hbm, ids_hbm, docs_hbm, cents_hbm, out_ref, docs_ref, cents_ref, w_ref, mass_ref, ids_ref, sems
):
    n_doc, n_cent = docs_hbm.shape[0], cents_hbm.shape[0]
    block = 512
    copies = [
        pltpu.make_async_copy(src, dst, sems.at[k])
        for k, (src, dst) in enumerate(((mass_hbm, mass_ref), (ids_hbm, ids_ref), (docs_hbm, docs_ref), (cents_hbm, cents_ref)))
    ]
    for copy in copies:
        copy.start()
    copies[0].wait()
    copies[1].wait()
    w = weights_of(ids_ref[...], mass_ref)
    w_ref[...] = w
    copies[2].wait()
    copies[3].wait()
    groups = n_doc // 256
    tops = [jnp.full((8, 256), -jnp.inf, F32)] * groups
    totals = [jnp.zeros((8, 256), F32)] * groups
    for q in range(n_cent // block):
        cents = cents_ref[q * block : (q + 1) * block, :]
        for g in range(groups):
            s = nt_dot(cents, docs_ref[g * 256 : (g + 1) * 256, :]).reshape(block // 8, 8, 256)
            top = jnp.maximum(tops[g], jnp.max(s, axis=0) * scale)
            totals[g] = totals[g] * jnp.exp2(tops[g] - top) + jnp.sum(jnp.exp2(s * scale - top[None]), axis=0)
            tops[g] = top
    rows = []
    for g in range(groups):
        top = jnp.max(tops[g], axis=0, keepdims=True)
        lse = top + jnp.log2(jnp.sum(totals[g] * jnp.exp2(tops[g] - top), axis=0, keepdims=True))
        rows += [lse[:, 0:LANES], lse[:, LANES:256]]
    out_ref[...] = jnp.broadcast_to((jnp.concatenate(rows, axis=0) - jnp.log2(w))[None], out_ref.shape)


def first_columns(
    scale, n_zh, parts_ref, docs_ref, other_ref, cents_ref,
    out_ref, tile_ref, top_ref, f_ref, docs_all_ref,
):
    zl = lax.axis_index("zl")
    n_doc, n_cent = docs_ref.shape[0], cents_ref.shape[0] // 2
    groups = 2 * n_doc // LANES
    docs_all_ref[pl.ds(pl.multiple_of(zl * n_doc, n_doc), n_doc), :] = docs_ref[...]
    docs_all_ref[pl.ds(pl.multiple_of((1 - zl) * n_doc, n_doc), n_doc), :] = other_ref[...]
    by_zl = parts_ref[...].reshape(n_zh, 2, parts_ref.shape[0] // (2 * n_zh), 8, LANES)
    for z in range(2):
        parts = by_zl[:, z].reshape(parts_ref.shape[0] // 2, 8, LANES)
        top = jnp.max(parts, axis=0)
        f_ref[z * 8 : (z + 1) * 8, :] = -(top + jnp.log2(jnp.sum(jnp.exp2(parts - top[None]), axis=0)))

    run = n_cent // 2
    maxima = []
    for q in range(n_cent // 256):
        start = (q * 256 // run) * n_cent + q * 256 % run
        cents = cents_ref[pl.ds(pl.multiple_of(start + zl * run, 256), 256), :]
        top = None
        for g in range(groups // 2):
            f = jnp.concatenate([f_ref[2 * g : 2 * g + 1, :], f_ref[2 * g + 1 : 2 * g + 2, :]], axis=1)
            s = nt_dot(cents, docs_all_ref[g * 256 : (g + 1) * 256, :]) * scale + f
            tile_ref[q * 256 : (q + 1) * 256, g * 256 : (g + 1) * 256] = s
            larger = jnp.maximum(s[:, 0:LANES], s[:, LANES:256])
            top = larger if top is None else jnp.maximum(top, larger)
        maxima += [top[0:LANES], top[LANES:256]]
    lane = lane_iota()
    tops = jnp.zeros((LANES, LANES), F32)
    lses = jnp.zeros((LANES, LANES), F32)
    for r in range(n_cent // LANES):
        rows = slice(r * LANES, (r + 1) * LANES)
        top = jnp.broadcast_to(jnp.max(maxima[r], axis=1, keepdims=True), (LANES, LANES))
        total = jnp.zeros((LANES, LANES), F32)
        for g in range(groups):
            e = jnp.exp2(tile_ref[rows, g * LANES : (g + 1) * LANES] - top)
            tile_ref[rows, g * LANES : (g + 1) * LANES] = e
            total = total + e
        tops = jnp.where(lane == r, top, tops)
        lses = jnp.where(lane == r, top + jnp.log2(jnp.sum(total, axis=1, keepdims=True)), lses)
    top_ref[...] = tops.T[0:8, :]
    out_ref[...] = jnp.broadcast_to(lses.T[0:8, :][None], out_ref.shape)


def weigh_columns(c, tile_ref, out_ref):
    groups = tile_ref.shape[1] // LANES
    totals = [jnp.zeros((8, LANES), F32) for _ in range(groups)]
    for r in range(tile_ref.shape[0] // LANES):
        col = jnp.broadcast_to(c[r : r + 1, :], (LANES, LANES)).T
        for g in range(groups):
            p = tile_ref[r * LANES : (r + 1) * LANES, g * LANES : (g + 1) * LANES] * col
            totals[g] = totals[g] + jnp.sum(p.reshape(LANES // 8, 8, LANES), axis=0)
    rows = jnp.concatenate([jnp.sum(t, axis=0, keepdims=True) for t in totals], axis=0)
    out_ref[:, 0:groups, :] = jnp.broadcast_to(rows[None], (out_ref.shape[0], groups, LANES)).astype(out_ref.dtype)


def rows_after_first(log_target, parts_ref, top_ref, w_ref, tile_ref, out_ref, c_ref):
    parts = parts_ref[...]
    top = jnp.max(parts, axis=0)
    lse = top + jnp.log2(jnp.sum(jnp.exp2(parts - top[None]), axis=0))
    c = jnp.exp2(top_ref[...] + (log_target - lse))
    c_ref[...] = c
    weigh_columns(c, tile_ref, out_ref)
    w = w_ref[...]
    groups = out_ref.shape[1] - w.shape[0]
    out_ref[:, groups:, :] = jnp.broadcast_to(w[None], (out_ref.shape[0], *w.shape)).astype(out_ref.dtype)


def rows_after(target, parts_ref, last_ref, tile_ref, out_ref, c_ref):
    c = last_ref[...] * (target / jnp.sum(parts_ref[...].astype(F32), axis=0))
    c_ref[...] = c
    weigh_columns(c, tile_ref, out_ref)


def columns_after_first(n_x, parts_ref, c_ref, tile_ref, out_ref, w_ref):
    groups = w_ref.shape[0]
    w = jnp.concatenate([parts_ref[z * n_x, groups:, :].astype(F32) for z in range(2)], axis=0)
    w_ref[...] = w
    weigh_rows(w / jnp.sum(parts_ref[:, 0:groups, :].astype(F32), axis=0), c_ref, tile_ref, out_ref)


def columns_after(parts_ref, w_ref, c_ref, tile_ref, out_ref):
    weigh_rows(w_ref[...] / jnp.sum(parts_ref[...].astype(F32), axis=0), c_ref, tile_ref, out_ref)


def weigh_rows(u, c_ref, tile_ref, out_ref):
    groups = tile_ref.shape[1] // LANES
    lane = lane_iota()
    sums = jnp.zeros((LANES, LANES), F32)
    for r in range(tile_ref.shape[0] // LANES):
        total = jnp.zeros((LANES, LANES), F32)
        for g in range(groups):
            total = total + tile_ref[r * LANES : (r + 1) * LANES, g * LANES : (g + 1) * LANES] * u[g : g + 1, :]
        sums = jnp.where(lane == r, jnp.sum(total, axis=1, keepdims=True), sums)
    out = sums.T[0:8, :] * c_ref[...]
    out_ref[...] = jnp.broadcast_to(out[None], out_ref.shape).astype(out_ref.dtype)


def half_sums(side, u, c_ref, tile_ref, docs_ref, out_ref, p_ref):
    n_half, n_doc = p_ref.shape
    groups = n_doc // LANES
    blocks = n_half // LANES
    cols = to_columns(c_ref[pl.ds(side * blocks, blocks), :])
    base = pl.multiple_of(side * n_half, n_half)
    lane = lane_iota()
    masses = jnp.zeros((LANES, LANES), F32)
    for r in range(blocks):
        rows = pl.ds(pl.multiple_of(base + r * LANES, LANES), LANES)
        col = jnp.broadcast_to(cols[:, r : r + 1], (LANES, LANES))
        total = jnp.zeros((LANES, LANES), F32)
        for g in range(groups):
            lanes = slice(g * LANES, (g + 1) * LANES)
            p = tile_ref[rows, lanes] * u[g : g + 1, :] * col
            total = total + p
            p_ref[r * LANES : (r + 1) * LANES, lanes] = p.astype(BF16)
        masses = jnp.where(lane == r, jnp.sum(total, axis=1, keepdims=True), masses)
    mass = masses.T[0:8, :]
    out_ref[n_half : n_half + 8, :] = jnp.concatenate([mass, mass], axis=1)
    for b in range(n_half // 256):
        rows = slice(b * 256, (b + 1) * 256)
        out_ref[rows, :] = jnp.dot(p_ref[rows, :], docs_ref[...], preferred_element_type=F32)


def final_other(parts_ref, w_ref, f_ref, c_ref, tile_ref, docs_ref, out_ref, pot_ref, u_ref, p_ref):
    u = w_ref[...] / jnp.sum(parts_ref[...].astype(F32), axis=0)
    u_ref[...] = u
    pot = (f_ref[...] + jnp.log2(u)) * LN2
    pot_ref[...] = jnp.where(lax.axis_index("zl") == 0, pot[0:8, :], pot[8:16, :])
    half_sums(1 - lax.axis_index("core"), u, c_ref, tile_ref, docs_ref, out_ref, p_ref)


def final_own(u_ref, c_ref, tile_ref, docs_ref, out_ref, p_ref):
    half_sums(lax.axis_index("core"), u_ref[...], c_ref, tile_ref, docs_ref, out_ref, p_ref)


def final_join(own_ref, other_ref, out_ref):
    peers = out_ref.shape[0]
    n_half = own_ref.shape[0] - 8
    chunk = n_half // peers
    mass = own_ref[n_half:, 0:LANES] + other_ref[n_half:, 0:LANES]
    high = mass.astype(BF16).astype(F32)
    low = mass - high
    for q in range(peers):
        for i in range(chunk // 16):
            rows = slice(q * chunk + i * 16, q * chunk + (i + 1) * 16)
            out_ref[q, :, i * 256 : (i + 1) * 256] = (own_ref[rows, :] + other_ref[rows, :]).astype(BF16)
        r = q * chunk // LANES
        pair = [jnp.broadcast_to(x[r : r + 1, :], (8, LANES)) for x in (high, low)]
        out_ref[q, :, 256 * (chunk // 16) :] = jnp.concatenate(pair, axis=0).astype(BF16)


def divide(parts_ref, out_ref, mass_ref):
    total = parts_ref[0].astype(F32)
    for p in range(1, parts_ref.shape[0]):
        total = total + parts_ref[p].astype(F32)
    tiles = total.shape[1] // LANES - 1
    chunk = tiles * 8
    mass = total[0:8, tiles * LANES :] + total[8:16, tiles * LANES :]
    mass_ref[...] = to_columns(mass)
    col = mass_ref[pl.ds(pl.multiple_of((lax.axis_index("yc")) * chunk, chunk), chunk), :]
    for i in range(chunk // 16):
        pair = [total[:, (i * 2 + h) * LANES : (i * 2 + h + 1) * LANES] / col[i * 16 : (i + 1) * 16, :] for h in range(2)]
        new = jnp.concatenate(pair, axis=1).astype(BF16)
        out_ref[:, i * 16 : (i + 1) * 16, :] = jnp.broadcast_to(new[None], (out_ref.shape[0], 16, 256))


def place_own(x_ref, pot_ref, out_ref, pot_out_ref, sems):
    rows = x_ref.shape[0]
    place = pl.ds(pl.multiple_of(lax.axis_index("core") * rows, rows), rows)
    copies = [pltpu.make_async_copy(x_ref, out_ref.at[place, :], sems.at[0]), pltpu.make_async_copy(pot_ref, pot_out_ref, sems.at[1])]
    for copy in copies:
        copy.start()
    for copy in copies:
        copy.wait()


def place_other(x_ref, _, out_ref, sem):
    rows = x_ref.shape[0]
    copy = pltpu.make_async_copy(x_ref, out_ref.at[pl.ds(pl.multiple_of((1 - lax.axis_index("core")) * rows, rows), rows), :], sem)
    copy.start()
    copy.wait()


def exchange(x, axes):
    return lax.all_to_all(x, axes, 0, 0)


def per_device(sizes, docs, cents, shard_ids, shard_mass):
    n_y, n_zl, n_core = math.prod(sizes[0:3]), sizes[3], sizes[4]
    n_zh, n_x = math.prod(sizes[5:7]), math.prod(sizes[7:9])
    row_peers, col_peers = n_zl * n_zh * n_x, n_y * n_core
    n_doc, n_cent = docs.shape[0] * 2, cents.shape[0] // 2
    doc_rows, cent_rows = n_doc // LANES, n_cent // LANES
    scale = 4.0 * docs.shape[1] ** -0.5 * LOG2E
    target = 0.5 * (docs.shape[0] * n_y * n_zl * n_core) / (cents.shape[0] * n_zh * n_x)
    swap = [(0, 1), (1, 0)]
    shape = jax.ShapeDtypeStruct
    tile_shape = pltpu.VMEM((n_cent, n_doc), F32)
    small = shape((cent_rows, LANES), F32)

    any_space = pl.BlockSpec(memory_space=pl.ANY)
    hbm = pl.BlockSpec(memory_space=pltpu.HBM)
    other_docs = lax.ppermute(docs, "zl", swap)
    parts, docs, cents, own_w = call(
        functools.partial(first_rows, scale),
        (
            shape((row_peers, doc_rows // 2, LANES), F32),
            pltpu.VMEM(docs.shape, BF16),
            pltpu.VMEM(cents.shape, BF16),
            shape((doc_rows // 2, LANES), F32),
        ),
        4,
        in_specs=[hbm] * 4,
        scratch=[pltpu.SMEM(shard_mass.shape, jnp.int32), pltpu.VMEM((doc_rows // 2, LANES), jnp.int32), pltpu.SemaphoreType.DMA((4,))],
        flops=2 * docs.shape[0] * cents.shape[0] * 256,
    )(*[pltpu.with_memory_space_constraint(x, pltpu.HBM) for x in (shard_mass, shard_ids.reshape(-1, LANES), docs, cents)])
    parts = exchange(parts, ROWS)
    chunk = n_cent // col_peers
    parts, tile, top, f, docs_all = call(
        functools.partial(first_columns, scale, n_zh),
        (
            shape((col_peers, cent_rows, LANES), F32),
            tile_shape,
            small,
            shape((doc_rows, LANES), F32),
            pltpu.VMEM((n_doc, 256), BF16),
        ),
        4,
        flops=2 * n_doc * n_cent * 256,
    )(parts, docs, other_docs, cents)

    rows_out = (shape((row_peers, doc_rows, LANES), BF16), small)
    parts = exchange(parts, COLS)
    log_target = math.log2(target)
    first_out = (shape((row_peers, doc_rows + doc_rows // 2, LANES), BF16), small)
    parts, c = call(functools.partial(rows_after_first, log_target), first_out, 4, flops=2 * n_doc * n_cent)(parts, top, own_w, tile)
    col_out = shape((col_peers, cent_rows, LANES), BF16)
    for turn in range(2):
        parts = exchange(parts, ROWS)
        if turn == 0:
            out = (col_out, shape((doc_rows, LANES), F32))
            parts, w = call(functools.partial(columns_after_first, n_x), out, 3, flops=2 * n_doc * n_cent)(parts, c, tile)
        else:
            parts = call(columns_after, col_out, 4, flops=2 * n_doc * n_cent)(parts, w, c, tile)
        parts = exchange(parts, COLS)
        parts, c = call(functools.partial(rows_after, target), rows_out, 3, flops=2 * n_doc * n_cent)(parts, c, tile)
    parts = exchange(parts, ROWS)
    n_half = n_cent // n_core
    half_flops = 2 * n_doc * n_half * 256
    part_shape = pltpu.VMEM((n_half + 8, 256), F32)
    p_scratch = [pltpu.VMEM((n_half, n_doc), BF16)]
    for_other, pot, u = call(
        final_other,
        (part_shape, pltpu.VMEM((doc_rows // 2, LANES), F32), shape((doc_rows, LANES), F32)),
        6,
        scratch=p_scratch,
        flops=half_flops,
    )(parts, w, f, c, tile, docs_all)
    from_other = lax.ppermute(for_other, "core", swap)
    for_own = call(final_own, part_shape, 4, scratch=p_scratch, flops=half_flops)(u, c, tile, docs_all)
    sums = call(final_join, shape((n_y, 16, 2 * LANES * (chunk // 16) + LANES), BF16), 2)(for_own, from_other)
    sums = exchange(sums, SUMS)
    new = call(divide, shape((n_y * n_zl, chunk, 256), BF16), 1, scratch=[pltpu.VMEM((LANES, LANES), F32)])(sums)
    own = exchange(new, ("zl", *SUMS)).reshape(n_y * n_zl * chunk, 256)
    other = lax.ppermute(own, "core", swap)
    placed = shape((cents.shape[0], 256), BF16)
    new, pot = call(
        place_own,
        (placed, shape((doc_rows // 2, LANES), F32)),
        2,
        in_specs=[any_space, pl.BlockSpec(memory_space=pltpu.VMEM)],
        out_specs=(any_space, any_space),
        scratch=[pltpu.SemaphoreType.DMA((2,))],
    )(own, pot)
    new = call(
        place_other, placed, 2, in_specs=[any_space, any_space], out_specs=any_space, scratch=[pltpu.SemaphoreType.DMA], alias={1: 0}
    )(other, new)
    return new, pot.reshape(-1)


SIZES = (2, 2, 2, 2, 2, 2, 2, 2, 2)


def solution(mesh, sizes=SIZES):
    fine = Mesh(mesh.devices.reshape(sizes), ("ya", "yb", "yc", "zl", "core", "za", "zb", "xa", "xb"))
    docs, cents = ("ya", "yb", "yc", "zl", "core"), ("za", "zb", "xa", "xb")
    return jax.shard_map(
        functools.partial(per_device, sizes),
        mesh=fine,
        in_specs=(P(docs, None), P(cents, None), P(docs), P()),
        out_specs=(P(cents, None), P(docs)),
        check_vma=False,
    )
```

```python
import functools
import math

import jax
import jax.numpy as jnp
from jax import lax
from jax.experimental import pallas as pl
from jax.experimental.pallas import tpu as pltpu
from jax.sharding import Mesh
from jax.sharding import PartitionSpec as P

LOG2E = 1.4426950408889634
LN2 = 0.6931471805599453
LANES = 128
VMEM_LIMIT = 32 * 1024 * 1024
ROWS = ("zb", "za", "zl", "xb", "xa")
COLS = ("yc", "yb", "ya", "core")
SUMS = ("yb", "ya", "yc")
F32 = jnp.float32
BF16 = jnp.bfloat16


def call(kernel, out_shape, n_in, scratch=(), flops=0, out_specs=None, in_specs=None, alias=None):
    vmem = pl.BlockSpec(memory_space=pltpu.VMEM)
    if in_specs is None:
        in_specs = [vmem] * n_in
    if out_specs is None:
        out_specs = jax.tree.map(lambda _: vmem, out_shape)
    return pl.pallas_call(
        kernel,
        out_shape=out_shape,
        in_specs=in_specs,
        out_specs=out_specs,
        scratch_shapes=list(scratch),
        input_output_aliases=alias or {},
        compiler_params=pltpu.CompilerParams(vmem_limit_bytes=VMEM_LIMIT),
        cost_estimate=pl.CostEstimate(flops=flops, bytes_accessed=1 << 20, transcendentals=0),
    )


def lane_iota():
    return lax.broadcasted_iota(jnp.int32, (LANES, LANES), 1)


def to_columns(dense):
    return jnp.concatenate([dense] * (LANES // dense.shape[0]), axis=0).T


def nt_dot(a, b):
    return lax.dot_general(a, b, (((1,), (1,)), ((), ())), preferred_element_type=F32)


def weights_of(ids, mass_ref):
    def step(s, total):
        return jnp.where(ids == s, mass_ref[s].astype(F32), total)

    return lax.fori_loop(0, mass_ref.shape[0], step, jnp.zeros(ids.shape, F32), unroll=True) * 0.125


def first_rows(
    scale, mass_hbm, ids_hbm, docs_hbm, cents_hbm, out_ref, docs_ref, cents_ref, w_ref, mass_ref, ids_ref, sems
):
    n_doc, n_cent = docs_hbm.shape[0], cents_hbm.shape[0]
    block = 512
    copies = [
        pltpu.make_async_copy(src, dst, sems.at[k])
        for k, (src, dst) in enumerate(((mass_hbm, mass_ref), (ids_hbm, ids_ref), (docs_hbm, docs_ref), (cents_hbm, cents_ref)))
    ]
    for copy in copies:
        copy.start()
    copies[0].wait()
    copies[1].wait()
    w = weights_of(ids_ref[...], mass_ref)
    w_ref[...] = w
    copies[2].wait()
    copies[3].wait()
    groups = n_doc // 256
    tops = [jnp.full((8, 256), -jnp.inf, F32)] * groups
    totals = [jnp.zeros((8, 256), F32)] * groups
    for q in range(n_cent // block):
        cents = cents_ref[q * block : (q + 1) * block, :]
        for g in range(groups):
            s = nt_dot(cents, docs_ref[g * 256 : (g + 1) * 256, :]).reshape(block // 8, 8, 256)
            top = jnp.maximum(tops[g], jnp.max(s, axis=0) * scale)
            totals[g] = totals[g] * jnp.exp2(tops[g] - top) + jnp.sum(jnp.exp2(s * scale - top[None]), axis=0)
            tops[g] = top
    rows = []
    for g in range(groups):
        top = jnp.max(tops[g], axis=0, keepdims=True)
        lse = top + jnp.log2(jnp.sum(totals[g] * jnp.exp2(tops[g] - top), axis=0, keepdims=True))
        rows += [lse[:, 0:LANES], lse[:, LANES:256]]
    out_ref[...] = jnp.broadcast_to((jnp.concatenate(rows, axis=0) - jnp.log2(w))[None], out_ref.shape)


def first_columns(
    scale, n_zh, parts_ref, docs_ref, other_ref, cents_ref,
    out_ref, tile_ref, top_ref, f_ref, docs_all_ref,
):
    zl = lax.axis_index("zl")
    n_doc, n_cent = docs_ref.shape[0], cents_ref.shape[0] // 2
    groups = 2 * n_doc // LANES
    docs_all_ref[pl.ds(pl.multiple_of(zl * n_doc, n_doc), n_doc), :] = docs_ref[...]
    docs_all_ref[pl.ds(pl.multiple_of((1 - zl) * n_doc, n_doc), n_doc), :] = other_ref[...]
    by_zl = parts_ref[...].reshape(n_zh, 2, parts_ref.shape[0] // (2 * n_zh), 8, LANES)
    for z in range(2):
        parts = by_zl[:, z].reshape(parts_ref.shape[0] // 2, 8, LANES)
        top = jnp.max(parts, axis=0)
        f_ref[z * 8 : (z + 1) * 8, :] = -(top + jnp.log2(jnp.sum(jnp.exp2(parts - top[None]), axis=0)))

    run = n_cent // 2
    maxima = []
    for q in range(n_cent // 256):
        start = (q * 256 // run) * n_cent + q * 256 % run
        cents = cents_ref[pl.ds(pl.multiple_of(start + zl * run, 256), 256), :]
        top = None
        for g in range(groups // 2):
            f = jnp.concatenate([f_ref[2 * g : 2 * g + 1, :], f_ref[2 * g + 1 : 2 * g + 2, :]], axis=1)
            s = nt_dot(cents, docs_all_ref[g * 256 : (g + 1) * 256, :]) * scale + f
            tile_ref[q * 256 : (q + 1) * 256, g * 256 : (g + 1) * 256] = s
            larger = jnp.maximum(s[:, 0:LANES], s[:, LANES:256])
            top = larger if top is None else jnp.maximum(top, larger)
        maxima += [top[0:LANES], top[LANES:256]]
    lane = lane_iota()
    tops = jnp.zeros((LANES, LANES), F32)
    lses = jnp.zeros((LANES, LANES), F32)
    for r in range(n_cent // LANES):
        rows = slice(r * LANES, (r + 1) * LANES)
        top = jnp.broadcast_to(jnp.max(maxima[r], axis=1, keepdims=True), (LANES, LANES))
        total = jnp.zeros((LANES, LANES), F32)
        for g in range(groups):
            e = jnp.exp2(tile_ref[rows, g * LANES : (g + 1) * LANES] - top)
            tile_ref[rows, g * LANES : (g + 1) * LANES] = e
            total = total + e
        tops = jnp.where(lane == r, top, tops)
        lses = jnp.where(lane == r, top + jnp.log2(jnp.sum(total, axis=1, keepdims=True)), lses)
    top_ref[...] = tops.T[0:8, :]
    out_ref[...] = jnp.broadcast_to(lses.T[0:8, :][None], out_ref.shape)


def weigh_columns(c, tile_ref, out_ref):
    groups = tile_ref.shape[1] // LANES
    totals = [jnp.zeros((8, LANES), F32) for _ in range(groups)]
    for r in range(tile_ref.shape[0] // LANES):
        col = jnp.broadcast_to(c[r : r + 1, :], (LANES, LANES)).T
        for g in range(groups):
            p = tile_ref[r * LANES : (r + 1) * LANES, g * LANES : (g + 1) * LANES] * col
            totals[g] = totals[g] + jnp.sum(p.reshape(LANES // 8, 8, LANES), axis=0)
    rows = jnp.concatenate([jnp.sum(t, axis=0, keepdims=True) for t in totals], axis=0)
    out_ref[:, 0:groups, :] = jnp.broadcast_to(rows[None], (out_ref.shape[0], groups, LANES)).astype(out_ref.dtype)


def rows_after_first(log_target, parts_ref, top_ref, w_ref, tile_ref, out_ref, c_ref):
    parts = parts_ref[...]
    top = jnp.max(parts, axis=0)
    lse = top + jnp.log2(jnp.sum(jnp.exp2(parts - top[None]), axis=0))
    c = jnp.exp2(top_ref[...] + (log_target - lse))
    c_ref[...] = c
    weigh_columns(c, tile_ref, out_ref)
    w = w_ref[...]
    groups = out_ref.shape[1] - w.shape[0]
    out_ref[:, groups:, :] = jnp.broadcast_to(w[None], (out_ref.shape[0], *w.shape)).astype(out_ref.dtype)


def rows_after(target, parts_ref, last_ref, tile_ref, out_ref, c_ref):
    c = last_ref[...] * (target / jnp.sum(parts_ref[...].astype(F32), axis=0))
    c_ref[...] = c
    weigh_columns(c, tile_ref, out_ref)


def columns_after_first(n_x, parts_ref, c_ref, tile_ref, out_ref, w_ref):
    groups = w_ref.shape[0]
    w = jnp.concatenate([parts_ref[z * n_x, groups:, :].astype(F32) for z in range(2)], axis=0)
    w_ref[...] = w
    weigh_rows(w / jnp.sum(parts_ref[:, 0:groups, :].astype(F32), axis=0), c_ref, tile_ref, out_ref)


def columns_after(parts_ref, w_ref, c_ref, tile_ref, out_ref):
    weigh_rows(w_ref[...] / jnp.sum(parts_ref[...].astype(F32), axis=0), c_ref, tile_ref, out_ref)


def weigh_rows(u, c_ref, tile_ref, out_ref):
    groups = tile_ref.shape[1] // LANES
    lane = lane_iota()
    sums = jnp.zeros((LANES, LANES), F32)
    for r in range(tile_ref.shape[0] // LANES):
        total = jnp.zeros((LANES, LANES), F32)
        for g in range(groups):
            total = total + tile_ref[r * LANES : (r + 1) * LANES, g * LANES : (g + 1) * LANES] * u[g : g + 1, :]
        sums = jnp.where(lane == r, jnp.sum(total, axis=1, keepdims=True), sums)
    out = sums.T[0:8, :] * c_ref[...]
    out_ref[...] = jnp.broadcast_to(out[None], out_ref.shape).astype(out_ref.dtype)


def half_sums(side, u, c_ref, tile_ref, docs_ref, out_ref, p_ref):
    n_half, n_doc = p_ref.shape
    groups = n_doc // LANES
    blocks = n_half // LANES
    c = c_ref[pl.ds(side * blocks, blocks), :]
    base = pl.multiple_of(side * n_half, n_half)
    lane = lane_iota()
    masses = jnp.zeros((LANES, LANES), F32)
    for r in range(blocks):
        rows = pl.ds(pl.multiple_of(base + r * LANES, LANES), LANES)
        col = jnp.broadcast_to(c[r : r + 1, :], (LANES, LANES)).T
        total = jnp.zeros((LANES, LANES), F32)
        for g in range(groups):
            lanes = slice(g * LANES, (g + 1) * LANES)
            p = tile_ref[rows, lanes] * u[g : g + 1, :] * col
            total = total + p
            p_ref[r * LANES : (r + 1) * LANES, lanes] = p.astype(BF16)
        masses = jnp.where(lane == r, jnp.sum(total, axis=1, keepdims=True), masses)
    mass = masses.T[0:8, :]
    out_ref[n_half : n_half + 8, :] = jnp.concatenate([mass, mass], axis=1)
    for b in range(n_half // 256):
        rows = slice(b * 256, (b + 1) * 256)
        out_ref[rows, :] = jnp.dot(p_ref[rows, :], docs_ref[...], preferred_element_type=F32)


def final_other(parts_ref, w_ref, f_ref, c_ref, tile_ref, docs_ref, out_ref, pot_ref, u_ref, p_ref):
    u = w_ref[...] / jnp.sum(parts_ref[...].astype(F32), axis=0)
    u_ref[...] = u
    pot = (f_ref[...] + jnp.log2(u)) * LN2
    pot_ref[...] = jnp.where(lax.axis_index("zl") == 0, pot[0:8, :], pot[8:16, :])
    half_sums(1 - lax.axis_index("core"), u, c_ref, tile_ref, docs_ref, out_ref, p_ref)


def final_own(u_ref, c_ref, tile_ref, docs_ref, out_ref, p_ref):
    half_sums(lax.axis_index("core"), u_ref[...], c_ref, tile_ref, docs_ref, out_ref, p_ref)


def final_join(own_ref, other_ref, out_ref):
    peers = out_ref.shape[0]
    n_half = own_ref.shape[0] - 8
    chunk = n_half // peers
    mass = own_ref[n_half:, 0:LANES] + other_ref[n_half:, 0:LANES]
    high = mass.astype(BF16).astype(F32)
    low = mass - high
    for q in range(peers):
        for i in range(chunk // 16):
            rows = slice(q * chunk + i * 16, q * chunk + (i + 1) * 16)
            out_ref[q, :, i * 256 : (i + 1) * 256] = (own_ref[rows, :] + other_ref[rows, :]).astype(BF16)
        r = q * chunk // LANES
        pair = [jnp.broadcast_to(x[r : r + 1, :], (8, LANES)) for x in (high, low)]
        out_ref[q, :, 256 * (chunk // 16) :] = jnp.concatenate(pair, axis=0).astype(BF16)


def divide(parts_ref, out_ref, mass_ref):
    total = parts_ref[0].astype(F32)
    for p in range(1, parts_ref.shape[0]):
        total = total + parts_ref[p].astype(F32)
    tiles = total.shape[1] // LANES - 1
    chunk = tiles * 8
    mass = total[0:8, tiles * LANES :] + total[8:16, tiles * LANES :]
    mass_ref[...] = to_columns(mass)
    col = mass_ref[pl.ds(pl.multiple_of((lax.axis_index("yc")) * chunk, chunk), chunk), :]
    for i in range(chunk // 16):
        pair = [total[:, (i * 2 + h) * LANES : (i * 2 + h + 1) * LANES] / col[i * 16 : (i + 1) * 16, :] for h in range(2)]
        new = jnp.concatenate(pair, axis=1).astype(BF16)
        out_ref[:, i * 16 : (i + 1) * 16, :] = jnp.broadcast_to(new[None], (out_ref.shape[0], 16, 256))


def place_own(x_ref, pot_ref, out_ref, pot_out_ref, sems):
    rows = x_ref.shape[0]
    place = pl.ds(pl.multiple_of(lax.axis_index("core") * rows, rows), rows)
    copies = [pltpu.make_async_copy(x_ref, out_ref.at[place, :], sems.at[0]), pltpu.make_async_copy(pot_ref, pot_out_ref, sems.at[1])]
    for copy in copies:
        copy.start()
    for copy in copies:
        copy.wait()


def place_other(x_ref, _, out_ref, sem):
    rows = x_ref.shape[0]
    copy = pltpu.make_async_copy(x_ref, out_ref.at[pl.ds(pl.multiple_of((1 - lax.axis_index("core")) * rows, rows), rows), :], sem)
    copy.start()
    copy.wait()


def exchange(x, axes):
    return lax.all_to_all(x, axes, 0, 0)


def per_device(sizes, docs, cents, shard_ids, shard_mass):
    n_y, n_zl, n_core = math.prod(sizes[0:3]), sizes[3], sizes[4]
    n_zh, n_x = math.prod(sizes[5:7]), math.prod(sizes[7:9])
    row_peers, col_peers = n_zl * n_zh * n_x, n_y * n_core
    n_doc, n_cent = docs.shape[0] * 2, cents.shape[0] // 2
    doc_rows, cent_rows = n_doc // LANES, n_cent // LANES
    scale = 4.0 * docs.shape[1] ** -0.5 * LOG2E
    target = 0.5 * (docs.shape[0] * n_y * n_zl * n_core) / (cents.shape[0] * n_zh * n_x)
    swap = [(0, 1), (1, 0)]
    shape = jax.ShapeDtypeStruct
    tile_shape = pltpu.VMEM((n_cent, n_doc), F32)
    small = shape((cent_rows, LANES), F32)

    any_space = pl.BlockSpec(memory_space=pl.ANY)
    hbm = pl.BlockSpec(memory_space=pltpu.HBM)
    other_docs = lax.ppermute(docs, "zl", swap)
    parts, docs, cents, own_w = call(
        functools.partial(first_rows, scale),
        (
            shape((row_peers, doc_rows // 2, LANES), F32),
            pltpu.VMEM(docs.shape, BF16),
            pltpu.VMEM(cents.shape, BF16),
            shape((doc_rows // 2, LANES), F32),
        ),
        4,
        in_specs=[hbm] * 4,
        scratch=[pltpu.SMEM(shard_mass.shape, jnp.int32), pltpu.VMEM((doc_rows // 2, LANES), jnp.int32), pltpu.SemaphoreType.DMA((4,))],
        flops=2 * docs.shape[0] * cents.shape[0] * 256,
    )(*[pltpu.with_memory_space_constraint(x, pltpu.HBM) for x in (shard_mass, shard_ids.reshape(-1, LANES), docs, cents)])
    parts = exchange(parts, ROWS)
    chunk = n_cent // col_peers
    parts, tile, top, f, docs_all = call(
        functools.partial(first_columns, scale, n_zh),
        (
            shape((col_peers, cent_rows, LANES), F32),
            tile_shape,
            small,
            shape((doc_rows, LANES), F32),
            pltpu.VMEM((n_doc, 256), BF16),
        ),
        4,
        flops=2 * n_doc * n_cent * 256,
    )(parts, docs, other_docs, cents)

    rows_out = (shape((row_peers, doc_rows, LANES), BF16), small)
    parts = exchange(parts, COLS)
    log_target = math.log2(target)
    first_out = (shape((row_peers, doc_rows + doc_rows // 2, LANES), BF16), small)
    parts, c = call(functools.partial(rows_after_first, log_target), first_out, 4, flops=2 * n_doc * n_cent)(parts, top, own_w, tile)
    col_out = shape((col_peers, cent_rows, LANES), BF16)
    for turn in range(2):
        parts = exchange(parts, ROWS)
        if turn == 0:
            out = (col_out, shape((doc_rows, LANES), F32))
            parts, w = call(functools.partial(columns_after_first, n_x), out, 3, flops=2 * n_doc * n_cent)(parts, c, tile)
        else:
            parts = call(columns_after, col_out, 4, flops=2 * n_doc * n_cent)(parts, w, c, tile)
        parts = exchange(parts, COLS)
        parts, c = call(functools.partial(rows_after, target), rows_out, 3, flops=2 * n_doc * n_cent)(parts, c, tile)
    parts = exchange(parts, ROWS)
    n_half = n_cent // n_core
    half_flops = 2 * n_doc * n_half * 256
    part_shape = pltpu.VMEM((n_half + 8, 256), F32)
    p_scratch = [pltpu.VMEM((n_half, n_doc), BF16)]
    for_other, pot, u = call(
        final_other,
        (part_shape, pltpu.VMEM((doc_rows // 2, LANES), F32), shape((doc_rows, LANES), F32)),
        6,
        scratch=p_scratch,
        flops=half_flops,
    )(parts, w, f, c, tile, docs_all)
    from_other = lax.ppermute(for_other, "core", swap)
    for_own = call(final_own, part_shape, 4, scratch=p_scratch, flops=half_flops)(u, c, tile, docs_all)
    sums = call(final_join, shape((n_y, 16, 2 * LANES * (chunk // 16) + LANES), BF16), 2)(for_own, from_other)
    sums = exchange(sums, SUMS)
    new = call(divide, shape((n_y * n_zl, chunk, 256), BF16), 1, scratch=[pltpu.VMEM((LANES, LANES), F32)])(sums)
    own = exchange(new, ("zl", *SUMS)).reshape(n_y * n_zl * chunk, 256)
    other = lax.ppermute(own, "core", swap)
    placed = shape((cents.shape[0], 256), BF16)
    new, pot = call(
        place_own,
        (placed, shape((doc_rows // 2, LANES), F32)),
        2,
        in_specs=[any_space, pl.BlockSpec(memory_space=pltpu.VMEM)],
        out_specs=(any_space, any_space),
        scratch=[pltpu.SemaphoreType.DMA((2,))],
    )(own, pot)
    new = call(
        place_other, placed, 2, in_specs=[any_space, any_space], out_specs=any_space, scratch=[pltpu.SemaphoreType.DMA], alias={1: 0}
    )(other, new)
    return new, pot.reshape(-1)


SIZES = (2, 2, 2, 2, 2, 2, 2, 2, 2)


def solution(mesh, sizes=SIZES):
    fine = Mesh(mesh.devices.reshape(sizes), ("ya", "yb", "yc", "zl", "core", "za", "zb", "xa", "xb"))
    docs, cents = ("ya", "yb", "yc", "zl", "core"), ("za", "zb", "xa", "xb")
    return jax.shard_map(
        functools.partial(per_device, sizes),
        mesh=fine,
        in_specs=(P(docs, None), P(cents, None), P(docs), P()),
        out_specs=(P(cents, None), P(docs)),
        check_vma=False,
    )
```
